32 devices in a mesh: fsdp: 16 (over z, y, x), row: 2 (over core).
Axes of the slice: x: 2, y: 2, z: 4, core: 2. Of those that a mesh axis runs over, the one named last changes fastest.
Arguments:
- tokens: bfloat16 [32768, 768], P(('fsdp', 'row')), may hold values from -6 to 6
- cotangent: bfloat16 [32768, 768], P(('fsdp', 'row')), may hold values from -6 to 6
- counts: int32 [32, 2], P(('fsdp', 'row')), may hold values from 0 to 1, as said below
- lengths: int32 [64], P(('fsdp', 'row')), may hold values from 128 to 512, as said below
- w_qkv: float32 [768, 2304], P('fsdp', 'row'), may hold values from -0.21875 to 0.21875
- w_out: float32 [768, 768], P('fsdp', 'row'), may hold values from -1.25 to 1.25
- w_up: float32 [768, 3072], P('fsdp', 'row'), may hold values from -0.21875 to 0.21875
- w_down: float32 [768, 3072], P('fsdp', 'row'), may hold values from -0.109375 to 0.109375
- vectors: float32 [12, 768], P('row', 'fsdp'), may hold values from -1.2 to 1.3
- mom_qkv: float32 [768, 2304], P('fsdp', 'row'), may hold values from -256 to 256
- mom_out: float32 [768, 768], P('fsdp', 'row'), may hold values from -64 to 64
- mom_up: float32 [768, 3072], P('fsdp', 'row'), may hold values from -128 to 128
- mom_down: float32 [768, 3072], P('fsdp', 'row'), may hold values from -256 to 256
- adam_first: float32 [12, 768], P('row', 'fsdp'), may hold values from -182.82953 to 182.82953
- adam_second: float32 [12, 768], P('row', 'fsdp'), may hold values from 6.5536 to 27852.8
Outputs:
- layer_out: bfloat16 [32768, 768], P(('fsdp', 'row'))
- input_grad: float32 [32768, 768], P(('fsdp', 'row'))
- grad_qkv: float32 [768, 2304], P('fsdp', 'row')
- grad_out: float32 [768, 768], P('fsdp', 'row')
- grad_up: float32 [768, 3072], P('fsdp', 'row')
- grad_down: float32 [768, 3072], P('fsdp', 'row')
- grad_vectors: float32 [12, 768], P('row', 'fsdp')
- moment_qkv: float32 [768, 2304], P('fsdp', 'row')
- moment_out: float32 [768, 768], P('fsdp', 'row')
- moment_up: float32 [768, 3072], P('fsdp', 'row')
- moment_down: float32 [768, 3072], P('fsdp', 'row')
- weight_qkv: float32 [768, 2304], P('fsdp', 'row')
- weight_out: float32 [768, 768], P('fsdp', 'row')
- weight_up: float32 [768, 3072], P('fsdp', 'row')
- weight_down: float32 [768, 3072], P('fsdp', 'row')
- first_moment: float32 [12, 768], P('row', 'fsdp')
- second_moment: float32 [12, 768], P('row', 'fsdp')
- new_vectors: float32 [12, 768], P('row', 'fsdp')
The draws below stay inside these ranges and needn't reach their ends.
Inputs may be any that keep to these rules, and one draw needn't show every extreme that they name: `counts`: some micro-batch of some group is full. `lengths`: some slot is not padded.
All inputs are finite; a program needn't handle non-finite values.
Results may differ from the reference program's by a relative error of at most 0.013.
The reference program's roundings to bfloat16 on the way count: a program that leaves them out, or rounds other values in their place, can miss the bound.
Values may be sent and summed in bfloat16 or wider, within the bound.
No kernel may reach another device: no remote copies, remote signals or barrier semaphores. Data moves between devices by JAX's collectives and lax.ppermute only.
A program may use at most 256 MiB of HBM per device.

```python
import math
import jax
import jax.numpy as jnp
from jax import lax

D = 768
FF = 3072
HEADS = 12
HEAD_DIM = 64
SEQ = 512
CAP = 1
MICRO = 2
NS_ITERS = 5
STEP = 10
GROUPS = 32
SLOTS = 64
TOKENS = 32768
VROWS = 12


def vector_scales():
    up_rows = FF // D
    row_scale = jnp.array([0.4, 4.3, 0.77, 1.0, 1.0] + [0.27] * up_rows + [0.85, 1.0, 1.0], jnp.float32)
    return row_scale * (0.53 * TOKENS ** 0.5)


def draw_counts(key, part):
    first_key = jax.random.fold_in(key, 101)
    second_key = jax.random.fold_in(key, 102)
    sampled = jax.random.randint(first_key, (GROUPS * MICRO,), 0, CAP + 1)
    chosen = jax.random.randint(second_key, (), 0, GROUPS * MICRO)
    filled = jnp.where(jnp.arange(GROUPS * MICRO) == chosen, CAP, sampled)
    return filled.reshape(GROUPS, MICRO).astype(jnp.int32)


def draw_lengths(key, part):
    first_key = jax.random.fold_in(key, 201)
    second_key = jax.random.fold_in(key, 202)
    sampled = jax.random.randint(first_key, (SLOTS,), SEQ // 4, SEQ + 1)
    chosen = jax.random.randint(second_key, (), 0, SLOTS)
    return jnp.where(jnp.arange(SLOTS) == chosen, SEQ, sampled).astype(jnp.int32)


def draw_vectors(key, part):
    first_key = jax.random.fold_in(key, 301)
    second_key = jax.random.fold_in(key, 302)
    row_ids = jnp.arange(VROWS)[:, None]
    gain_row = (row_ids == 3) | (row_ids == 6 + FF // D)
    gains = 0.7 + 0.6 * jax.random.uniform(first_key, (VROWS, D), jnp.float32)
    biases = 0.3 * jax.random.truncated_normal(second_key, -4.0, 4.0, (VROWS, D), jnp.float32)
    return jnp.where(gain_row, gains, biases).astype(jnp.float32)


def draw_adam_first(key, part):
    sample_key = jax.random.fold_in(key, 401)
    normal_draw = jax.random.truncated_normal(sample_key, -4.0, 4.0, (VROWS, D), jnp.float32)
    return (0.11 * vector_scales()[:, None] * normal_draw).astype(jnp.float32)


def draw_adam_second(key, part):
    sample_key = jax.random.fold_in(key, 501)
    factor = jnp.exp(jax.random.uniform(sample_key, (VROWS, D), jnp.float32, math.log(0.5), math.log(8.0)))
    row_scale = vector_scales()[:, None]
    return (0.02 / 0.98 * row_scale * row_scale * factor).astype(jnp.float32)


def shard_levels(stream_key, shape, split, low, largest):
    def one(axis_at, shards_of):
        draws = jax.random.uniform(jax.random.fold_in(jax.random.fold_in(stream_key, 6), axis_at), (shards_of,), jnp.float32, low / len(split), largest / len(split))
        return jnp.repeat(jnp.exp(draws), shape[axis_at] // shards_of).reshape((-1,) + (1,) * (len(shape) - axis_at - 1))

    gain = one(*split[0])
    for cut in split[1:]:
        gain = gain * one(*cut)
    return gain


def gaussian(rng, extent, scale, bound, shards=(), kind=jnp.bfloat16):
    level = shard_levels(rng, extent, shards, -0.22, 0.18) if shards else 1.0
    values = jax.random.normal(rng, extent, jnp.float32) * scale * level
    return jnp.minimum(jnp.maximum(values, -bound), bound).astype(kind)


def setup_inputs(seed: int = 0) -> dict:
    splits = jax.random.split(jax.random.key(seed), 16)
    tokens = gaussian(splits[0], (TOKENS, D), 1.0, 6.0, ((0, 32),))
    cotangent = gaussian(splits[1], (TOKENS, D), 1.0, 6.0, ((0, 32),))
    counts = draw_counts(jax.random.fold_in(splits[15], 71), 0)
    lengths = draw_lengths(jax.random.fold_in(splits[15], 71), 0)
    w_qkv = gaussian(splits[4], (D, 3 * D), D ** -0.5, 0.21875, ((0, 16), (1, 2)), jnp.float32)
    w_out = gaussian(splits[5], (D, D), (D // 32) ** -0.5, 1.25, ((0, 16), (1, 2)), jnp.float32)
    w_up = gaussian(splits[6], (D, FF), D ** -0.5, 0.21875, ((0, 16), (1, 2)), jnp.float32)
    w_down = gaussian(splits[7], (D, FF), FF ** -0.5, 0.109375, ((0, 16), (1, 2)), jnp.float32)
    vectors = draw_vectors(jax.random.fold_in(splits[15], 71), 0)
    mom_qkv = gaussian(splits[9], (D, 3 * D), (0.25 * TOKENS ** 0.5), 256.0, ((0, 16), (1, 2)), jnp.float32)
    mom_out = gaussian(splits[10], (D, D), (0.06 * TOKENS ** 0.5), 64.0, ((0, 16), (1, 2)), jnp.float32)
    mom_up = gaussian(splits[11], (D, FF), (0.13 * TOKENS ** 0.5), 128.0, ((0, 16), (1, 2)), jnp.float32)
    mom_down = gaussian(splits[12], (D, FF), (0.25 * TOKENS ** 0.5), 256.0, ((0, 16), (1, 2)), jnp.float32)
    adam_first = draw_adam_first(jax.random.fold_in(splits[15], 71), 0)
    adam_second = draw_adam_second(jax.random.fold_in(splits[15], 71), 0)
    return {"tokens": tokens, "cotangent": cotangent, "counts": counts, "lengths": lengths, "w_qkv": w_qkv, "w_out": w_out, "w_up": w_up, "w_down": w_down, "vectors": vectors, "mom_qkv": mom_qkv, "mom_out": mom_out, "mom_up": mom_up, "mom_down": mom_down, "adam_first": adam_first, "adam_second": adam_second}


@jax.custom_vjp
def low(v):
    return lax.optimization_barrier(v.astype(jnp.bfloat16)).astype(jnp.float32)

@jax.custom_vjp
def low_back(v):
    return v

def low_keep(v):
    return (low(v), None)

def low_pass(kept, grad):
    return (grad,)

def back_keep(v):
    return (v, None)

def back_low(kept, grad):
    return (low(grad),)
low.defvjp(low_keep, low_pass)
low_back.defvjp(back_keep, back_low)
norm_eps = 1e-05
mask_fill = -1e+30
poly_first = 3.4445
poly_second = -4.775
poly_third = 2.0315
muon_rate = 0.2
adam_rate = 0.8
decay_rate = 0.01
moment_decay = 0.5
beta_first = 0.9
beta_second = 0.98
adam_eps = 1e-06

def highest(former, latter):
    return jnp.dot(former, latter, precision=lax.Precision.HIGHEST, preferred_element_type=jnp.float32)

def norm_rows(values, scaling, offset):
    center = values - lax.optimization_barrier(jnp.mean(values, axis=-1, keepdims=True))
    spread = lax.optimization_barrier(jnp.mean(center * center, axis=-1, keepdims=True))
    return center * lax.rsqrt(spread + norm_eps) * scaling + offset

def attend_one(query_rows, key_rows, value_rows, length):
    head_shape = (SEQ, HEADS, HEAD_DIM)
    raw_scores = jnp.einsum('qhd,khd->hqk', query_rows.reshape(head_shape), key_rows.reshape(head_shape), precision=lax.Precision.HIGHEST) / math.sqrt(HEAD_DIM)
    key_valid = jnp.arange(SEQ) < length
    scores = low_back(jnp.where(key_valid[None, None, :], raw_scores, mask_fill))
    probs = low(jax.nn.softmax(scores, axis=-1))
    context = jnp.einsum('hqk,khd->qhd', probs, value_rows.reshape(head_shape), precision=lax.Precision.HIGHEST)
    return context.reshape(SEQ, D)

def layer(rows_in, qkv_weight, out_weight, up_weight, down_weight, vector_rows, seq_lengths):
    up_rows = FF // D
    vec_low = low(vector_rows)
    projected = highest(rows_in, low(qkv_weight))
    queries = low_back(low(projected[:, :D] + vec_low[0]))
    key_part = low_back(low(projected[:, D:2 * D]))
    value_part = low_back(low(projected[:, 2 * D:] + vec_low[1]))
    seq_count = seq_lengths.shape[0]
    attend_block = jax.checkpoint(attend_one)
    context = lax.map(lambda pieces: attend_block(pieces[0], pieces[1], pieces[2], pieces[3]), (queries.reshape(seq_count, SEQ, D), key_part.reshape(seq_count, SEQ, D), value_part.reshape(seq_count, SEQ, D), seq_lengths))
    context = low_back(low(context.reshape(seq_count * SEQ, D)))
    attended = low_back(highest(context, low(out_weight)) + vec_low[2])
    hidden = norm_rows(rows_in + attended, vec_low[3], vec_low[4])
    pre_act = low_back(highest(low(hidden), low(up_weight)) + vec_low[5:5 + up_rows].reshape(FF))
    activated = low(jax.nn.gelu(pre_act, approximate=False))
    branch = low_back(highest(activated, low(down_weight).T) + vec_low[5 + up_rows])
    return norm_rows(hidden + branch, vec_low[6 + up_rows], vec_low[7 + up_rows])

def orthogonalize(moment):
    iterate = moment / (jnp.sqrt(jnp.sum(moment * moment)) + 1e-07)
    for sweep_index in range(NS_ITERS):
        gram = highest(iterate, iterate.T)
        poly = poly_second * gram + poly_third * highest(gram, gram)
        iterate = poly_first * iterate + highest(poly, iterate)
    return iterate

def reference(tokens, cotangent, counts, lengths, w_qkv, w_out, w_up, w_down, vectors, mom_qkv, mom_out, mom_up, mom_down, adam_first, adam_second):
    slot_total = lengths.shape[0]
    slot_ids = jnp.arange(slot_total)
    live_slots = slot_ids % CAP < counts.reshape(-1)[slot_ids // CAP]
    valid = (live_slots[:, None] & (jnp.arange(SEQ)[None, :] < lengths[:, None])).astype(jnp.float32)
    masked = cotangent.astype(jnp.float32).reshape(slot_total, SEQ, D) * valid[:, :, None]
    per_block = math.gcd(slot_total, max(1, 4096 // SEQ))
    block_count = slot_total // per_block
    inputs = tokens.astype(jnp.float32).reshape(block_count, per_block * SEQ, D)
    cot_blocks = masked.reshape(block_count, per_block * SEQ, D)
    len_blocks = lengths.reshape(block_count, per_block)

    def accumulate(totals, item):
        rows_in, cot_rows, seq_lengths = item

        def forward(rows, qkv_weight, out_weight, up_weight, down_weight, vector_rows):
            return layer(rows, qkv_weight, out_weight, up_weight, down_weight, vector_rows, seq_lengths)
        outputs, pull = jax.vjp(forward, rows_in, w_qkv, w_out, w_up, w_down, vectors)
        grads = pull(cot_rows)
        summed = tuple((total + grad for total, grad in zip(totals, grads[1:])))
        return (summed, (outputs.astype(jnp.bfloat16), grads[0]))
    starts = (jnp.zeros(w_qkv.shape, jnp.float32), jnp.zeros(w_out.shape, jnp.float32), jnp.zeros(w_up.shape, jnp.float32), jnp.zeros(w_down.shape, jnp.float32), jnp.zeros(vectors.shape, jnp.float32))
    grads, (layer_rows, grad_rows) = lax.scan(accumulate, starts, (inputs, cot_blocks, len_blocks))
    grad_qkv, grad_out, grad_up, grad_down, grad_vectors = grads
    layer_out = layer_rows.reshape(TOKENS, D)
    input_grad = grad_rows.reshape(TOKENS, D)
    moments = (moment_decay * mom_qkv + grad_qkv, moment_decay * mom_out + grad_out, moment_decay * mom_up + grad_up, moment_decay * mom_down + grad_down)
    masters = (w_qkv, w_out, w_up, w_down)
    columns = (3 * D, D, FF, FF)
    updated = tuple((master * (1.0 - muon_rate * decay_rate) - muon_rate * 0.2 * math.sqrt(count) * orthogonalize(moment) for master, count, moment in zip(masters, columns, moments)))
    first_moment = beta_first * adam_first + (1.0 - beta_first) * grad_vectors
    second_moment = beta_second * adam_second + (1.0 - beta_second) * grad_vectors * grad_vectors
    direction = first_moment / (1.0 - beta_first ** STEP) / (jnp.sqrt(second_moment / (1.0 - beta_second ** STEP)) + adam_eps)
    new_vectors = vectors - adam_rate * (direction + decay_rate * vectors)
    return (layer_out, input_grad, grad_qkv, grad_out, grad_up, grad_down, grad_vectors, moments[0], moments[1], moments[2], moments[3], updated[0], updated[1], updated[2], updated[3], first_moment, second_moment, new_vectors)
```

```python
import math

import jax
import jax.numpy as jnp
from jax import lax
from jax.sharding import PartitionSpec as P

D = 768
FF = 3072
HEADS = 12
HEAD_DIM = 64
SEQ = 512
CAP = 1
MICRO = 2
NS_ITERS = 5
STEP = 10

norm_eps = 1e-05
mask_fill = -1e30
poly_first = 3.4445
poly_second = -4.775
poly_third = 2.0315
muon_rate = 0.2
adam_rate = 0.8
decay_rate = 0.01
moment_decay = 0.5
beta_first = 0.9
beta_second = 0.98
adam_eps = 1e-06

SWAP = [(0, 1), (1, 0)]
VEC_PAD = 128
GROUP = 4


def matmul(former, latter):
    return jnp.dot(former, latter, preferred_element_type=jnp.float32)


def matmul_tn(former, latter):
    return lax.dot_general(
        former, latter, (((0,), (0,)), ((), ())), preferred_element_type=jnp.float32
    )


def matmul_nt(former, latter):
    return lax.dot_general(
        former, latter, (((1,), (1,)), ((), ())), preferred_element_type=jnp.float32
    )


def close_dot(former, latter):
    return jnp.dot(
        former, latter, precision=lax.Precision.HIGH, preferred_element_type=jnp.float32
    )


def flip(values, bit, size):
    return lax.ppermute(values, "fsdp", [(i, i ^ (1 << bit)) for i in range(size)])


def swap_cores(values):
    return lax.ppermute(values, "row", SWAP)


def bit_orders(size):
    count = size.bit_length() - 1
    every = list(range(count))[::-1]
    high, rest = every[:2], every[2:]
    half = len(rest) // 2
    return high, rest[:half] + rest[half:], rest[half:] + rest[:half]


def my_bit(bit):
    return (lax.axis_index("fsdp") >> bit) & 1


def gather_bits(values, have, bits, size):
    for bit in bits:
        arrived = flip(values, bit, size)
        place = sum(1 for other in have if other > bit)
        values = jnp.where(
            my_bit(bit) == 1,
            jnp.stack([arrived, values], axis=place),
            jnp.stack([values, arrived], axis=place),
        )
        have = have + [bit]
    return values, have


def gather_rows(values, cut, size):
    high, order_a, order_b = bit_orders(size)
    values, have = gather_bits(values, [], high, size)
    part_a, _ = gather_bits(values[..., :cut], have, order_a, size)
    part_b, _ = gather_bits(values[..., cut:], have, order_b, size)
    return part_a.reshape(D, -1), part_b.reshape(D, -1)


def reduce_bits(values, have, bits, size):
    for bit in bits:
        place = sum(1 for other in have if other > bit)
        mine = my_bit(bit)
        leaving = lax.dynamic_index_in_dim(values, 1 - mine, place, keepdims=False)
        kept = lax.dynamic_index_in_dim(values, mine, place, keepdims=False)
        values = kept + flip(leaving.astype(jnp.bfloat16), bit, size).astype(jnp.float32)
        have = [other for other in have if other != bit]
    return values, have


def reduce_rows(part_a, part_b, size):
    high, order_a, order_b = bit_orders(size)
    every = high + order_a
    shape = (2,) * len(every) + (D // size,)
    part_a = part_a.reshape(shape + (-1,))
    part_b = part_b.reshape(shape + (-1,))
    part_a, have = reduce_bits(part_a, every, order_a[::-1], size)
    part_b, have = reduce_bits(part_b, every, order_b[::-1], size)
    total = jnp.concatenate([part_a, part_b], axis=-1)
    total, _ = reduce_bits(total, have, high[::-1], size)
    return total


def column_halves(core, own, other):
    return jnp.where(
        core == 0,
        jnp.concatenate([own, other], axis=1),
        jnp.concatenate([other, own], axis=1),
    )


def chip_grad(core, former, latter):
    half = latter.shape[1] // 2
    leaving = matmul_tn(former, lax.dynamic_slice_in_dim(latter, (1 - core) * half, half, 1))
    arrived = swap_cores(leaving.astype(jnp.bfloat16))
    kept = matmul_tn(former, lax.dynamic_slice_in_dim(latter, core * half, half, 1))
    return kept + arrived.astype(jnp.float32)


def erf_gelu(pre_act):
    cdf = 0.5 * (1.0 + lax.erf(pre_act * math.sqrt(0.5)))
    pdf = jnp.exp(-0.5 * pre_act * pre_act) * (1.0 / math.sqrt(2.0 * math.pi))
    return pre_act * cdf, cdf + pre_act * pdf


def norm_parts(values):
    center = values - jnp.mean(values, axis=-1, keepdims=True)
    rstd = lax.rsqrt(jnp.mean(center * center, axis=-1, keepdims=True) + norm_eps)
    return center * rstd, rstd


def norm_pull(grad, gain, xhat, rstd):
    scaled = grad * gain
    return rstd * (
        scaled
        - jnp.mean(scaled, axis=-1, keepdims=True)
        - xhat * jnp.mean(scaled * xhat, axis=-1, keepdims=True)
    )


def column_sum(values):
    return jnp.sum(values, axis=0, dtype=jnp.float32)


def attend(query_heads, key_heads, key_valid):
    scores = jnp.einsum(
        "cqhd,ckhd->chqk", query_heads, key_heads, preferred_element_type=jnp.float32
    ) / math.sqrt(HEAD_DIM)
    return jnp.where(key_valid[:, None, None, :], scores, mask_fill)


def newton_schulz(gram, row_start, row_count):
    scale = jnp.sqrt(jnp.trace(gram)) + 1e-07
    gram = gram / (scale * scale)
    rows = None
    for sweep in range(NS_ITERS):
        square = close_dot(gram, gram)
        step = poly_second * gram + poly_third * square
        step = step + poly_first * jnp.eye(D, dtype=jnp.float32)
        if rows is None:
            rows = lax.dynamic_slice_in_dim(step, row_start, row_count, 0)
        else:
            rows = close_dot(rows, step)
        if sweep < NS_ITERS - 1:
            gram = close_dot(close_dot(step, gram), step)
    return rows / scale


def per_device(
    size,
    tokens,
    cotangent,
    counts,
    lengths,
    w_qkv,
    w_out,
    w_up,
    w_down,
    vectors,
    mom_qkv,
    mom_out,
    mom_up,
    mom_down,
    adam_first,
    adam_second,
):
    me = lax.axis_index("fsdp")
    core = lax.axis_index("row")
    slots = lengths.shape[0]
    rows = tokens.shape[0]
    up_rows = FF // D
    low = jnp.bfloat16

    vec_block = jnp.pad(vectors.T, ((0, 0), (0, VEC_PAD - vectors.shape[0]))).astype(low)
    first_block = jnp.concatenate([w_qkv.astype(low), vec_block], axis=1)
    first_a, first_b = gather_rows(first_block, 640, size)
    own_first = jnp.concatenate([first_a, first_b], axis=1)
    other_first = swap_cores(own_first)
    qkv_half = w_qkv.shape[1]
    qkv_weight = column_halves(core, own_first[:, :qkv_half], other_first[:, :qkv_half])
    vec_rows = vectors.shape[0]
    vec_own = own_first[:, qkv_half : qkv_half + vec_rows].T
    vec_other = other_first[:, qkv_half : qkv_half + vec_rows].T
    vec = jnp.where(
        core == 0,
        jnp.concatenate([vec_own, vec_other], axis=0),
        jnp.concatenate([vec_other, vec_own], axis=0),
    ).astype(jnp.float32)
    bias_query, bias_value, bias_out, gain_attn, shift_attn = (vec[i] for i in range(5))
    bias_up = vec[5 : 5 + up_rows].reshape(FF)
    bias_down, gain_ffn, shift_ffn = (vec[i] for i in range(5 + up_rows, 8 + up_rows))

    out_low, up_low, down_low = w_out.astype(low), w_up.astype(low), w_down.astype(low)
    second_block = jnp.concatenate([up_low, out_low, down_low], axis=1)
    second_a, second_b = gather_rows(second_block, 1792, size)
    other_a, other_b = swap_cores(second_a), swap_cores(second_b)
    up_half = w_up.shape[1]
    up_weight = column_halves(core, second_a[:, :up_half], other_a[:, :up_half])
    out_weight = column_halves(
        core,
        jnp.concatenate([second_a[:, up_half:], second_b[:, :128]], axis=1),
        jnp.concatenate([other_a[:, up_half:], other_b[:, :128]], axis=1),
    )
    down_weight = column_halves(core, second_b[:, 128:], other_b[:, 128:])

    head_shape = (slots, SEQ, HEADS, HEAD_DIM)
    key_valid = jnp.arange(SEQ)[None, :] < lengths[:, None]
    projected = matmul(tokens, qkv_weight)
    query = (projected[:, :D] + bias_query).astype(low).reshape(head_shape)
    key = projected[:, D : 2 * D].astype(low).reshape(head_shape)
    value = (projected[:, 2 * D :] + bias_value).astype(low).reshape(head_shape)
    scores = attend(query, key, key_valid)
    top_score = jnp.max(scores, axis=-1, keepdims=True)
    exp_scores = jnp.exp(scores - top_score)
    row_total = jnp.sum(exp_scores, axis=-1, keepdims=True)
    log_total = top_score + jnp.log(row_total)
    context = (
        jnp.einsum(
            "chqk,ckhd->cqhd",
            (exp_scores / row_total).astype(low),
            value,
            preferred_element_type=jnp.float32,
        )
        .reshape(rows, D)
        .astype(low)
    )
    resid_one = tokens.astype(jnp.float32) + (matmul(context, out_weight) + bias_out)
    xhat_one, rstd_one = norm_parts(resid_one)
    hidden = xhat_one * gain_attn + shift_attn
    hidden_low = hidden.astype(low)
    pre_act = matmul(hidden_low, up_weight) + bias_up
    activated, slope = erf_gelu(pre_act)
    act_low = activated.astype(low)
    branch = matmul_nt(act_low, down_weight) + bias_down
    xhat_two, rstd_two = norm_parts(hidden + branch)
    layer_out = (xhat_two * gain_ffn + shift_ffn).astype(low)

    live = jnp.arange(slots) % CAP < counts.reshape(-1)[jnp.arange(slots) // CAP]
    valid = (live[:, None] & key_valid).reshape(rows, 1).astype(jnp.float32)
    masked = cotangent.astype(jnp.float32) * valid
    gain_two = column_sum(masked * xhat_two)
    shift_two = column_sum(masked)
    top_grad = norm_pull(masked, gain_ffn, xhat_two, rstd_two)
    branch_low = top_grad.astype(low)
    down_bias = column_sum(branch_low)
    down_part = chip_grad(core, branch_low, act_low)
    pre_low = (matmul(branch_low, down_weight) * slope).astype(low)
    up_bias = column_sum(pre_low)
    up_part = chip_grad(core, hidden_low, pre_low)
    hidden_grad = top_grad + matmul_nt(pre_low, up_weight)
    gain_one = column_sum(hidden_grad * xhat_one)
    shift_one = column_sum(hidden_grad)
    skip_grad = norm_pull(hidden_grad, gain_attn, xhat_one, rstd_one)
    attn_low = skip_grad.astype(low)
    out_bias = column_sum(attn_low)
    out_part = chip_grad(core, context, attn_low)
    context_grad = matmul_nt(attn_low, out_weight).astype(low).reshape(head_shape)
    scores = attend(query, key, key_valid)
    probs = jnp.exp(scores - log_total)
    prob_grad = jnp.einsum(
        "cqhd,ckhd->chqk", context_grad, value, preferred_element_type=jnp.float32
    )
    value_grad = jnp.einsum(
        "chqk,cqhd->ckhd", probs.astype(low), context_grad, preferred_element_type=jnp.float32
    ).astype(low)
    row_dot = jnp.sum(probs * prob_grad, axis=-1, keepdims=True)
    score_grad = (probs * (prob_grad - row_dot)).astype(low)
    query_grad = (
        jnp.einsum("chqk,ckhd->cqhd", score_grad, key, preferred_element_type=jnp.float32)
        / math.sqrt(HEAD_DIM)
    ).astype(low)
    key_grad = (
        jnp.einsum("chqk,cqhd->ckhd", score_grad, query, preferred_element_type=jnp.float32)
        / math.sqrt(HEAD_DIM)
    ).astype(low)
    qkv_low = jnp.concatenate(
        [query_grad.reshape(rows, D), key_grad.reshape(rows, D), value_grad.reshape(rows, D)],
        axis=1,
    )
    qkv_part = chip_grad(core, tokens, qkv_low)
    query_bias, value_bias = column_sum(qkv_low[:, :D]), column_sum(qkv_low[:, 2 * D :])
    input_grad = skip_grad + matmul_nt(qkv_low, qkv_weight)

    half = up_half // 2
    grad_down = reduce_rows(down_part[:, :half], down_part[:, half:], size)
    grad_up = reduce_rows(up_part[:, :half], up_part[:, half:], size)
    last_part = jnp.concatenate([qkv_part, out_part], axis=1)
    grad_last = reduce_rows(last_part[:, :half], last_part[:, half:], size)
    grad_qkv, grad_out = grad_last[:, :qkv_half], grad_last[:, qkv_half:]
    vector_grad = jnp.concatenate(
        [
            jnp.stack([query_bias, value_bias, out_bias, gain_one, shift_one]),
            up_bias.reshape(up_rows, D),
            jnp.stack([down_bias, gain_two, shift_two]),
        ],
        axis=0,
    )
    grad_vectors = lax.psum_scatter(vector_grad, "fsdp", scatter_dimension=1, tiled=True)
    grad_vectors = lax.psum_scatter(grad_vectors, "row", scatter_dimension=0, tiled=True)

    moment_qkv = moment_decay * mom_qkv + grad_qkv
    moment_out = moment_decay * mom_out + grad_out
    moment_up = moment_decay * mom_up + grad_up
    moment_down = moment_decay * mom_down + grad_down

    def whole_columns(block):
        part_a, part_b = gather_rows(block, half, size)
        return jnp.concatenate([part_a, part_b], axis=1)

    down_cols = whole_columns(moment_down.astype(low))
    up_cols = whole_columns(moment_up.astype(low))
    last_cols = whole_columns(jnp.concatenate([moment_qkv, moment_out], axis=1).astype(low))
    columns = (last_cols[:, :qkv_half], last_cols[:, qkv_half:], up_cols, down_cols)

    place = me % GROUP
    gram = lax.switch(
        place,
        [
            lambda cols: matmul_nt(cols[0], cols[0]),
            lambda cols: matmul_nt(cols[1], cols[1]),
            lambda cols: matmul_nt(cols[2], cols[2]),
            lambda cols: matmul_nt(cols[3], cols[3]),
        ],
        columns,
    )
    gram = gram + swap_cores(gram)
    block_rows = D // size
    polar_rows = newton_schulz(gram, (me - place) * block_rows, GROUP * block_rows)
    polar_rows = polar_rows.reshape(GROUP, block_rows, D)
    arrived = []
    for offset in range(GROUP):
        block = lax.dynamic_index_in_dim(polar_rows, place ^ offset, 0, keepdims=False)
        if offset:
            block = lax.ppermute(block, "fsdp", [(i, i ^ offset) for i in range(size)])
        arrived.append(block)
    arrived = jnp.stack(arrived)
    masters = (w_qkv, w_out, w_up, w_down)
    counts_of = (3 * D, D, FF, FF)
    updated = []
    for index in range(GROUP):
        polar = lax.dynamic_index_in_dim(arrived, place ^ index, 0, keepdims=False)
        polar_high = polar.astype(low)
        polar_rest = (polar - polar_high.astype(jnp.float32)).astype(low)
        product = matmul(jnp.concatenate([polar_high, polar_rest], axis=0), columns[index])
        ortho = product[:block_rows] + product[block_rows:]
        updated.append(
            masters[index] * (1.0 - muon_rate * decay_rate)
            - muon_rate * 0.2 * math.sqrt(counts_of[index]) * ortho
        )

    first_moment = beta_first * adam_first + (1.0 - beta_first) * grad_vectors
    second_moment = beta_second * adam_second + (1.0 - beta_second) * grad_vectors * grad_vectors
    direction = (
        first_moment
        / (1.0 - beta_first**STEP)
        / (jnp.sqrt(second_moment / (1.0 - beta_second**STEP)) + adam_eps)
    )
    new_vectors = vectors - adam_rate * (direction + decay_rate * vectors)
    return (
        layer_out,
        input_grad,
        grad_qkv,
        grad_out,
        grad_up,
        grad_down,
        grad_vectors,
        moment_qkv,
        moment_out,
        moment_up,
        moment_down,
        updated[0],
        updated[1],
        updated[2],
        updated[3],
        first_moment,
        second_moment,
        new_vectors,
    )


def solution(mesh):
    size = mesh.shape["fsdp"]

    def run(*arrays):
        return per_device(size, *arrays)

    weight = P("fsdp", "row")
    vector = P("row", "fsdp")
    sample = P(("fsdp", "row"), None)
    return jax.shard_map(
        run,
        mesh=mesh,
        in_specs=(sample, sample, sample, P(("fsdp", "row")))
        + (weight,) * 4
        + (vector,)
        + (weight,) * 4
        + (vector,) * 2,
        out_specs=(sample, sample)
        + (weight,) * 4
        + (vector,)
        + (weight,) * 8
        + (vector,) * 3,
        check_vma=False,
    )
```

```python
import functools
import math

import jax
import jax.numpy as jnp
from jax import lax
from jax.experimental import pallas as pl
from jax.experimental.pallas import tpu as pltpu
from jax.sharding import PartitionSpec as P

D = 768
FF = 3072
HEADS = 12
HEAD_DIM = 64
SEQ = 512
CAP = 1
MICRO = 2
NS_ITERS = 5
STEP = 10

norm_eps = 1e-05
mask_fill = -1e30
poly_first = 3.4445
poly_second = -4.775
poly_third = 2.0315
muon_rate = 0.2
adam_rate = 0.8
decay_rate = 0.01
moment_decay = 0.5
beta_first = 0.9
beta_second = 0.98
adam_eps = 1e-06

SWAP = [(0, 1), (1, 0)]
VEC_PAD = 128
GROUP = 4
TILE = 256
ROWS = 256
VROWS = 8 + FF // D
PAIR = 2 * HEAD_DIM
PAIRS = HEADS // 2
BLOCKS = 3 * PAIRS
INFO = 1 + CAP * MICRO
WIDE = FF // 2
ORDER = (tuple(range(9)), tuple(range(12, 18)) + tuple(range(9, 12)))
SPOTS = tuple(
    tuple((ORDER[core] + ORDER[1 - core]).index(block) for block in range(BLOCKS))
    for core in range(2)
)


def matmul(former, latter):
    return jnp.dot(former, latter, preferred_element_type=jnp.float32)


def matmul_tn(former, latter):
    return lax.dot_general(
        former, latter, (((0,), (0,)), ((), ())), preferred_element_type=jnp.float32
    )


def matmul_nt(former, latter):
    return lax.dot_general(
        former, latter, (((1,), (1,)), ((), ())), preferred_element_type=jnp.float32
    )


def flip(values, mask, size):
    return lax.ppermute(values, "fsdp", [(i, i ^ mask) for i in range(size)])


def swap_cores(values):
    return lax.ppermute(values, "row", SWAP)


def together(*values):
    return lax.optimization_barrier(values)


def my_bit(bit):
    return (lax.axis_index("fsdp") >> bit) & 1


def pair_of(bit):
    return (lax.axis_index("fsdp") >> bit) & 3


def send_four(values, bit, size):
    return [values] + [flip(values, step << bit, size) for step in (1, 2, 3)]


def sort_four(pieces, bit, axis):
    low, high = my_bit(bit) == 1, my_bit(bit + 1) == 1
    first = jnp.where(low, jnp.stack(pieces[1::-1], axis), jnp.stack(pieces[:2], axis))
    second = jnp.where(low, jnp.stack(pieces[:1:-1], axis), jnp.stack(pieces[2:], axis))
    return jnp.where(
        high,
        jnp.concatenate([second, first], axis),
        jnp.concatenate([first, second], axis),
    )


def merge_rows(values):
    return values.reshape(-1, values.shape[-1])


def send_high(block, size):
    return send_four(block, size.bit_length() - 3, size)


def sort_high(pieces, size):
    return sort_four(pieces, size.bit_length() - 3, 0)


def send_low(values, size):
    for bit in range(size.bit_length() - 5, 0, -2):
        values = sort_four(send_four(values, bit, size), bit, -3)
    return send_four(values, 0, size)


def sort_low(pieces):
    return merge_rows(sort_four(pieces, 0, -3))


def pick_four(parts, axis, place):
    return [lax.dynamic_index_in_dim(part, place, axis, keepdims=False) for part in parts]


def leave_four(parts, axis, bit, size):
    mine = pair_of(bit)
    kept = pick_four(parts, axis, mine)
    arrived = []
    for step in (1, 2, 3):
        leaving = pick_four(parts, axis, mine ^ step)
        leaving = jnp.concatenate([part.astype(jnp.bfloat16) for part in leaving], axis=-1)
        arrived.append(flip(leaving, step << bit, size))
    return kept, arrived


def add_four(kept, arrived):
    totals, place = [], 0
    for part in kept:
        cols = slice(place, place + part.shape[-1])
        place = cols.stop
        for piece in arrived:
            part = part + piece[..., cols].astype(jnp.float32)
        totals.append(part)
    return totals


def leave_low(parts, size):
    shape = (4,) * ((size.bit_length() - 1) // 2) + (D // size, -1)
    parts = [part.reshape(shape) for part in parts]
    return leave_four(parts, len(shape) - 3, 0, size)


def leave_high(kept, arrived, size):
    parts = add_four(kept, arrived)
    for bit in range(2, size.bit_length() - 3, 2):
        parts = add_four(*leave_four(parts, parts[0].ndim - 3, bit, size))
    return leave_four(parts, 0, size.bit_length() - 3, size)


erf_slope = 0.3275911
erf_terms = (1.061405429, -1.453152027, 1.421413741, -0.284496736, 0.254829592)


def gelu_parts(pre_act):
    bell = jnp.exp(pre_act * pre_act * -0.5)
    inverse = 1.0 / (1.0 + jnp.abs(pre_act) * (erf_slope * math.sqrt(0.5)))
    poly = 0.5 * erf_terms[0] * inverse + 0.5 * erf_terms[1]
    for term in erf_terms[2:]:
        poly = poly * inverse + 0.5 * term
    tail = poly * inverse * bell
    cdf = jnp.where(pre_act < 0.0, tail, 1.0 - tail)
    return pre_act * cdf, cdf + pre_act * bell * (1.0 / math.sqrt(2.0 * math.pi))


def norm_parts(values):
    center = values - jnp.mean(values, axis=-1, keepdims=True)
    rstd = lax.rsqrt(jnp.mean(center * center, axis=-1, keepdims=True) + norm_eps)
    return center * rstd, rstd


def norm_pull(grad, gain, xhat, rstd):
    scaled = grad * gain
    return rstd * (
        scaled
        - jnp.mean(scaled, axis=-1, keepdims=True)
        - xhat * jnp.mean(scaled * xhat, axis=-1, keepdims=True)
    )


def head_lanes(shape, h):
    lane = lax.broadcasted_iota(jnp.int32, shape, 1)
    return (lane >= HEAD_DIM) if h else (lane < HEAD_DIM), lane == (0 if h else HEAD_DIM)

def masked_pair(q, k, length, h):
    inside, spare = head_lanes(q.shape, h)
    zero = jnp.zeros_like(q)
    q_in = jnp.where(inside, q * jnp.bfloat16(0.125), zero)
    q_aug = jnp.where(spare, jnp.ones_like(q), q_in)
    row = lax.broadcasted_iota(jnp.int32, q.shape, 0)
    fill = jnp.where(row < length, 0.0, mask_fill).astype(jnp.bfloat16)
    k_aug = jnp.where(inside, k, jnp.where(spare, fill, zero))
    return q_in, q_aug, k_aug, inside

def fwd_kernel(info, q_ref, k_ref, v_ref, ctx_ref, lse_ref):
    length = info[1 + pl.program_id(0)]
    q, k, v = q_ref[...], k_ref[...], v_ref[...]
    tops = []
    for h in range(2):
        _, q_aug, k_aug, _ = masked_pair(q, k, length, h)
        scores = matmul_nt(k_aug, q_aug)
        top = jnp.max(scores, axis=0, keepdims=True)
        e = jnp.exp(scores - top)
        total = jnp.sum(e, axis=0, keepdims=True)
        p = (e * (1.0 / total)).astype(jnp.bfloat16)
        lse_ref[0, 0, h:h+1, :] = top + jnp.log(total)
        tops.append(matmul_tn(v, p))
    ctx = jnp.concatenate([tops[0][:HEAD_DIM], tops[1][HEAD_DIM:]], axis=0)
    ctx_ref[...] = jnp.transpose(ctx).astype(jnp.bfloat16)

def bwd_kernel(slot, skipped, info, q_ref, k_ref, v_ref, g_ref, lse_ref, *refs):
    own_ref, other_ref, key_ref, sum_ref = refs[skipped:]
    length = info[1 + slot]
    q, k, v, g = q_ref[...], k_ref[...], v_ref[...], g_ref[...]
    dv = dk = dqt = None
    for h in range(2):
        q_in, q_aug, k_aug, inside = masked_pair(q, k, length, h)
        g_in = jnp.where(inside, g, jnp.zeros_like(g))
        scores = matmul_nt(k_aug, q_aug)
        p = jnp.exp(scores - lse_ref[0, 0, h:h+1, :])
        dp = matmul_nt(v, g_in)
        dv_h = matmul(p.astype(jnp.bfloat16), g_in)
        rd = jnp.sum(p * dp, axis=0, keepdims=True)
        ds = (p * (dp - rd)).astype(jnp.bfloat16)
        dk_h = matmul(ds, q_in)
        k_in = jnp.where(inside, k * jnp.bfloat16(0.125), jnp.zeros_like(k))
        dq_h = matmul_tn(k_in, ds)
        dv = dv_h if dv is None else dv + dv_h
        dk = dk_h if dk is None else dk + dk_h
        dqt = dq_h if dqt is None else dqt + dq_h
    dq = jnp.transpose(dqt).astype(jnp.bfloat16)
    dv = dv.astype(jnp.bfloat16)
    early = info[0] == 0
    own_ref[...] = jnp.where(early, dq, dv)
    other_ref[...] = jnp.where(early, dv, dq)
    key_ref[...] = dk.astype(jnp.bfloat16)
    sum_ref[0, 0, 0:1, :] = jnp.sum(dq.astype(jnp.float32), axis=0, keepdims=True)
    sum_ref[0, 0, 1:2, :] = jnp.sum(dv.astype(jnp.float32), axis=0, keepdims=True)


def pick(kind):
    def spot(s, p, info):
        return s, info[INFO + kind * PAIRS + p]

    return pl.BlockSpec((SEQ, PAIR), spot)


def pair_spec():
    return pl.BlockSpec((SEQ, PAIR), lambda s, p, info: (s, p))


def pair_rows(width):
    return pl.BlockSpec((1, 1, 2, width), lambda s, p, info: (s, p, 0, 0))


def attention(info, qkv, slots):
    rows = qkv.shape[0]
    return pl.pallas_call(
        fwd_kernel,
        grid_spec=pltpu.PrefetchScalarGridSpec(
            num_scalar_prefetch=1,
            grid=(slots, PAIRS),
            in_specs=[pick(kind) for kind in range(3)],
            out_specs=[pair_spec(), pair_rows(SEQ)],
        ),
        out_shape=[
            jax.ShapeDtypeStruct((rows, D), jnp.bfloat16),
            jax.ShapeDtypeStruct((slots, PAIRS, 2, SEQ), jnp.float32),
        ],
        cost_estimate=pl.CostEstimate(
            flops=20 << 30, bytes_accessed=8 << 20, transcendentals=slots * HEADS * SEQ * SEQ
        ),
        name="attention",
    )(info, qkv, qkv, qkv)


def attention_pull(info, qkv, grad, log_total, slots, slot, parts):
    rows = qkv.shape[0]

    def at_slot(spec):
        return pl.BlockSpec(
            spec.block_shape, lambda s, p, info: spec.index_map(slot, p, info)
        )

    def key_spot(s, p, info):
        return s, lax.rem(p + info[0] * (PAIRS // 2), PAIRS)

    table = jax.ShapeDtypeStruct((rows, D), jnp.bfloat16)
    before = [] if parts is None else list(parts)
    return pl.pallas_call(
        functools.partial(bwd_kernel, slot, len(before)),
        grid_spec=pltpu.PrefetchScalarGridSpec(
            num_scalar_prefetch=1,
            grid=(1, PAIRS),
            in_specs=[at_slot(pick(kind)) for kind in range(3)]
            + [at_slot(pair_spec()), at_slot(pair_rows(SEQ))]
            + [pl.BlockSpec(memory_space=pl.ANY)] * len(before),
            out_specs=[
                at_slot(pair_spec()),
                at_slot(pair_spec()),
                at_slot(pl.BlockSpec((SEQ, PAIR), key_spot)),
                at_slot(pair_rows(PAIR)),
            ],
        ),
        out_shape=[table] * 3 + [jax.ShapeDtypeStruct((slots, PAIRS, 2, PAIR), jnp.float32)],
        input_output_aliases={6 + place: place for place in range(len(before))},
        cost_estimate=pl.CostEstimate(
            flops=14 << 30, bytes_accessed=8 << 20, transcendentals=HEADS * SEQ * SEQ
        ),
        name="attention_pull",
    )(info, qkv, qkv, qkv, grad, log_total, *before)


def join_halves(core, own, other):
    return jnp.where(
        core == 0,
        jnp.concatenate([own, other], axis=1),
        jnp.concatenate([other, own], axis=1),
    )


def vector_kernel(info, own_ref, other_ref, vec_ref, bias_ref, own_bias_ref, other_bias_ref):
    early_core = info[0] == 0
    rows = VROWS // 2
    own = jnp.transpose(own_ref[...].astype(jnp.float32))[:rows]
    other = jnp.transpose(other_ref[...].astype(jnp.float32))[:rows]
    vec = jnp.concatenate(
        [jnp.where(early_core, own, other), jnp.where(early_core, other, own)], axis=0
    )
    vec_ref[0:VROWS, :] = vec
    up_rows = FF // D
    for place in range(up_rows):
        early, late = 5 + place, 5 + (place + up_rows // 2) % up_rows
        row = jnp.where(early_core, vec[early : early + 1], vec[late : late + 1])
        bias_ref[0:1, place * D : (place + 1) * D] = row
    own_bias_ref[...] = jnp.zeros_like(own_bias_ref)
    other_bias_ref[...] = jnp.zeros_like(other_bias_ref)
    own_bias_ref[0:1, :D] = jnp.where(early_core, vec[0:1], vec[1:2])
    other_bias_ref[0:1, :D] = jnp.where(early_core, vec[1:2], vec[0:1])


def vector_tables(info, own, other):
    half = own.shape[1] - VEC_PAD
    spec = pl.BlockSpec((D, VEC_PAD), lambda i: (0, half // VEC_PAD))
    shapes = [(16, D), (8, FF), (8, half), (8, half)]
    return pl.pallas_call(
        vector_kernel,
        grid=(1,),
        in_specs=[pl.BlockSpec(memory_space=pltpu.SMEM), spec, spec],
        out_specs=[pl.BlockSpec(shape, lambda i: (0, 0)) for shape in shapes],
        out_shape=[jax.ShapeDtypeStruct(shape, jnp.float32) for shape in shapes],
        name="vector_tables",
    )(info, own, other)


def vector_grad_kernel(info, low_ref, high_ref, bias_ref, head_ref, out_ref):
    early_core = info[0] == 0
    out_ref[...] = jnp.zeros_like(out_ref)
    for pair in range(PAIRS):
        cols = slice(pair * PAIR, (pair + 1) * PAIR)
        out_ref[0:2, cols] = jnp.sum(head_ref[:, pair], axis=0)
    out_ref[2:5, :] = low_ref[0:3, :]
    up_rows = FF // D
    for place in range(up_rows):
        late = (place + up_rows // 2) % up_rows
        out_ref[5 + place : 6 + place, :] = jnp.where(
            early_core,
            bias_ref[0:1, place * D : (place + 1) * D],
            bias_ref[0:1, late * D : (late + 1) * D],
        )
    out_ref[5 + up_rows : 8 + up_rows, :] = high_ref[0:3, :]


def vector_grads(info, low_sums, high_sums, bias_sums, head_sums):
    whole = pl.BlockSpec(memory_space=pltpu.VMEM)
    return pl.pallas_call(
        vector_grad_kernel,
        in_specs=[pl.BlockSpec(memory_space=pltpu.SMEM)] + [whole] * 4,
        out_specs=whole,
        out_shape=jax.ShapeDtypeStruct((16, D), jnp.float32),
        name="vector_grads",
    )(info, low_sums, high_sums, bias_sums, head_sums)


def hidden_pieces(own, other):
    return [
        (ref, slice(first, first + D), place + first)
        for place, ref in ((0, own), (WIDE, other))
        for first in range(0, WIDE, D)
    ]


OUT_COLS = slice(WIDE, WIDE + D // 2)


def raise_kernel(
    info, vec_ref, bias_ref, x_ref, ctx_ref, own, other, xhat_ref, rstd_ref, low_ref, act_ref, slope_ref
):
    ctx = ctx_ref[...]
    attended = join_halves(info[0], matmul(ctx, own[:, OUT_COLS]), matmul(ctx, other[:, OUT_COLS]))
    xhat, rstd = norm_parts(x_ref[...].astype(jnp.float32) + (attended + vec_ref[2:3, :]))
    xhat_ref[...] = xhat
    rstd_ref[...] = jnp.broadcast_to(rstd, rstd_ref.shape)
    hidden = (xhat * vec_ref[3:4, :] + vec_ref[4:5, :]).astype(jnp.bfloat16)
    low_ref[...] = hidden
    for ref, cols, place in hidden_pieces(own, other):
        spot = slice(place, place + D)
        act, slope = gelu_parts(matmul(hidden, ref[:, cols]) + bias_ref[0:1, spot])
        act_ref[:, spot] = act.astype(jnp.bfloat16)
        slope_ref[:, spot] = slope.astype(jnp.bfloat16)


def add_sums(ref, sums):
    first = pl.program_id(0) == 0
    for place, values in enumerate(sums):
        total = jnp.sum(values, axis=0, keepdims=True)
        spot = slice(place, place + 1)
        ref[spot, :] = jnp.where(first, total, ref[spot, :] + total)


def lower_kernel(
    info, vec_ref, xhat_ref, act_ref, cot_ref, own, other, out_ref, grad_ref, low_ref, sum_ref
):
    first = pl.program_id(0) * ROWS
    branch = vec_ref[9:10, :]
    for ref, cols, place in hidden_pieces(own, other):
        branch = branch + matmul_nt(act_ref[:, place : place + D], ref[:, cols])
    hidden = xhat_ref[...] * vec_ref[3:4, :] + vec_ref[4:5, :]
    xhat, rstd = norm_parts(hidden + branch)
    gain = vec_ref[10:11, :]
    out_ref[...] = (xhat * gain + vec_ref[11:12, :]).astype(jnp.bfloat16)
    limit = info[INFO + BLOCKS + lax.div(first, SEQ)]
    row = lax.broadcasted_iota(jnp.int32, (ROWS, 1), 0) + lax.rem(first, SEQ)
    cot = jnp.where(row < limit, cot_ref[...].astype(jnp.float32), 0.0)
    grad = norm_pull(cot, gain, xhat, rstd)
    grad_ref[...] = grad
    low = grad.astype(jnp.bfloat16)
    low_ref[...] = low
    add_sums(sum_ref, (low.astype(jnp.float32), cot * xhat, cot))


def pull_kernel(
    info,
    vec_ref,
    xhat_ref,
    rstd_ref,
    slope_ref,
    grad_ref,
    low_ref,
    up_own,
    up_other,
    own,
    other,
    pre_ref,
    skip_ref,
    attn_ref,
    ctx_ref,
    sum_ref,
    bias_ref,
):
    core = info[0]
    low = low_ref[...]
    hidden_grad = grad_ref[...]
    for down, up in zip(hidden_pieces(own, other), hidden_pieces(up_own, up_other)):
        ref, cols, place = down
        spot = slice(place, place + D)
        pre = matmul(low, ref[:, cols]) * slope_ref[:, spot].astype(jnp.float32)
        pre = pre.astype(jnp.bfloat16)
        pre_ref[:, spot] = pre
        hidden_grad = hidden_grad + matmul_nt(pre, up[0][:, up[1]])
    xhat = xhat_ref[...]
    skip = norm_pull(hidden_grad, vec_ref[3:4, :], xhat, rstd_ref[:, 0:1])
    skip_ref[...] = skip
    attn = skip.astype(jnp.bfloat16)
    attn_ref[...] = attn
    left, right = attn[:, : D // 2], attn[:, D // 2 :]
    ctx = matmul_nt(jnp.where(core == 0, left, right), up_own[:, OUT_COLS])
    ctx = ctx + matmul_nt(jnp.where(core == 0, right, left), up_other[:, OUT_COLS])
    ctx_ref[...] = ctx.astype(jnp.bfloat16)
    add_sums(sum_ref, (attn.astype(jnp.float32), hidden_grad * xhat, hidden_grad))
    add_sums(bias_ref, (pre_ref[...].astype(jnp.float32),))


def row_spec(width):
    return pl.BlockSpec((ROWS, width), lambda i: (i, 0))


def whole_spec():
    return pl.BlockSpec(memory_space=pltpu.VMEM)


def row_call(kernel, name, in_specs, rows, outs, sums, flops, operands):
    shapes = [jax.ShapeDtypeStruct((rows, width), kind) for width, kind in outs]
    shapes += [jax.ShapeDtypeStruct((8, width), jnp.float32) for width in sums]
    return pl.pallas_call(
        kernel,
        grid=(rows // ROWS,),
        in_specs=[pl.BlockSpec(memory_space=pltpu.SMEM)] + in_specs,
        out_specs=[row_spec(width) for width, kind in outs]
        + [pl.BlockSpec((8, width), lambda i: (0, 0)) for width in sums],
        out_shape=shapes,
        compiler_params=pltpu.CompilerParams(vmem_limit_bytes=52 << 20),
        cost_estimate=pl.CostEstimate(
            flops=flops, bytes_accessed=24 << 20, transcendentals=rows * FF
        ),
        name=name,
    )(*operands)


def raise_rows(info, vec, bias, tokens, context, own, other):
    low, full = jnp.bfloat16, jnp.float32
    return row_call(
        raise_kernel,
        "raise_rows",
        [whole_spec()] * 2 + [row_spec(D)] * 2 + [whole_spec()] * 2,
        tokens.shape[0],
        [(D, full), (PAIR, full), (D, low), (FF, low), (FF, low)],
        [],
        14 << 30,
        (info, vec, bias, tokens, context, own, other),
    )


def lower_rows(info, vec, xhat, act, cotangent, own, other):
    low, full = jnp.bfloat16, jnp.float32
    return row_call(
        lower_kernel,
        "lower_rows",
        [whole_spec(), row_spec(D), row_spec(FF), row_spec(D)] + [whole_spec()] * 2,
        act.shape[0],
        [(D, low), (D, full), (D, low)],
        [D],
        9 << 30,
        (info, vec, xhat, act, cotangent, own, other),
    )


def pull_rows(info, vec, xhat, rstd, slope, grad, low_grad, up, down):
    low, full = jnp.bfloat16, jnp.float32
    return row_call(
        pull_kernel,
        "pull_rows",
        [whole_spec(), row_spec(D), row_spec(PAIR), row_spec(FF), row_spec(D), row_spec(D)]
        + [whole_spec()] * 4,
        xhat.shape[0],
        [(FF, low), (D, full), (D, low), (D, low)],
        [D, FF],
        18 << 30,
        (info, vec, xhat, rstd, slope, grad, low_grad, *up, *down),
    )


def split_low(values):
    high = values.astype(jnp.bfloat16)
    return high, (values - high.astype(jnp.float32)).astype(jnp.bfloat16)

def store_split(values, where, high_ref, rest_ref):
    high_ref[where], rest_ref[where] = split_low(values)

def close_product(left, right, rows, cols):
    left_high, left_rest = left[0][rows, :], left[1][rows, :]
    right_high, right_rest = right[0][:, cols], right[1][:, cols]
    return matmul(
        jnp.concatenate([left_high, left_high, left_rest], axis=1),
        jnp.concatenate([right_high, right_rest, right_high], axis=0),
    )


def mirrored_product(left, right, finish):
    for first in range(0, D, TILE):
        rows = slice(first, first + TILE)
        wide = close_product(left, right, rows, slice(first, D))
        for last in range(first, D, TILE):
            tile = wide[:, last - first : last - first + TILE]
            cols = slice(last, last + TILE)
            finish(tile, rows, cols)
            if first < last:
                finish(jnp.transpose(tile), cols, rows)


def polar_kernel(
    start_ref,
    own_ref,
    other_ref,
    cols_ref,
    polar_ref,
    out_ref,
    gram,
    a_high,
    a_rest,
    q_high,
    q_rest,
    b_high,
    b_rest,
    r_high,
    r_rest,
):
    a, q, b, r = (a_high, a_rest), (q_high, q_rest), (b_high, b_rest), (r_high, r_rest)
    count = out_ref.shape[0]
    start = pl.multiple_of(start_ref[0], 8)
    whole = own_ref[...] + other_ref[...]
    row = lax.broadcasted_iota(jnp.int32, (D, D), 0)
    col = lax.broadcasted_iota(jnp.int32, (D, D), 1)
    scale = jnp.sqrt(jnp.sum(jnp.where(row == col, whole, 0.0), keepdims=True)) + 1e-07
    gram[...] = whole / (scale * scale)
    rows = lax.broadcasted_iota(jnp.int32, (count, D), 0) + start
    cols = lax.broadcasted_iota(jnp.int32, (count, D), 1)
    out_ref[...] = jnp.where(rows == cols, 1.0, 0.0)

    def sweep(index, carry):
        every = slice(0, D)
        store_split(gram[...], (every, every), a_high, a_rest)

        def step_tile(tile, where_rows, where_cols):
            step = poly_second * gram[where_rows, where_cols] + poly_third * tile
            if where_rows == where_cols:
                tile_row = lax.broadcasted_iota(jnp.int32, (TILE, TILE), 0)
                tile_col = lax.broadcasted_iota(jnp.int32, (TILE, TILE), 1)
                step = step + jnp.where(tile_row == tile_col, poly_first, 0.0)
            store_split(step, (where_rows, where_cols), q_high, q_rest)

        mirrored_product(a, a, step_tile)
        store_split(out_ref[...], (slice(0, count), every), r_high, r_rest)
        out_ref[...] = close_product(r, q, slice(0, count), every)

        @pl.when(index < NS_ITERS - 1)
        def _():
            def half_tile(tile, where_rows, where_cols):
                store_split(tile, (where_rows, where_cols), b_high, b_rest)

            def gram_tile(tile, where_rows, where_cols):
                gram[where_rows, where_cols] = tile

            mirrored_product(q, a, half_tile)
            mirrored_product(b, q, gram_tile)

        return carry

    lax.fori_loop(0, NS_ITERS, sweep, 0)
    both = jnp.concatenate(split_low(out_ref[...] / scale), axis=0)
    for place in range(0, cols_ref.shape[1], D):
        spot = slice(place, place + D)
        product = matmul(both, cols_ref[:, spot])
        polar_ref[:, spot] = (product[:count] + product[count:]).astype(jnp.bfloat16)

def polar_rows(start, own, other, columns, count):
    half = pltpu.VMEM((D, D), jnp.bfloat16)
    short = pltpu.VMEM((count, D), jnp.bfloat16)
    return pl.pallas_call(
        polar_kernel,
        in_specs=[pl.BlockSpec(memory_space=pltpu.SMEM)]
        + [pl.BlockSpec(memory_space=pltpu.VMEM)] * 3,
        out_specs=pl.BlockSpec(memory_space=pltpu.VMEM),
        out_shape=jax.ShapeDtypeStruct((count, columns.shape[1]), jnp.bfloat16),
        scratch_shapes=[pltpu.VMEM((count, D), jnp.float32), pltpu.VMEM((D, D), jnp.float32)]
        + [half] * 6
        + [short] * 2,
        compiler_params=pltpu.CompilerParams(vmem_limit_bytes=40 << 20),
        name="polar_rows",
    )(start, own, other, columns)


def per_device(
    size,
    tokens,
    cotangent,
    counts,
    lengths,
    w_qkv,
    w_out,
    w_up,
    w_down,
    vectors,
    mom_qkv,
    mom_out,
    mom_up,
    mom_down,
    adam_first,
    adam_second,
):
    me = lax.axis_index("fsdp")
    core = lax.axis_index("row")
    slots = lengths.shape[0]
    rows = tokens.shape[0]
    up_rows = FF // D
    low = jnp.bfloat16

    block_rows = D // size
    qkv_half, up_half = w_qkv.shape[1], w_up.shape[1]
    vec_rows = vectors.shape[0]
    narrow = qkv_half - D

    def pick_core(early, late):
        return jnp.where(core == 0, early, late)

    def turn(values, cut):
        return pick_core(values, jnp.concatenate([values[:, cut:], values[:, :cut]], axis=1))

    vec_block = jnp.pad(vectors.T, ((0, 0), (0, VEC_PAD - vec_rows))).astype(low)
    first_block = jnp.concatenate([turn(w_qkv.astype(low), narrow), vec_block], axis=1)
    second_block = jnp.concatenate([w_up.astype(low), w_out.astype(low)], axis=1)
    third_block = w_down.astype(low)
    first_pieces = together(*send_high(first_block, size), second_block)
    second_block = first_pieces[-1]
    first_pieces = send_low(sort_high(first_pieces[:4], size), size)
    second_pieces = send_high(second_block, size)
    *pieces, third_block = together(*first_pieces, *second_pieces, third_block)
    first_own = sort_low(pieces[:4])
    second_pieces = send_low(sort_high(pieces[4:], size), size)
    third_pieces = send_high(third_block, size)
    first_other = swap_cores(first_own)

    spots = pick_core(jnp.array(SPOTS[0], jnp.int32), jnp.array(SPOTS[1], jnp.int32))
    live = jnp.arange(slots) % CAP < counts.reshape(-1)[jnp.arange(slots) // CAP]
    info = jnp.concatenate(
        [core.reshape(1).astype(jnp.int32), lengths, spots, jnp.where(live, lengths, 0)]
    )
    vec, bias_up, bias_own, bias_other = vector_tables(info, first_own, first_other)
    qkv_own, qkv_other = first_own[:, :qkv_half], first_other[:, :qkv_half]
    projected = jnp.concatenate(
        [
            (matmul(tokens, qkv_own) + bias_own[:1]).astype(low),
            (matmul(tokens, qkv_other) + bias_other[:1]).astype(low),
        ],
        axis=1,
    )
    context, log_total = attention(info, projected, slots)
    context, *pieces = together(context, *second_pieces, *third_pieces)
    second_own = sort_low(pieces[:4])
    third_pieces = send_low(sort_high(pieces[4:], size), size)
    second_other = swap_cores(second_own)
    xhat_one, rstd_one, hidden_low, act_low, slope = raise_rows(
        info, vec, bias_up, tokens, context, second_own, second_other
    )
    act_low, *third_pieces = together(act_low, *third_pieces)
    third_own = sort_low(third_pieces)
    third_other = swap_cores(third_own)
    layer_out, top_grad, branch_low, high_sums = lower_rows(
        info, vec, xhat_one, act_low, cotangent, third_own, third_other
    )

    leaving = matmul_tn(branch_low, act_low[:, up_half:]).astype(low)
    leaving, branch_low = together(leaving, branch_low)
    down_arrived = swap_cores(leaving)
    down_own = matmul_tn(branch_low, act_low[:, :up_half])
    down_own, down_arrived, branch_low = together(down_own, down_arrived, branch_low)
    down_kept, down_sent = leave_low([down_own + down_arrived.astype(jnp.float32)], size)
    pre_low, skip_grad, attn_low, context_grad, low_sums, bias_sums = pull_rows(
        info,
        vec,
        xhat_one,
        rstd_one,
        slope,
        top_grad,
        branch_low,
        (second_own, second_other),
        (third_own, third_other),
    )
    pre_low, *down_sent = together(pre_low, *down_sent)
    down_kept, down_sent = leave_high(down_kept, down_sent, size)
    out_own = pick_core(attn_low[:, : D // 2], attn_low[:, D // 2 :])
    out_other = pick_core(attn_low[:, D // 2 :], attn_low[:, : D // 2])
    leaving = jnp.concatenate(
        [
            matmul_tn(hidden_low, pre_low[:, up_half:]).astype(low),
            matmul_tn(context, out_other).astype(low),
        ],
        axis=1,
    )
    leaving, context_grad = together(leaving, context_grad)
    wide_arrived = swap_cores(leaving)
    up_own = matmul_tn(hidden_low, pre_low[:, :up_half])
    out_own = matmul_tn(context, out_own)
    up_own, out_own, wide_arrived, context_grad = together(
        up_own, out_own, wide_arrived, context_grad
    )
    wide_arrived = wide_arrived.astype(jnp.float32)
    wide_kept, wide_sent = leave_low(
        [up_own + wide_arrived[:, :up_half], out_own + wide_arrived[:, up_half:]], size
    )
    parts = attention_pull(info, projected, context_grad, log_total, slots, 0, None)
    parts, wide_sent, down_sent = together(parts, wide_sent, down_sent)
    (grad_down,) = add_four(down_kept, down_sent)
    moment_down = moment_decay * mom_down + grad_down
    down_pieces = send_high(moment_down.astype(low), size)
    wide_kept, wide_sent = leave_high(wide_kept, wide_sent, size)
    for slot in range(1, slots):
        parts = attention_pull(info, projected, context_grad, log_total, slots, slot, parts)
    parts, wide_sent, down_pieces = together(parts, wide_sent, down_pieces)
    main_own, main_other, keys, head_sums = parts
    grad_own = jnp.concatenate([main_own, keys[:, :narrow]], axis=1)
    grad_other = jnp.concatenate([main_other, keys[:, narrow:]], axis=1)
    leaving = matmul_tn(tokens, grad_other).astype(low)
    leaving, grad_own = together(leaving, grad_own)
    qkv_arrived = swap_cores(leaving)
    vector_grad = vector_grads(info, low_sums, high_sums, bias_sums, head_sums)
    vector_grad = vector_grad + swap_cores(vector_grad)
    vector_part = pick_core(vector_grad[:vec_rows], vector_grad[vec_rows : 2 * vec_rows])
    vector_part = jnp.pad(vector_part, ((0, VEC_PAD - vec_rows), (0, 0))).T
    grad_up, grad_out = add_four(wide_kept, wide_sent)
    moment_up = moment_decay * mom_up + grad_up
    moment_out = moment_decay * mom_out + grad_out
    wide_block = jnp.concatenate([moment_up.astype(low), moment_out.astype(low)], axis=1)
    qkv_part = matmul_tn(tokens, grad_own)
    qkv_part, vector_part, qkv_arrived, wide_block, grad_own = together(
        qkv_part, vector_part, qkv_arrived, wide_block, grad_own
    )
    qkv_kept, qkv_sent = leave_low(
        [qkv_part + qkv_arrived.astype(jnp.float32), vector_part], size
    )
    wide_pieces = send_high(wide_block, size)
    input_grad = skip_grad + matmul_nt(grad_own, qkv_own) + matmul_nt(grad_other, qkv_other)
    down_rows = merge_rows(sort_high(down_pieces, size))
    input_grad, down_rows, qkv_sent, wide_pieces = together(
        input_grad, down_rows, qkv_sent, wide_pieces
    )
    qkv_kept, qkv_sent = leave_high(qkv_kept, qkv_sent, size)
    wide_rows = merge_rows(sort_high(wide_pieces, size))
    mom_turned = turn(mom_qkv, narrow)
    wide_rows, mom_turned, qkv_sent = together(wide_rows, mom_turned, qkv_sent)
    grad_turned, grad_vectors = add_four(qkv_kept, qkv_sent)
    qkv_pieces = send_high((moment_decay * mom_turned + grad_turned).astype(low), size)
    grad_qkv = turn(grad_turned, D)
    moment_qkv = moment_decay * mom_qkv + grad_qkv
    grad_vectors = grad_vectors[:, :vec_rows].T
    grad_qkv, moment_qkv, qkv_pieces = together(grad_qkv, moment_qkv, qkv_pieces)

    qkv_rows = merge_rows(sort_high(qkv_pieces, size))
    place = me % GROUP

    def widen(values):
        return jnp.pad(values, ((0, 0), (0, WIDE - values.shape[1])))

    matrices = (
        widen(qkv_rows),
        widen(wide_rows[:, up_half:]),
        wide_rows[:, :up_half],
        down_rows,
    )

    def matrix_at(which):
        lower = jnp.where(which == 0, matrices[0], matrices[1])
        upper = jnp.where(which == 2, matrices[2], matrices[3])
        return jnp.where(which < 2, lower, upper)

    pieces = []
    for step in range(GROUP):
        piece = matrix_at(place ^ step).reshape(-1, block_rows, WIDE)
        pieces.append(flip(piece, step, size) if step else piece)
    columns = sort_low(pieces)
    for bit in range(2, size.bit_length() - 3, 2):
        columns = sort_low(send_four(columns.reshape(4, -1, WIDE), bit, size))
    gram = matmul_nt(columns, columns)
    start = ((me - place) * block_rows).reshape(1).astype(jnp.int32)
    polar = polar_rows(start, gram, swap_cores(gram), columns, GROUP * block_rows)
    polar = polar.reshape(GROUP, block_rows, WIDE)
    arrived = []
    for step in range(GROUP):
        block = lax.dynamic_index_in_dim(polar, place ^ step, 0, keepdims=False)
        arrived.append(flip(block, step, size) if step else block)
    arrived = sort_four(arrived, 0, 0)
    masters = (w_qkv, w_out, w_up, w_down)
    counts_of = (3 * D, D, FF, FF)
    updated = []
    for index in range(GROUP):
        ortho = arrived[index][:, : masters[index].shape[1]].astype(jnp.float32)
        if index == 0:
            ortho = turn(ortho, D)
        updated.append(
            masters[index] * (1.0 - muon_rate * decay_rate)
            - muon_rate * 0.2 * math.sqrt(counts_of[index]) * ortho
        )

    first_moment = beta_first * adam_first + (1.0 - beta_first) * grad_vectors
    second_moment = beta_second * adam_second + (1.0 - beta_second) * grad_vectors * grad_vectors
    direction = (
        first_moment
        / (1.0 - beta_first**STEP)
        / (jnp.sqrt(second_moment / (1.0 - beta_second**STEP)) + adam_eps)
    )
    new_vectors = vectors - adam_rate * (direction + decay_rate * vectors)
    return (
        layer_out,
        input_grad,
        grad_qkv,
        grad_out,
        grad_up,
        grad_down,
        grad_vectors,
        moment_qkv,
        moment_out,
        moment_up,
        moment_down,
        updated[0],
        updated[1],
        updated[2],
        updated[3],
        first_moment,
        second_moment,
        new_vectors,
    )


def solution(mesh):
    size = mesh.shape["fsdp"]

    def run(*arrays):
        return per_device(size, *arrays)

    weight = P("fsdp", "row")
    vector = P("row", "fsdp")
    sample = P(("fsdp", "row"), None)
    return jax.shard_map(
        run,
        mesh=mesh,
        in_specs=(sample, sample, sample, P(("fsdp", "row")))
        + (weight,) * 4
        + (vector,)
        + (weight,) * 4
        + (vector,) * 2,
        out_specs=(sample, sample)
        + (weight,) * 4
        + (vector,)
        + (weight,) * 8
        + (vector,) * 3,
        check_vma=False,
    )
```

```python
import math

import jax
import jax.numpy as jnp
from jax import lax
from jax.experimental import pallas as pl
from jax.experimental.layout import Layout, with_layout_constraint
from jax.experimental.pallas import tpu as pltpu
from jax.sharding import PartitionSpec as P

D = 768
FF = 3072
HEADS = 12
HEAD_DIM = 64
SEQ = 512
CAP = 1
MICRO = 2
NS_ITERS = 5
STEP = 10

norm_eps = 1e-05
mask_fill = -1e30
poly_first = 3.4445
poly_second = -4.775
poly_third = 2.0315
muon_rate = 0.2
adam_rate = 0.8
decay_rate = 0.01
moment_decay = 0.5
beta_first = 0.9
beta_second = 0.98
adam_eps = 1e-06

SWAP = [(0, 1), (1, 0)]
VEC_PAD = 128
GROUP = 4
TILE = 256
CHUNK = 256
ROWS = 256
VROWS = 8 + FF // D
SMALL = pl.CostEstimate(flops=1 << 20, bytes_accessed=1 << 16, transcendentals=0)
PAIR = 2 * HEAD_DIM
PAIRS = HEADS // 2
BLOCKS = 3 * PAIRS
INFO = 1 + CAP * MICRO
WIDE = FF // 2
ORDER = (tuple(range(9)), tuple(range(12, 18)) + tuple(range(9, 12)))
SPOTS = tuple(
    tuple((ORDER[core] + ORDER[1 - core]).index(block) for block in range(BLOCKS))
    for core in range(2)
)


def matmul(former, latter):
    return jnp.dot(former, latter, preferred_element_type=jnp.float32)


def matmul_tn(former, latter):
    return lax.dot_general(
        former, latter, (((0,), (0,)), ((), ())), preferred_element_type=jnp.float32
    )


def matmul_nt(former, latter):
    return lax.dot_general(
        former, latter, (((1,), (1,)), ((), ())), preferred_element_type=jnp.float32
    )


def by_rows(values):
    return with_layout_constraint(values, Layout(major_to_minor=tuple(range(values.ndim))))


def flip(values, mask, size):
    return by_rows(lax.ppermute(by_rows(values), "fsdp", [(i, i ^ mask) for i in range(size)]))


def swap_cores(values):
    return by_rows(lax.ppermute(by_rows(values), "row", SWAP))


def together(*values):
    return lax.optimization_barrier(values)


def my_bit(bit):
    return (lax.axis_index("fsdp") >> bit) & 1


def pair_of(bit):
    return (lax.axis_index("fsdp") >> bit) & 3


def send_four(values, bit, size):
    return [values] + [flip(values, step << bit, size) for step in (1, 2, 3)]


def sort_four(pieces, bit, axis):
    low, high = my_bit(bit) == 1, my_bit(bit + 1) == 1
    first = jnp.where(low, jnp.stack(pieces[1::-1], axis), jnp.stack(pieces[:2], axis))
    second = jnp.where(low, jnp.stack(pieces[:1:-1], axis), jnp.stack(pieces[2:], axis))
    return jnp.where(
        high,
        jnp.concatenate([second, first], axis),
        jnp.concatenate([first, second], axis),
    )


def merge_rows(values):
    return values.reshape(-1, values.shape[-1])


def send_high(block, size):
    return send_four(block, size.bit_length() - 3, size)


def sort_high(pieces, size):
    return sort_four(pieces, size.bit_length() - 3, 0)


def send_low(values, size):
    for bit in range(size.bit_length() - 5, 0, -2):
        values = sort_four(send_four(values, bit, size), bit, -3)
    return send_four(values, 0, size)


def sort_low(pieces):
    return merge_rows(sort_four(pieces, 0, -3))


def pick_four(parts, axis, place):
    return [lax.dynamic_index_in_dim(part, place, axis, keepdims=False) for part in parts]


def split_four(parts, axis, bit):
    mine = pair_of(bit)
    leaving = []
    for step in (1, 2, 3):
        pieces = pick_four(parts, axis, mine ^ step)
        leaving.append(jnp.concatenate([part.astype(jnp.bfloat16) for part in pieces], axis=-1))
    return pick_four(parts, axis, mine), leaving


def fly_four(leaving, bit, size):
    return [flip(piece, step << bit, size) for step, piece in zip((1, 2, 3), leaving)]


def split_two(parts, axis, bit):
    mine = my_bit(bit)
    pieces = pick_four(parts, axis, 1 - mine)
    leaving = jnp.concatenate([part.astype(jnp.bfloat16) for part in pieces], axis=-1)
    return pick_four(parts, axis, mine), leaving


def place_two(values, arrived, bit, axis):
    return jnp.where(
        my_bit(bit) == 1,
        jnp.stack([arrived, values], axis),
        jnp.stack([values, arrived], axis),
    )


def add_four(kept, arrived):
    totals, place = [], 0
    for part in kept:
        cols = slice(place, place + part.shape[-1])
        place = cols.stop
        for piece in arrived:
            part = part + piece[..., cols].astype(jnp.float32)
        totals.append(part)
    return totals


def split_low(parts, size):
    shape = (4,) * ((size.bit_length() - 1) // 2) + (D // size, -1)
    parts = [part.reshape(shape) for part in parts]
    return split_four(parts, len(shape) - 3, 0)


def fly_low(leaving, size):
    return fly_four(leaving, 0, size)


def add_low(kept, arrived, size):
    parts = add_four(kept, arrived)
    for bit in range(2, size.bit_length() - 3, 2):
        kept, leaving = split_four(parts, parts[0].ndim - 3, bit)
        parts = add_four(kept, fly_four(leaving, bit, size))
    return parts


def split_high(kept, arrived, size):
    return split_four(add_low(kept, arrived, size), 0, size.bit_length() - 3)


def split_near(kept, arrived, size):
    parts = [part.reshape((2, 2) + part.shape[1:]) for part in add_low(kept, arrived, size)]
    return split_two(parts, 1, size.bit_length() - 3)


def split_far(kept, arrived, size):
    return split_two(add_four(kept, [arrived]), 0, size.bit_length() - 2)


def fly_near(values, size):
    return flip(values, 1 << size.bit_length() - 3, size)


def fly_far(values, size):
    return flip(values, 1 << size.bit_length() - 2, size)


def place_far(values, arrived, size):
    return place_two(values, arrived, size.bit_length() - 2, 0)


def place_near(values, arrived, size):
    return merge_rows(place_two(values, arrived, size.bit_length() - 3, 1))


def fly_high(leaving, size):
    return fly_four(leaving, size.bit_length() - 3, size)


erf_slope = 0.3275911
erf_terms = (1.061405429, -1.453152027, 1.421413741, -0.284496736, 0.254829592)


def gelu_parts(pre_act):
    bell = jnp.exp(pre_act * pre_act * -0.5)
    inverse = 1.0 / (1.0 + jnp.abs(pre_act) * (erf_slope * math.sqrt(0.5)))
    poly = 0.5 * erf_terms[0] * inverse + 0.5 * erf_terms[1]
    for term in erf_terms[2:]:
        poly = poly * inverse + 0.5 * term
    tail = poly * inverse * bell
    cdf = jnp.where(pre_act < 0.0, tail, 1.0 - tail)
    return pre_act * cdf, cdf + pre_act * bell * (1.0 / math.sqrt(2.0 * math.pi))


def norm_parts(values):
    center = values - jnp.mean(values, axis=-1, keepdims=True)
    rstd = lax.rsqrt(jnp.mean(center * center, axis=-1, keepdims=True) + norm_eps)
    return center * rstd, rstd


def norm_pull(grad, gain, xhat, rstd):
    scaled = grad * gain
    return rstd * (
        scaled
        - jnp.mean(scaled, axis=-1, keepdims=True)
        - xhat * jnp.mean(scaled * xhat, axis=-1, keepdims=True)
    )


def head_lanes(shape, head):
    lane = lax.broadcasted_iota(jnp.int32, shape, 1)
    return (lane >= HEAD_DIM) if head else (lane < HEAD_DIM), lane == (0 if head else HEAD_DIM)


def head_operands(query, key, length, head):
    inside, spare = head_lanes(query.shape, head)
    zero = jnp.zeros_like(query)
    query_in = jnp.where(inside, query * jnp.bfloat16(0.125), zero)
    query_mask = jnp.where(spare, jnp.ones_like(query), query_in)
    row = lax.broadcasted_iota(jnp.int32, query.shape, 0)
    fill = jnp.where(row < length, 0.0, mask_fill).astype(jnp.bfloat16)
    key_mask = jnp.where(inside, key, jnp.where(spare, fill, zero))
    return query_in, query_mask, key_mask, inside


def attention_kernel(info, query_ref, key_ref, value_ref, ctx_ref, total_ref):
    length = info[1 + pl.program_id(0)]
    query, key = query_ref[...], key_ref[...]
    value = jnp.transpose(value_ref[...])
    operands = [head_operands(query, key, length, head) for head in range(2)]
    scores = [matmul_nt(operand[2], operand[1]) for operand in operands]
    parts = []
    for head in range(2):
        top = jnp.max(scores[head], axis=0, keepdims=True)
        powers = jnp.exp(scores[head] - top)
        total = jnp.sum(powers, axis=0, keepdims=True)
        probs = (powers * (1.0 / total)).astype(jnp.bfloat16)
        total_ref[0, 0, head : head + 1, :] = top + jnp.log(total)
        parts.append(matmul(value[head * HEAD_DIM : (head + 1) * HEAD_DIM], probs))
    ctx_ref[...] = jnp.transpose(jnp.concatenate(parts, axis=0)).astype(jnp.bfloat16)


def attention_pull_kernel(
    info,
    query_ref,
    key_ref,
    value_ref,
    grad_ref,
    total_ref,
    own_ref,
    other_ref,
    keys_ref,
    sum_ref,
    queries_ref,
):
    length = info[1 + pl.program_id(0)]
    query, key, value, grad = query_ref[...], key_ref[...], value_ref[...], grad_ref[...]
    operands = [head_operands(query, key, length, head) for head in range(2)]
    grads = [jnp.where(operand[3], grad, jnp.zeros_like(grad)) for operand in operands]
    flat_key = jnp.transpose(key * jnp.bfloat16(0.125))
    jobs = [(head, first) for first in range(0, SEQ, CHUNK) for head in range(2)]

    def begin(head, first):
        spot = slice(first, first + CHUNK)
        return (
            matmul_nt(operands[head][2], operands[head][1][spot]),
            matmul_nt(value, grads[head][spot]),
        )

    ready = begin(*jobs[0])
    key_grad = value_grad = jnp.zeros((SEQ, PAIR), jnp.float32)
    flat = []
    for index, (head, first) in enumerate(jobs):
        scores, prob_grad = ready
        if index + 1 < len(jobs):
            ready = begin(*jobs[index + 1])
        spot = slice(first, first + CHUNK)
        probs = jnp.exp(scores - total_ref[0, 0, head : head + 1, spot])
        row_dot = jnp.sum(probs * prob_grad, axis=0, keepdims=True)
        score_grad = (probs * (prob_grad - row_dot)).astype(jnp.bfloat16)
        value_grad += matmul(probs.astype(jnp.bfloat16), grads[head][spot])
        key_grad += matmul(score_grad, operands[head][0][spot])
        flat.append(matmul(flat_key[head * HEAD_DIM : (head + 1) * HEAD_DIM], score_grad))
        if head:
            queries_ref[spot, :] = jnp.transpose(jnp.concatenate(flat, axis=0)).astype(jnp.bfloat16)
            flat = []
    query_grad = queries_ref[...]
    value_grad = value_grad.astype(jnp.bfloat16)
    early = info[0] == 0
    own_ref[...] = jnp.where(early, query_grad, value_grad)
    other_ref[...] = jnp.where(early, value_grad, query_grad)
    keys_ref[...] = key_grad.astype(jnp.bfloat16)
    sum_ref[0, 0, 0:1, :] = jnp.sum(query_grad.astype(jnp.float32), axis=0, keepdims=True)
    sum_ref[0, 0, 1:2, :] = jnp.sum(value_grad.astype(jnp.float32), axis=0, keepdims=True)


def pick(kind):
    def spot(s, p, info):
        return s, info[INFO + kind * PAIRS + p]

    return pl.BlockSpec((SEQ, PAIR), spot)


def pair_spec():
    return pl.BlockSpec((SEQ, PAIR), lambda s, p, info: (s, p))


def pair_rows(width):
    return pl.BlockSpec((1, 1, 2, width), lambda s, p, info: (s, p, 0, 0))


def attention(info, qkv, slots):
    rows = qkv.shape[0]
    return pl.pallas_call(
        attention_kernel,
        grid_spec=pltpu.PrefetchScalarGridSpec(
            num_scalar_prefetch=1,
            grid=(slots, PAIRS),
            in_specs=[pick(kind) for kind in range(3)],
            out_specs=[pair_spec(), pair_rows(SEQ)],
        ),
        out_shape=[
            jax.ShapeDtypeStruct((rows, D), jnp.bfloat16),
            jax.ShapeDtypeStruct((slots, PAIRS, 2, SEQ), jnp.float32),
        ],
        cost_estimate=SMALL,
        name="attention",
    )(info, qkv, qkv, qkv)


def attention_pull(info, qkv, grad, log_total, slots):
    rows = qkv.shape[0]

    def key_spot(s, p, info):
        return s, lax.rem(p + info[0] * (PAIRS // 2), PAIRS)

    table = jax.ShapeDtypeStruct((rows, D), jnp.bfloat16)
    return pl.pallas_call(
        attention_pull_kernel,
        grid_spec=pltpu.PrefetchScalarGridSpec(
            num_scalar_prefetch=1,
            grid=(slots, PAIRS),
            in_specs=[pick(kind) for kind in range(3)] + [pair_spec(), pair_rows(SEQ)],
            out_specs=[
                pair_spec(),
                pair_spec(),
                pl.BlockSpec((SEQ, PAIR), key_spot),
                pair_rows(PAIR),
            ],
            scratch_shapes=[pltpu.VMEM((SEQ, PAIR), jnp.bfloat16)],
        ),
        out_shape=[table] * 3 + [jax.ShapeDtypeStruct((slots, PAIRS, 2, PAIR), jnp.float32)],
        cost_estimate=SMALL,
        name="attention_pull",
    )(info, qkv, qkv, qkv, grad, log_total)


def join_halves(core, own, other):
    return jnp.where(
        core == 0,
        jnp.concatenate([own, other], axis=1),
        jnp.concatenate([other, own], axis=1),
    )


def vector_kernel(info, own_ref, other_ref, vec_ref, bias_ref, own_bias_ref, other_bias_ref):
    early_core = info[0] == 0
    rows = VROWS // 2
    own = jnp.transpose(own_ref[...].astype(jnp.float32))[:rows]
    other = jnp.transpose(other_ref[...].astype(jnp.float32))[:rows]
    vec = jnp.concatenate(
        [jnp.where(early_core, own, other), jnp.where(early_core, other, own)], axis=0
    )
    vec_ref[0:VROWS, :] = vec
    up_rows = FF // D
    for place in range(up_rows):
        early, late = 5 + place, 5 + (place + up_rows // 2) % up_rows
        row = jnp.where(early_core, vec[early : early + 1], vec[late : late + 1])
        bias_ref[0:1, place * D : (place + 1) * D] = row
    own_bias_ref[...] = jnp.zeros_like(own_bias_ref)
    other_bias_ref[...] = jnp.zeros_like(other_bias_ref)
    own_bias_ref[0:1, :D] = jnp.where(early_core, vec[0:1], vec[1:2])
    other_bias_ref[0:1, :D] = jnp.where(early_core, vec[1:2], vec[0:1])


def vector_tables(info, own, other):
    half = own.shape[1] - VEC_PAD
    spec = pl.BlockSpec((D, VEC_PAD), lambda i: (0, half // VEC_PAD))
    shapes = [(16, D), (8, FF), (8, half), (8, half)]
    return pl.pallas_call(
        vector_kernel,
        grid=(1,),
        in_specs=[pl.BlockSpec(memory_space=pltpu.SMEM), spec, spec],
        out_specs=[pl.BlockSpec(shape, lambda i: (0, 0)) for shape in shapes],
        out_shape=[jax.ShapeDtypeStruct(shape, jnp.float32) for shape in shapes],
        name="vector_tables",
    )(info, own, other)


def vector_grad_kernel(info, low_ref, high_ref, bias_ref, head_ref, out_ref):
    early_core = info[0] == 0
    out_ref[...] = jnp.zeros_like(out_ref)
    for pair in range(PAIRS):
        cols = slice(pair * PAIR, (pair + 1) * PAIR)
        out_ref[0:2, cols] = jnp.sum(head_ref[:, pair], axis=0)
    out_ref[2:5, :] = low_ref[0:3, :]
    up_rows = FF // D
    for place in range(up_rows):
        late = (place + up_rows // 2) % up_rows
        out_ref[5 + place : 6 + place, :] = jnp.where(
            early_core,
            bias_ref[0:1, place * D : (place + 1) * D],
            bias_ref[0:1, late * D : (late + 1) * D],
        )
    out_ref[5 + up_rows : 8 + up_rows, :] = high_ref[0:3, :]


def vector_grads(info, low_sums, high_sums, bias_sums, head_sums):
    whole = pl.BlockSpec(memory_space=pltpu.VMEM)
    return pl.pallas_call(
        vector_grad_kernel,
        in_specs=[pl.BlockSpec(memory_space=pltpu.SMEM)] + [whole] * 4,
        out_specs=whole,
        out_shape=jax.ShapeDtypeStruct((16, D), jnp.float32),
        name="vector_grads",
    )(info, low_sums, high_sums, bias_sums, head_sums)


def hidden_pieces(own, other):
    return [
        (ref, slice(first, first + D), place + first)
        for place, ref in ((0, own), (WIDE, other))
        for first in range(0, WIDE, D)
    ]


OUT_COLS = slice(WIDE, WIDE + D // 2)


def raise_kernel(
    info,
    vec_ref,
    bias_ref,
    x_ref,
    ctx_ref,
    own,
    other,
    xhat_ref,
    rstd_ref,
    low_ref,
    own_act_ref,
    other_act_ref,
    slope_ref,
):
    ctx = ctx_ref[...]
    attended = join_halves(info[0], matmul(ctx, own[:, OUT_COLS]), matmul(ctx, other[:, OUT_COLS]))
    xhat, rstd = norm_parts(x_ref[...].astype(jnp.float32) + (attended + vec_ref[2:3, :]))
    xhat_ref[...] = xhat
    rstd_ref[...] = jnp.broadcast_to(rstd, rstd_ref.shape)
    hidden = (xhat * vec_ref[3:4, :] + vec_ref[4:5, :]).astype(jnp.bfloat16)
    low_ref[...] = hidden
    for ref, cols, place in hidden_pieces(own, other):
        spot = slice(place, place + D)
        act, slope = gelu_parts(matmul(hidden, ref[:, cols]) + bias_ref[0:1, spot])
        act_ref = own_act_ref if place < WIDE else other_act_ref
        act_ref[:, cols] = act.astype(jnp.bfloat16)
        slope_ref[:, spot] = slope.astype(jnp.bfloat16)


def add_sums(ref, sums):
    first = pl.program_id(0) == 0
    for place, values in enumerate(sums):
        total = jnp.sum(values, axis=0, keepdims=True)
        spot = slice(place, place + 1)
        ref[spot, :] = jnp.where(first, total, ref[spot, :] + total)


def lower_kernel(
    info, vec_ref, xhat_ref, first_ref, second_ref, cot_ref, out_ref, grad_ref, low_ref, sum_ref
):
    first = pl.program_id(0) * ROWS
    hidden = xhat_ref[...] * vec_ref[3:4, :] + vec_ref[4:5, :]
    xhat, rstd = norm_parts(hidden + (first_ref[...] + second_ref[...] + vec_ref[9:10, :]))
    gain = vec_ref[10:11, :]
    out_ref[...] = (xhat * gain + vec_ref[11:12, :]).astype(jnp.bfloat16)
    limit = info[INFO + BLOCKS + lax.div(first, SEQ)]
    row = lax.broadcasted_iota(jnp.int32, (ROWS, 1), 0) + lax.rem(first, SEQ)
    cot = jnp.where(row < limit, cot_ref[...].astype(jnp.float32), 0.0)
    grad = norm_pull(cot, gain, xhat, rstd)
    grad_ref[...] = grad
    low = grad.astype(jnp.bfloat16)
    low_ref[...] = low
    add_sums(sum_ref, (low.astype(jnp.float32), cot * xhat, cot))


def pull_kernel(
    info,
    vec_ref,
    xhat_ref,
    rstd_ref,
    slope_ref,
    grad_ref,
    low_ref,
    up_own,
    up_other,
    own,
    other,
    own_pre_ref,
    other_pre_ref,
    skip_ref,
    attn_ref,
    ctx_ref,
    sum_ref,
    bias_ref,
):
    core = info[0]
    low = low_ref[...]
    hidden_grad = grad_ref[...]
    for down, up in zip(hidden_pieces(own, other), hidden_pieces(up_own, up_other)):
        ref, cols, place = down
        spot = slice(place, place + D)
        pre = matmul(low, ref[:, cols]) * slope_ref[:, spot].astype(jnp.float32)
        pre = pre.astype(jnp.bfloat16)
        pre_ref = own_pre_ref if place < WIDE else other_pre_ref
        pre_ref[:, cols] = pre
        hidden_grad = hidden_grad + matmul_nt(pre, up[0][:, up[1]])
    xhat = xhat_ref[...]
    skip = norm_pull(hidden_grad, vec_ref[3:4, :], xhat, rstd_ref[:, 0:1])
    skip_ref[...] = skip
    attn = skip.astype(jnp.bfloat16)
    attn_ref[...] = attn
    left, right = attn[:, : D // 2], attn[:, D // 2 :]
    ctx = matmul_nt(jnp.where(core == 0, left, right), up_own[:, OUT_COLS])
    ctx = ctx + matmul_nt(jnp.where(core == 0, right, left), up_other[:, OUT_COLS])
    ctx_ref[...] = ctx.astype(jnp.bfloat16)
    add_sums(sum_ref, (attn.astype(jnp.float32), hidden_grad * xhat, hidden_grad))
    add_sums(bias_ref.at[:, :WIDE], (own_pre_ref[...].astype(jnp.float32),))
    add_sums(bias_ref.at[:, WIDE:], (other_pre_ref[...].astype(jnp.float32),))


def row_spec(width):
    return pl.BlockSpec((ROWS, width), lambda i: (i, 0))


def whole_spec():
    return pl.BlockSpec(memory_space=pltpu.VMEM)


def row_call(kernel, name, in_specs, rows, outs, sums, flops, operands):
    shapes = [jax.ShapeDtypeStruct((rows, width), kind) for width, kind in outs]
    shapes += [jax.ShapeDtypeStruct((8, width), jnp.float32) for width in sums]
    return pl.pallas_call(
        kernel,
        grid=(rows // ROWS,),
        in_specs=[pl.BlockSpec(memory_space=pltpu.SMEM)] + in_specs,
        out_specs=[row_spec(width) for width, kind in outs]
        + [pl.BlockSpec((8, width), lambda i: (0, 0)) for width in sums],
        out_shape=shapes,
        compiler_params=pltpu.CompilerParams(vmem_limit_bytes=52 << 20),
        cost_estimate=SMALL,
        name=name,
    )(*operands)


def raise_rows(info, vec, bias, tokens, context, own, other):
    low, full = jnp.bfloat16, jnp.float32
    return row_call(
        raise_kernel,
        "raise_rows",
        [whole_spec()] * 2 + [row_spec(D)] * 2 + [whole_spec()] * 2,
        tokens.shape[0],
        [(D, full), (PAIR, full), (D, low), (WIDE, low), (WIDE, low), (FF, low)],
        [],
        14 << 30,
        (info, vec, bias, tokens, context, own, other),
    )


def lower_rows(info, vec, xhat, first, second, cotangent):
    low, full = jnp.bfloat16, jnp.float32
    return row_call(
        lower_kernel,
        "lower_rows",
        [whole_spec()] + [row_spec(D)] * 4,
        first.shape[0],
        [(D, low), (D, full), (D, low)],
        [D],
        4 << 30,
        (info, vec, xhat, first, second, cotangent),
    )


def pull_rows(info, vec, xhat, rstd, slope, grad, low_grad, up, down):
    low, full = jnp.bfloat16, jnp.float32
    return row_call(
        pull_kernel,
        "pull_rows",
        [whole_spec(), row_spec(D), row_spec(PAIR), row_spec(FF), row_spec(D), row_spec(D)]
        + [whole_spec()] * 4,
        xhat.shape[0],
        [(WIDE, low), (WIDE, low), (D, full), (D, low), (D, low)],
        [D, FF],
        18 << 30,
        (info, vec, xhat, rstd, slope, grad, low_grad, *up, *down),
    )


def split_rest(values):
    high = values.astype(jnp.bfloat16)
    return high, (values - high.astype(jnp.float32)).astype(jnp.bfloat16)

def store_split(values, where, high_ref, rest_ref):
    high_ref[where], rest_ref[where] = split_rest(values)

def close_product(left, right, rows, cols):
    left_high, left_rest = left[0][rows, :], left[1][rows, :]
    right_high, right_rest = right[0][:, cols], right[1][:, cols]
    return matmul(
        jnp.concatenate([left_high, left_high, left_rest], axis=1),
        jnp.concatenate([right_high, right_rest, right_high], axis=0),
    )


def mirrored_product(left, right, finish):
    for first in range(0, D, TILE):
        rows = slice(first, first + TILE)
        wide = close_product(left, right, rows, slice(first, D))
        for last in range(first, D, TILE):
            tile = wide[:, last - first : last - first + TILE]
            cols = slice(last, last + TILE)
            finish(tile, rows, cols)
            if first < last:
                finish(jnp.transpose(tile), cols, rows)


def polar_kernel(
    start_ref,
    own_ref,
    other_ref,
    cols_ref,
    polar_ref,
    out_ref,
    gram,
    a_high,
    a_rest,
    q_high,
    q_rest,
    b_high,
    b_rest,
    r_high,
    r_rest,
):
    a, q, b, r = (a_high, a_rest), (q_high, q_rest), (b_high, b_rest), (r_high, r_rest)
    count = out_ref.shape[0]
    start = pl.multiple_of(start_ref[0], 8)
    whole = own_ref[...] + other_ref[...]
    row = lax.broadcasted_iota(jnp.int32, (D, D), 0)
    col = lax.broadcasted_iota(jnp.int32, (D, D), 1)
    scale = jnp.sqrt(jnp.sum(jnp.where(row == col, whole, 0.0), keepdims=True)) + 1e-07
    gram[...] = whole / (scale * scale)
    rows = lax.broadcasted_iota(jnp.int32, (count, D), 0) + start
    cols = lax.broadcasted_iota(jnp.int32, (count, D), 1)
    out_ref[...] = jnp.where(rows == cols, 1.0, 0.0)

    def sweep(index, carry):
        every = slice(0, D)
        store_split(gram[...], (every, every), a_high, a_rest)

        def step_tile(tile, where_rows, where_cols):
            step = poly_second * gram[where_rows, where_cols] + poly_third * tile
            if where_rows == where_cols:
                tile_row = lax.broadcasted_iota(jnp.int32, (TILE, TILE), 0)
                tile_col = lax.broadcasted_iota(jnp.int32, (TILE, TILE), 1)
                step = step + jnp.where(tile_row == tile_col, poly_first, 0.0)
            store_split(step, (where_rows, where_cols), q_high, q_rest)

        mirrored_product(a, a, step_tile)
        store_split(out_ref[...], (slice(0, count), every), r_high, r_rest)
        out_ref[...] = close_product(r, q, slice(0, count), every)

        @pl.when(index < NS_ITERS - 1)
        def _():
            def half_tile(tile, where_rows, where_cols):
                store_split(tile, (where_rows, where_cols), b_high, b_rest)

            def gram_tile(tile, where_rows, where_cols):
                gram[where_rows, where_cols] = tile

            mirrored_product(q, a, half_tile)
            mirrored_product(b, q, gram_tile)

        return carry

    lax.fori_loop(0, NS_ITERS, sweep, 0)
    both = jnp.concatenate(split_rest(out_ref[...] / scale), axis=0)
    for place in range(0, cols_ref.shape[1], D):
        spot = slice(place, place + D)
        product = matmul(both, cols_ref[:, spot])
        polar_ref[:, spot] = (product[:count] + product[count:]).astype(jnp.bfloat16)

def polar_rows(start, own, other, columns, count):
    half = pltpu.VMEM((D, D), jnp.bfloat16)
    short = pltpu.VMEM((count, D), jnp.bfloat16)
    return pl.pallas_call(
        polar_kernel,
        in_specs=[pl.BlockSpec(memory_space=pltpu.SMEM)]
        + [pl.BlockSpec(memory_space=pltpu.VMEM)] * 3,
        out_specs=pl.BlockSpec(memory_space=pltpu.VMEM),
        out_shape=jax.ShapeDtypeStruct((count, columns.shape[1]), jnp.bfloat16),
        scratch_shapes=[pltpu.VMEM((count, D), jnp.float32), pltpu.VMEM((D, D), jnp.float32)]
        + [half] * 6
        + [short] * 2,
        compiler_params=pltpu.CompilerParams(vmem_limit_bytes=40 << 20),
        name="polar_rows",
    )(start, own, other, columns)


def per_device(
    size,
    tokens,
    cotangent,
    counts,
    lengths,
    w_qkv,
    w_out,
    w_up,
    w_down,
    vectors,
    mom_qkv,
    mom_out,
    mom_up,
    mom_down,
    adam_first,
    adam_second,
):
    me = lax.axis_index("fsdp")
    core = lax.axis_index("row")
    slots = lengths.shape[0]
    rows = tokens.shape[0]
    up_rows = FF // D
    low = jnp.bfloat16

    block_rows = D // size
    qkv_half, up_half = w_qkv.shape[1], w_up.shape[1]
    vec_rows = vectors.shape[0]
    narrow = qkv_half - D

    def pick_core(early, late):
        return jnp.where(core == 0, early, late)

    def turn(values, cut):
        return pick_core(values, jnp.concatenate([values[:, cut:], values[:, :cut]], axis=1))

    vec_block = jnp.pad(vectors.T, ((0, 0), (0, VEC_PAD - vec_rows))).astype(low)
    first_block = jnp.concatenate([turn(w_qkv.astype(low), narrow), vec_block], axis=1)
    second_block = jnp.concatenate([w_up.astype(low), w_out.astype(low)], axis=1)
    third_block = w_down.astype(low)
    near, far = size.bit_length() - 3, size.bit_length() - 2
    steps = [1 << near, 1 << far, 3 << near]
    first_pieces = send_high(first_block, size)
    second_pieces = [second_block, flip(second_block, steps[0], size)]
    first_pieces, second_pieces, third_block = together(first_pieces, second_pieces, third_block)
    first_pieces = send_low(sort_high(first_pieces, size), size)
    second_pieces += [flip(second_pieces[0], step, size) for step in steps[1:]]
    first_pieces, second_pieces, third_block = together(first_pieces, second_pieces, third_block)
    first_own = sort_low(first_pieces)
    first_other = swap_cores(first_own)
    second_pieces = send_low(sort_high(second_pieces, size), size)
    third_pieces = [third_block, flip(third_block, steps[0], size)]

    spots = pick_core(jnp.array(SPOTS[0], jnp.int32), jnp.array(SPOTS[1], jnp.int32))
    live = jnp.arange(slots) % CAP < counts.reshape(-1)[jnp.arange(slots) // CAP]
    info = jnp.concatenate(
        [core.reshape(1).astype(jnp.int32), lengths, spots, jnp.where(live, lengths, 0)]
    )
    vec, bias_up, bias_own, bias_other = vector_tables(info, first_own, first_other)
    qkv_own, qkv_other = first_own[:, :qkv_half], first_other[:, :qkv_half]
    projected = jnp.concatenate(
        [
            (matmul(tokens, qkv_own) + bias_own[:1]).astype(low),
            (matmul(tokens, qkv_other) + bias_other[:1]).astype(low),
        ],
        axis=1,
    )
    projected, third_pieces = together(projected, third_pieces)
    third_pieces += [flip(third_pieces[0], step, size) for step in steps[1:]]
    context, log_total = attention(info, projected, slots)
    context, second_pieces, third_pieces = together(context, second_pieces, third_pieces)
    second_own = sort_low(second_pieces)
    third_pieces = send_low(sort_high(third_pieces, size), size)
    second_other = swap_cores(second_own)
    xhat_one, rstd_one, hidden_low, act_own, act_other, slope = raise_rows(
        info, vec, bias_up, tokens, context, second_own, second_other
    )
    act_own, act_other, *third_pieces = together(act_own, act_other, *third_pieces)
    third_own = sort_low(third_pieces)
    third_other = swap_cores(third_own)
    branch = matmul_nt(act_own, third_own)
    branch, third_other = together(branch, third_other)
    layer_out, top_grad, branch_low, high_sums = lower_rows(
        info, vec, xhat_one, branch, matmul_nt(act_other, third_other), cotangent
    )

    full = jnp.float32
    leaving = matmul_tn(branch_low, act_other).astype(low)
    leaving, branch_low = together(leaving, branch_low)
    down_arrived = swap_cores(leaving)
    down_own = matmul_tn(branch_low, act_own)
    down_own, down_arrived, branch_low = together(down_own, down_arrived, branch_low)
    down_kept, leaving = split_low([down_own + down_arrived.astype(full)], size)
    leaving, branch_low = together(leaving, branch_low)
    down_sent = fly_low(leaving, size)
    pulled = pull_rows(
        info,
        vec,
        xhat_one,
        rstd_one,
        slope,
        top_grad,
        branch_low,
        (second_own, second_other),
        (third_own, third_other),
    )
    pulled, down_sent = together(pulled, down_sent)
    pre_own, pre_other, skip_grad, attn_low, context_grad, low_sums, bias_sums = pulled
    down_kept, leaving = split_near(down_kept, down_sent, size)
    leaving, pre_own, pre_other, attn_low = together(leaving, pre_own, pre_other, attn_low)
    down_sent = fly_near(leaving, size)
    up_leaving = matmul_tn(hidden_low, pre_other).astype(low)
    up_leaving, pre_own, attn_low, down_sent = together(up_leaving, pre_own, attn_low, down_sent)
    up_arrived = swap_cores(up_leaving)
    down_kept, down_leaving = split_far(down_kept, down_sent, size)
    out_own = pick_core(attn_low[:, : D // 2], attn_low[:, D // 2 :])
    out_other = pick_core(attn_low[:, D // 2 :], attn_low[:, : D // 2])
    out_arrived = swap_cores(matmul_tn(context, out_other).astype(low))
    up_own = matmul_tn(hidden_low, pre_own)
    out_own = matmul_tn(context, out_own)
    up_own, out_own, up_arrived, out_arrived = together(up_own, out_own, up_arrived, out_arrived)
    wide_kept, leaving = split_low(
        [up_own + up_arrived.astype(full), out_own + out_arrived.astype(full)], size
    )
    leaving, down_leaving, context_grad = together(leaving, down_leaving, context_grad)
    wide_sent = fly_low(leaving, size)
    down_sent = fly_far(down_leaving, size)
    parts = attention_pull(info, projected, context_grad, log_total, slots)
    parts, down_sent = together(parts, down_sent)

    grads = (parts[0], parts[1], parts[2][:, :narrow], parts[2][:, narrow:])
    main_leaving = matmul_tn(tokens, grads[1]).astype(low)
    keys_leaving = matmul_tn(tokens, grads[3]).astype(low)
    vector_grad = vector_grads(info, low_sums, high_sums, bias_sums, parts[3])
    main_leaving, keys_leaving, grads, vector_grad, wide_sent = together(
        main_leaving, keys_leaving, grads, vector_grad, wide_sent
    )
    wide_kept, leaving = split_near(wide_kept, wide_sent, size)
    leaving, grads = together(leaving, grads)
    wide_sent = fly_near(leaving, size)
    main_arrived, keys_arrived = swap_cores(main_leaving), swap_cores(keys_leaving)
    main_part, keys_part = matmul_tn(tokens, grads[0]), matmul_tn(tokens, grads[2])
    (grad_down,) = add_four(down_kept, [down_sent])
    moment_down = moment_decay * mom_down + grad_down
    main_part, keys_part, main_arrived, keys_arrived, grads, moment_down = together(
        main_part, keys_part, main_arrived, keys_arrived, grads, moment_down
    )
    qkv_kept, leaving = split_low(
        [main_part + main_arrived.astype(full), keys_part + keys_arrived.astype(full)], size
    )
    leaving, grads, down_block = together(leaving, grads, moment_down.astype(low))
    qkv_sent = fly_low(leaving, size)
    down_sent = fly_far(down_block, size)
    wide_sent, down_sent = together(wide_sent, down_sent)
    wide_kept, wide_leaving = split_far(wide_kept, wide_sent, size)
    wide_sent = fly_far(wide_leaving, size)
    qkv_sent, wide_sent, down_sent = together(qkv_sent, wide_sent, down_sent)
    grad_up, grad_out = add_four(wide_kept, [wide_sent])
    moment_up = moment_decay * mom_up + grad_up
    moment_out = moment_decay * mom_out + grad_out
    wide_block = jnp.concatenate([moment_up.astype(low), moment_out.astype(low)], axis=1)
    mom_turned = turn(mom_qkv, narrow)
    qkv_kept, leaving = split_high(qkv_kept, qkv_sent, size)
    down_pair = place_far(down_block, down_sent, size)
    leaving, down_pair, wide_block, grads, vector_grad, mom_turned = together(
        leaving, down_pair, wide_block, grads, vector_grad, mom_turned
    )
    qkv_sent = fly_high(leaving, size)
    wide_sent = fly_far(wide_block, size)
    down_sent = fly_near(down_pair, size)
    qkv_sent, wide_sent, down_sent = together(qkv_sent, wide_sent, down_sent)
    grad_main, grad_keys = add_four(qkv_kept, qkv_sent)
    grad_turned = jnp.concatenate([grad_main, grad_keys], axis=1)
    qkv_block = (moment_decay * mom_turned + grad_turned).astype(low)
    wide_pair = place_far(wide_block, wide_sent, size)
    qkv_block, grad_turned, wide_pair = together(qkv_block, grad_turned, wide_pair)
    qkv_pieces = send_high(qkv_block, size)
    wide_sent = fly_near(wide_pair, size)
    vector_grad = vector_grad + swap_cores(vector_grad)
    vector_arrived = flip(vector_grad, 1, size)
    down_rows = place_near(down_pair, down_sent, size)
    grad_qkv = turn(grad_turned, D)
    moment_qkv = moment_decay * mom_qkv + grad_qkv
    grad_qkv, moment_qkv, qkv_pieces, wide_sent, down_rows = together(
        grad_qkv, moment_qkv, qkv_pieces, wide_sent, down_rows
    )
    wide_rows = place_near(wide_pair, wide_sent, size)

    qkv_rows = merge_rows(sort_high(qkv_pieces, size))
    place = me % GROUP

    def widen(values):
        return jnp.pad(values, ((0, 0), (0, WIDE - values.shape[1])))

    matrices = (
        widen(qkv_rows),
        widen(wide_rows[:, up_half:]),
        wide_rows[:, :up_half],
        down_rows,
    )

    def matrix_at(which):
        lower = jnp.where(which == 0, matrices[0], matrices[1])
        upper = jnp.where(which == 2, matrices[2], matrices[3])
        return jnp.where(which < 2, lower, upper)

    pieces = []
    for step in range(GROUP):
        pieces.append(matrix_at(place ^ step).reshape(-1, block_rows, WIDE))
    pieces, grads, vector_grad, vector_arrived = together(
        pieces, grads, vector_grad, vector_arrived
    )
    pieces = pieces[:1] + [flip(pieces[step], step, size) for step in range(1, GROUP)]
    vector_grad = vector_grad + vector_arrived
    vector_arrived = flip(vector_grad, 2, size)
    input_grad = (
        skip_grad
        + matmul_nt(grads[0], qkv_own[:, :D])
        + matmul_nt(grads[1], qkv_other[:, :D])
        + matmul_nt(grads[2], qkv_own[:, D:])
        + matmul_nt(grads[3], qkv_other[:, D:])
    )
    pieces, input_grad, vector_grad, vector_arrived = together(
        pieces, input_grad, vector_grad, vector_arrived
    )
    columns = sort_low(pieces)
    for bit in range(2, size.bit_length() - 3, 2):
        columns = sort_low(send_four(columns.reshape(4, -1, WIDE), bit, size))
    gram = matmul_nt(columns, columns)
    start = ((me - place) * block_rows).reshape(1).astype(jnp.int32)
    vector_grad = vector_grad + vector_arrived
    gram, vector_grad = together(gram, vector_grad)
    gram_arrived = swap_cores(gram)
    vector_arrived = flip(vector_grad, 4, size)
    gram_arrived, vector_arrived = together(gram_arrived, vector_arrived)
    vector_grad = vector_grad + vector_arrived
    polar = polar_rows(start, gram, gram_arrived, columns, GROUP * block_rows)
    polar, vector_grad = together(polar, vector_grad)
    for bit in range(3, size.bit_length() - 1):
        vector_grad = vector_grad + flip(vector_grad, 1 << bit, size)
    grad_vectors = lax.dynamic_slice(
        vector_grad, (core * vec_rows, me * block_rows), (vec_rows, block_rows)
    )
    polar = polar.reshape(GROUP, block_rows, WIDE)
    arrived = []
    for step in range(GROUP):
        block = lax.dynamic_index_in_dim(polar, place ^ step, 0, keepdims=False)
        arrived.append(flip(block, step, size) if step else block)
    arrived = sort_four(arrived, 0, 0)
    masters = (w_qkv, w_out, w_up, w_down)
    counts_of = (3 * D, D, FF, FF)
    updated = []
    for index in range(GROUP):
        ortho = arrived[index][:, : masters[index].shape[1]].astype(jnp.float32)
        if index == 0:
            ortho = turn(ortho, D)
        updated.append(
            masters[index] * (1.0 - muon_rate * decay_rate)
            - muon_rate * 0.2 * math.sqrt(counts_of[index]) * ortho
        )

    first_moment = beta_first * adam_first + (1.0 - beta_first) * grad_vectors
    second_moment = beta_second * adam_second + (1.0 - beta_second) * grad_vectors * grad_vectors
    direction = (
        first_moment
        / (1.0 - beta_first**STEP)
        / (jnp.sqrt(second_moment / (1.0 - beta_second**STEP)) + adam_eps)
    )
    new_vectors = vectors - adam_rate * (direction + decay_rate * vectors)
    return (
        layer_out,
        input_grad,
        grad_qkv,
        grad_out,
        grad_up,
        grad_down,
        grad_vectors,
        moment_qkv,
        moment_out,
        moment_up,
        moment_down,
        updated[0],
        updated[1],
        updated[2],
        updated[3],
        first_moment,
        second_moment,
        new_vectors,
    )


def solution(mesh):
    size = mesh.shape["fsdp"]

    def run(*arrays):
        return per_device(size, *arrays)

    weight = P("fsdp", "row")
    vector = P("row", "fsdp")
    sample = P(("fsdp", "row"), None)
    return jax.shard_map(
        run,
        mesh=mesh,
        in_specs=(sample, sample, sample, P(("fsdp", "row")))
        + (weight,) * 4
        + (vector,)
        + (weight,) * 4
        + (vector,) * 2,
        out_specs=(sample, sample)
        + (weight,) * 4
        + (vector,)
        + (weight,) * 8
        + (vector,) * 3,
        check_vma=False,
    )
```

```python
import math

import jax
import jax.numpy as jnp
from jax import lax
from jax.experimental import pallas as pl
from jax.experimental.layout import Layout, with_layout_constraint
from jax.experimental.pallas import tpu as pltpu
from jax.sharding import PartitionSpec as P

D = 768
FF = 3072
HEADS = 12
HEAD_DIM = 64
SEQ = 512
CAP = 1
MICRO = 2
NS_ITERS = 5
STEP = 10

norm_eps = 1e-05
mask_fill = -1e30
poly_first = 3.4445
poly_second = -4.775
poly_third = 2.0315
muon_rate = 0.2
adam_rate = 0.8
decay_rate = 0.01
moment_decay = 0.5
beta_first = 0.9
beta_second = 0.98
adam_eps = 1e-06

SWAP = [(0, 1), (1, 0)]
VEC_PAD = 128
GROUP = 4
TILE = 256
CHUNK = 256
ROWS = 256
VROWS = 8 + FF // D
SMALL = pl.CostEstimate(flops=1 << 20, bytes_accessed=1 << 16, transcendentals=0)
PAIR = 2 * HEAD_DIM
PAIRS = HEADS // 2
BLOCKS = 3 * PAIRS
INFO = 1 + CAP * MICRO
WIDE = FF // 2
ORDER = (tuple(range(9)), tuple(range(12, 18)) + tuple(range(9, 12)))
SPOTS = tuple(
    tuple((ORDER[core] + ORDER[1 - core]).index(block) for block in range(BLOCKS))
    for core in range(2)
)


def matmul(former, latter):
    return jnp.dot(former, latter, preferred_element_type=jnp.float32)


def matmul_tn(former, latter):
    return lax.dot_general(
        former, latter, (((0,), (0,)), ((), ())), preferred_element_type=jnp.float32
    )


def matmul_nt(former, latter):
    return lax.dot_general(
        former, latter, (((1,), (1,)), ((), ())), preferred_element_type=jnp.float32
    )


def by_rows(values):
    return with_layout_constraint(values, Layout(major_to_minor=tuple(range(values.ndim))))


def flip(values, mask, size):
    return by_rows(lax.ppermute(by_rows(values), "fsdp", [(i, i ^ mask) for i in range(size)]))


def swap_cores(values):
    return by_rows(lax.ppermute(by_rows(values), "row", SWAP))


def together(*values):
    return lax.optimization_barrier(values)


def my_bit(bit):
    return (lax.axis_index("fsdp") >> bit) & 1


def pair_of(bit):
    return (lax.axis_index("fsdp") >> bit) & 3


def send_four(values, bit, size):
    return [values] + [flip(values, step << bit, size) for step in (1, 2, 3)]


def sort_four(pieces, bit, axis):
    low, high = my_bit(bit) == 1, my_bit(bit + 1) == 1
    first = jnp.where(low, jnp.stack(pieces[1::-1], axis), jnp.stack(pieces[:2], axis))
    second = jnp.where(low, jnp.stack(pieces[:1:-1], axis), jnp.stack(pieces[2:], axis))
    return jnp.where(
        high,
        jnp.concatenate([second, first], axis),
        jnp.concatenate([first, second], axis),
    )


def merge_rows(values):
    return values.reshape(-1, values.shape[-1])


def send_high(block, size):
    return send_four(block, size.bit_length() - 3, size)


def sort_high(pieces, size):
    return sort_four(pieces, size.bit_length() - 3, 0)


def send_low(values, size):
    for bit in range(size.bit_length() - 5, 0, -2):
        values = sort_four(send_four(values, bit, size), bit, -3)
    return send_four(values, 0, size)


def sort_low(pieces):
    return merge_rows(sort_four(pieces, 0, -3))


def pick_four(parts, axis, place):
    return [lax.dynamic_index_in_dim(part, place, axis, keepdims=False) for part in parts]


def split_four(parts, axis, bit):
    mine = pair_of(bit)
    leaving = []
    for step in (1, 2, 3):
        pieces = pick_four(parts, axis, mine ^ step)
        leaving.append(jnp.concatenate([part.astype(jnp.bfloat16) for part in pieces], axis=-1))
    return pick_four(parts, axis, mine), leaving


def fly_four(leaving, bit, size):
    return [flip(piece, step << bit, size) for step, piece in zip((1, 2, 3), leaving)]


def split_two(parts, axis, bit):
    mine = my_bit(bit)
    pieces = pick_four(parts, axis, 1 - mine)
    leaving = jnp.concatenate([part.astype(jnp.bfloat16) for part in pieces], axis=-1)
    return pick_four(parts, axis, mine), leaving


def place_two(values, arrived, bit, axis):
    return jnp.where(
        my_bit(bit) == 1,
        jnp.stack([arrived, values], axis),
        jnp.stack([values, arrived], axis),
    )


def add_four(kept, arrived):
    totals, place = [], 0
    for part in kept:
        cols = slice(place, place + part.shape[-1])
        place = cols.stop
        for piece in arrived:
            part = part + piece[..., cols].astype(jnp.float32)
        totals.append(part)
    return totals


def split_low(parts, size):
    shape = (4,) * ((size.bit_length() - 1) // 2) + (D // size, -1)
    parts = [part.reshape(shape) for part in parts]
    return split_four(parts, len(shape) - 3, 0)


def fly_low(leaving, size):
    return fly_four(leaving, 0, size)


def add_low(kept, arrived, size):
    parts = add_four(kept, arrived)
    for bit in range(2, size.bit_length() - 3, 2):
        kept, leaving = split_four(parts, parts[0].ndim - 3, bit)
        parts = add_four(kept, fly_four(leaving, bit, size))
    return parts


def split_high(kept, arrived, size):
    return split_four(add_low(kept, arrived, size), 0, size.bit_length() - 3)


def split_near(kept, arrived, size):
    parts = [part.reshape((2, 2) + part.shape[1:]) for part in add_low(kept, arrived, size)]
    return split_two(parts, 1, size.bit_length() - 3)


def split_far(kept, arrived, size):
    return split_two(add_four(kept, [arrived]), 0, size.bit_length() - 2)


def fly_near(values, size):
    return flip(values, 1 << size.bit_length() - 3, size)


def fly_far(values, size):
    return flip(values, 1 << size.bit_length() - 2, size)


def place_far(values, arrived, size):
    return place_two(values, arrived, size.bit_length() - 2, 0)


def place_near(values, arrived, size):
    return merge_rows(place_two(values, arrived, size.bit_length() - 3, 1))


def fly_high(leaving, size):
    return fly_four(leaving, size.bit_length() - 3, size)


erf_slope = 0.3275911
erf_terms = (1.061405429, -1.453152027, 1.421413741, -0.284496736, 0.254829592)


def gelu_parts(pre_act):
    bell = jnp.exp(pre_act * pre_act * -0.5)
    inverse = 1.0 / (1.0 + jnp.abs(pre_act) * (erf_slope * math.sqrt(0.5)))
    poly = 0.5 * erf_terms[0] * inverse + 0.5 * erf_terms[1]
    for term in erf_terms[2:]:
        poly = poly * inverse + 0.5 * term
    tail = poly * inverse * bell
    cdf = jnp.where(pre_act < 0.0, tail, 1.0 - tail)
    return pre_act * cdf, cdf + pre_act * bell * (1.0 / math.sqrt(2.0 * math.pi))


def norm_parts(values):
    center = values - jnp.mean(values, axis=-1, keepdims=True)
    rstd = lax.rsqrt(jnp.mean(center * center, axis=-1, keepdims=True) + norm_eps)
    return center * rstd, rstd


def norm_pull(grad, gain, xhat, rstd):
    scaled = grad * gain
    return rstd * (
        scaled
        - jnp.mean(scaled, axis=-1, keepdims=True)
        - xhat * jnp.mean(scaled * xhat, axis=-1, keepdims=True)
    )


def head_lanes(shape, head):
    lane = lax.broadcasted_iota(jnp.int32, shape, 1)
    return (lane >= HEAD_DIM) if head else (lane < HEAD_DIM), lane == (0 if head else HEAD_DIM)


def head_operands(query, key, length, head):
    inside, spare = head_lanes(query.shape, head)
    zero = jnp.zeros_like(query)
    query_in = jnp.where(inside, query * jnp.bfloat16(0.125), zero)
    query_mask = jnp.where(spare, jnp.ones_like(query), query_in)
    row = lax.broadcasted_iota(jnp.int32, query.shape, 0)
    fill = jnp.where(row < length, 0.0, mask_fill).astype(jnp.bfloat16)
    key_mask = jnp.where(inside, key, jnp.where(spare, fill, zero))
    return query_in, query_mask, key_mask, inside


def attention_kernel(info, query_ref, key_ref, value_ref, ctx_ref, total_ref):
    length = info[1 + pl.program_id(0)]
    query, key = query_ref[...], key_ref[...]
    value = jnp.transpose(value_ref[...])
    operands = [head_operands(query, key, length, head) for head in range(2)]
    scores = [matmul_nt(operand[2], operand[1]) for operand in operands]
    parts = []
    for head in range(2):
        top = jnp.max(scores[head], axis=0, keepdims=True)
        powers = jnp.exp(scores[head] - top)
        total = jnp.sum(powers, axis=0, keepdims=True)
        probs = (powers * (1.0 / total)).astype(jnp.bfloat16)
        total_ref[0, 0, head : head + 1, :] = top + jnp.log(total)
        parts.append(matmul(value[head * HEAD_DIM : (head + 1) * HEAD_DIM], probs))
    ctx_ref[...] = jnp.transpose(jnp.concatenate(parts, axis=0)).astype(jnp.bfloat16)


def attention_pull_kernel(
    info,
    query_ref,
    key_ref,
    value_ref,
    grad_ref,
    total_ref,
    own_ref,
    other_ref,
    sum_ref,
    queries_ref,
    out_buffer,
    sems,
):
    length = info[1 + pl.program_id(0)]
    query, key, value, grad = query_ref[...], key_ref[...], value_ref[...], grad_ref[...]
    operands = [head_operands(query, key, length, head) for head in range(2)]
    grads = [jnp.where(operand[3], grad, jnp.zeros_like(grad)) for operand in operands]
    flat_key = jnp.transpose(key * jnp.bfloat16(0.125))
    jobs = [(head, first) for first in range(0, SEQ, CHUNK) for head in range(2)]

    def begin(head, first):
        spot = slice(first, first + CHUNK)
        return (
            matmul_nt(operands[head][2], operands[head][1][spot]),
            matmul_nt(value, grads[head][spot]),
        )

    ready = begin(*jobs[0])
    key_grad = value_grad = jnp.zeros((SEQ, PAIR), jnp.float32)
    flat = []
    for index, (head, first) in enumerate(jobs):
        scores, prob_grad = ready
        if index + 1 < len(jobs):
            ready = begin(*jobs[index + 1])
        spot = slice(first, first + CHUNK)
        probs = jnp.exp(scores - total_ref[0, 0, head : head + 1, spot])
        row_dot = jnp.sum(probs * prob_grad, axis=0, keepdims=True)
        score_grad = (probs * (prob_grad - row_dot)).astype(jnp.bfloat16)
        value_grad += matmul(probs.astype(jnp.bfloat16), grads[head][spot])
        key_grad += matmul(score_grad, operands[head][0][spot])
        flat.append(matmul(flat_key[head * HEAD_DIM : (head + 1) * HEAD_DIM], score_grad))
        if head:
            queries_ref[spot, :] = jnp.transpose(jnp.concatenate(flat, axis=0)).astype(jnp.bfloat16)
            flat = []
    query_grad = queries_ref[...]
    value_grad = value_grad.astype(jnp.bfloat16)
    early = info[0] == 0
    pair = pl.program_id(1)
    step = pl.program_id(0) * PAIRS + pair
    last = pl.num_programs(0) * PAIRS - 1
    slot = lax.rem(step, 2)
    rows = pl.ds(pl.multiple_of(pl.program_id(0) * SEQ, SEQ), SEQ)

    def copy(which, ref, block, slot):
        cols = pl.ds(pl.multiple_of(block * PAIR, PAIR), PAIR)
        return pltpu.make_async_copy(
            out_buffer.at[slot, which], ref.at[rows, cols], sems.at[slot, which]
        )

    def wait(slot):
        for which in range(3):
            copy(which, own_ref, 0, slot).wait()

    @pl.when(step >= 2)
    def _():
        wait(slot)

    out_buffer[slot, 0] = jnp.where(early, query_grad, value_grad)
    out_buffer[slot, 1] = jnp.where(early, value_grad, query_grad)
    out_buffer[slot, 2] = key_grad.astype(jnp.bfloat16)
    copy(0, own_ref, pair, slot).start()
    copy(1, other_ref, pair, slot).start()
    key_block = PAIRS + lax.rem(pair, PAIRS // 2)
    mine = (pair < PAIRS // 2) == early

    @pl.when(mine)
    def _():
        copy(2, own_ref, key_block, slot).start()

    @pl.when(jnp.logical_not(mine))
    def _():
        copy(2, other_ref, key_block, slot).start()

    @pl.when(step == last)
    def _():
        wait(1 - slot)
        wait(slot)

    sum_ref[0, 0, 0:1, :] = jnp.sum(query_grad.astype(jnp.float32), axis=0, keepdims=True)
    sum_ref[0, 0, 1:2, :] = jnp.sum(value_grad.astype(jnp.float32), axis=0, keepdims=True)


def pick(kind):
    def spot(s, p, info):
        return s, info[INFO + kind * PAIRS + p]

    return pl.BlockSpec((SEQ, PAIR), spot)


def pair_spec():
    return pl.BlockSpec((SEQ, PAIR), lambda s, p, info: (s, p))


def pair_rows(width):
    return pl.BlockSpec((1, 1, 2, width), lambda s, p, info: (s, p, 0, 0))


def attention(info, qkv, slots):
    rows = qkv.shape[0]
    return pl.pallas_call(
        attention_kernel,
        grid_spec=pltpu.PrefetchScalarGridSpec(
            num_scalar_prefetch=1,
            grid=(slots, PAIRS),
            in_specs=[pick(kind) for kind in range(3)],
            out_specs=[pair_spec(), pair_rows(SEQ)],
        ),
        out_shape=[
            jax.ShapeDtypeStruct((rows, D), jnp.bfloat16),
            jax.ShapeDtypeStruct((slots, PAIRS, 2, SEQ), jnp.float32),
        ],
        cost_estimate=SMALL,
        name="attention",
    )(info, qkv, qkv, qkv)


def attention_pull(info, qkv, grad, log_total, slots):
    rows = qkv.shape[0]

    table = jax.ShapeDtypeStruct((rows, BLOCKS // 2 * PAIR), jnp.bfloat16)
    return pl.pallas_call(
        attention_pull_kernel,
        grid_spec=pltpu.PrefetchScalarGridSpec(
            num_scalar_prefetch=1,
            grid=(slots, PAIRS),
            in_specs=[pick(kind) for kind in range(3)] + [pair_spec(), pair_rows(SEQ)],
            out_specs=[pl.BlockSpec(memory_space=pl.ANY)] * 2 + [pair_rows(PAIR)],
            scratch_shapes=[
                pltpu.VMEM((SEQ, PAIR), jnp.bfloat16),
                pltpu.VMEM((2, 3, SEQ, PAIR), jnp.bfloat16),
                pltpu.SemaphoreType.DMA((2, 3)),
            ],
        ),
        out_shape=[table] * 2 + [jax.ShapeDtypeStruct((slots, PAIRS, 2, PAIR), jnp.float32)],
        cost_estimate=SMALL,
        name="attention_pull",
    )(info, qkv, qkv, qkv, grad, log_total)


def join_halves(core, own, other):
    return jnp.where(
        core == 0,
        jnp.concatenate([own, other], axis=1),
        jnp.concatenate([other, own], axis=1),
    )


def vector_kernel(info, own_ref, other_ref, vec_ref, bias_ref, own_bias_ref, other_bias_ref):
    early_core = info[0] == 0
    rows = VROWS // 2
    own = jnp.transpose(own_ref[...].astype(jnp.float32))[:rows]
    other = jnp.transpose(other_ref[...].astype(jnp.float32))[:rows]
    vec = jnp.concatenate(
        [jnp.where(early_core, own, other), jnp.where(early_core, other, own)], axis=0
    )
    vec_ref[0:VROWS, :] = vec
    up_rows = FF // D
    for place in range(up_rows):
        early, late = 5 + place, 5 + (place + up_rows // 2) % up_rows
        row = jnp.where(early_core, vec[early : early + 1], vec[late : late + 1])
        bias_ref[0:1, place * D : (place + 1) * D] = row
    own_bias_ref[...] = jnp.zeros_like(own_bias_ref)
    other_bias_ref[...] = jnp.zeros_like(other_bias_ref)
    own_bias_ref[0:1, :D] = jnp.where(early_core, vec[0:1], vec[1:2])
    other_bias_ref[0:1, :D] = jnp.where(early_core, vec[1:2], vec[0:1])


def vector_tables(info, own, other):
    half = own.shape[1] - VEC_PAD
    spec = pl.BlockSpec((D, VEC_PAD), lambda i: (0, half // VEC_PAD))
    shapes = [(16, D), (8, FF), (8, half), (8, half)]
    return pl.pallas_call(
        vector_kernel,
        grid=(1,),
        in_specs=[pl.BlockSpec(memory_space=pltpu.SMEM), spec, spec],
        out_specs=[pl.BlockSpec(shape, lambda i: (0, 0)) for shape in shapes],
        out_shape=[jax.ShapeDtypeStruct(shape, jnp.float32) for shape in shapes],
        name="vector_tables",
    )(info, own, other)


def vector_grad_kernel(info, low_ref, high_ref, bias_ref, head_ref, out_ref):
    early_core = info[0] == 0
    out_ref[...] = jnp.zeros_like(out_ref)
    for pair in range(PAIRS):
        cols = slice(pair * PAIR, (pair + 1) * PAIR)
        out_ref[0:2, cols] = jnp.sum(head_ref[:, pair], axis=0)
    out_ref[2:5, :] = low_ref[0:3, :]
    up_rows = FF // D
    for place in range(up_rows):
        late = (place + up_rows // 2) % up_rows
        out_ref[5 + place : 6 + place, :] = jnp.where(
            early_core,
            bias_ref[0:1, place * D : (place + 1) * D],
            bias_ref[0:1, late * D : (late + 1) * D],
        )
    out_ref[5 + up_rows : 8 + up_rows, :] = high_ref[0:3, :]


def vector_grads(info, low_sums, high_sums, bias_sums, head_sums):
    whole = pl.BlockSpec(memory_space=pltpu.VMEM)
    return pl.pallas_call(
        vector_grad_kernel,
        in_specs=[pl.BlockSpec(memory_space=pltpu.SMEM)] + [whole] * 4,
        out_specs=whole,
        out_shape=jax.ShapeDtypeStruct((16, D), jnp.float32),
        name="vector_grads",
    )(info, low_sums, high_sums, bias_sums, head_sums)


def hidden_pieces(own, other):
    return [
        (ref, slice(first, first + D), place + first)
        for place, ref in ((0, own), (WIDE, other))
        for first in range(0, WIDE, D)
    ]


OUT_COLS = slice(WIDE, WIDE + D // 2)


def raise_kernel(
    info,
    vec_ref,
    bias_ref,
    x_ref,
    ctx_ref,
    own,
    other,
    xhat_ref,
    rstd_ref,
    low_ref,
    own_act_ref,
    other_act_ref,
    slope_ref,
):
    ctx = ctx_ref[...]
    attended = join_halves(info[0], matmul(ctx, own[:, OUT_COLS]), matmul(ctx, other[:, OUT_COLS]))
    xhat, rstd = norm_parts(x_ref[...].astype(jnp.float32) + (attended + vec_ref[2:3, :]))
    xhat_ref[...] = xhat
    rstd_ref[...] = jnp.broadcast_to(rstd, rstd_ref.shape)
    hidden = (xhat * vec_ref[3:4, :] + vec_ref[4:5, :]).astype(jnp.bfloat16)
    low_ref[...] = hidden
    for ref, cols, place in hidden_pieces(own, other):
        spot = slice(place, place + D)
        act, slope = gelu_parts(matmul(hidden, ref[:, cols]) + bias_ref[0:1, spot])
        act_ref = own_act_ref if place < WIDE else other_act_ref
        act_ref[:, cols] = act.astype(jnp.bfloat16)
        slope_ref[:, spot] = slope.astype(jnp.bfloat16)


def add_sums(ref, sums):
    first = pl.program_id(0) == 0
    for place, values in enumerate(sums):
        total = jnp.sum(values, axis=0, keepdims=True)
        spot = slice(place, place + 1)
        ref[spot, :] = jnp.where(first, total, ref[spot, :] + total)


def lower_kernel(
    info, vec_ref, xhat_ref, first_ref, second_ref, cot_ref, out_ref, grad_ref, low_ref, sum_ref
):
    first = pl.program_id(0) * ROWS
    hidden = xhat_ref[...] * vec_ref[3:4, :] + vec_ref[4:5, :]
    xhat, rstd = norm_parts(hidden + (first_ref[...] + second_ref[...] + vec_ref[9:10, :]))
    gain = vec_ref[10:11, :]
    out_ref[...] = (xhat * gain + vec_ref[11:12, :]).astype(jnp.bfloat16)
    limit = info[INFO + BLOCKS + lax.div(first, SEQ)]
    row = lax.broadcasted_iota(jnp.int32, (ROWS, 1), 0) + lax.rem(first, SEQ)
    cot = jnp.where(row < limit, cot_ref[...].astype(jnp.float32), 0.0)
    grad = norm_pull(cot, gain, xhat, rstd)
    grad_ref[...] = grad
    low = grad.astype(jnp.bfloat16)
    low_ref[...] = low
    add_sums(sum_ref, (low.astype(jnp.float32), cot * xhat, cot))


def pull_kernel(
    info,
    vec_ref,
    xhat_ref,
    rstd_ref,
    slope_ref,
    grad_ref,
    low_ref,
    up_own,
    up_other,
    own,
    other,
    own_pre_ref,
    other_pre_ref,
    skip_ref,
    attn_ref,
    ctx_ref,
    sum_ref,
    bias_ref,
):
    core = info[0]
    low = low_ref[...]
    hidden_grad = grad_ref[...]
    for down, up in zip(hidden_pieces(own, other), hidden_pieces(up_own, up_other)):
        ref, cols, place = down
        spot = slice(place, place + D)
        pre = matmul(low, ref[:, cols]) * slope_ref[:, spot].astype(jnp.float32)
        pre = pre.astype(jnp.bfloat16)
        pre_ref = own_pre_ref if place < WIDE else other_pre_ref
        pre_ref[:, cols] = pre
        hidden_grad = hidden_grad + matmul_nt(pre, up[0][:, up[1]])
    xhat = xhat_ref[...]
    skip = norm_pull(hidden_grad, vec_ref[3:4, :], xhat, rstd_ref[:, 0:1])
    skip_ref[...] = skip
    attn = skip.astype(jnp.bfloat16)
    attn_ref[...] = attn
    left, right = attn[:, : D // 2], attn[:, D // 2 :]
    ctx = matmul_nt(jnp.where(core == 0, left, right), up_own[:, OUT_COLS])
    ctx = ctx + matmul_nt(jnp.where(core == 0, right, left), up_other[:, OUT_COLS])
    ctx_ref[...] = ctx.astype(jnp.bfloat16)
    add_sums(sum_ref, (attn.astype(jnp.float32), hidden_grad * xhat, hidden_grad))
    add_sums(bias_ref.at[:, :WIDE], (own_pre_ref[...].astype(jnp.float32),))
    add_sums(bias_ref.at[:, WIDE:], (other_pre_ref[...].astype(jnp.float32),))


def row_spec(width):
    return pl.BlockSpec((ROWS, width), lambda i: (i, 0))


def whole_spec():
    return pl.BlockSpec(memory_space=pltpu.VMEM)


def row_call(kernel, name, in_specs, rows, outs, sums, flops, operands):
    shapes = [jax.ShapeDtypeStruct((rows, width), kind) for width, kind in outs]
    shapes += [jax.ShapeDtypeStruct((8, width), jnp.float32) for width in sums]
    return pl.pallas_call(
        kernel,
        grid=(rows // ROWS,),
        in_specs=[pl.BlockSpec(memory_space=pltpu.SMEM)] + in_specs,
        out_specs=[row_spec(width) for width, kind in outs]
        + [pl.BlockSpec((8, width), lambda i: (0, 0)) for width in sums],
        out_shape=shapes,
        compiler_params=pltpu.CompilerParams(vmem_limit_bytes=52 << 20),
        cost_estimate=SMALL,
        name=name,
    )(*operands)


def raise_rows(info, vec, bias, tokens, context, own, other):
    low, full = jnp.bfloat16, jnp.float32
    return row_call(
        raise_kernel,
        "raise_rows",
        [whole_spec()] * 2 + [row_spec(D)] * 2 + [whole_spec()] * 2,
        tokens.shape[0],
        [(D, full), (PAIR, full), (D, low), (WIDE, low), (WIDE, low), (FF, low)],
        [],
        14 << 30,
        (info, vec, bias, tokens, context, own, other),
    )


def lower_rows(info, vec, xhat, first, second, cotangent):
    low, full = jnp.bfloat16, jnp.float32
    return row_call(
        lower_kernel,
        "lower_rows",
        [whole_spec()] + [row_spec(D)] * 4,
        first.shape[0],
        [(D, low), (D, full), (D, low)],
        [D],
        4 << 30,
        (info, vec, xhat, first, second, cotangent),
    )


def pull_rows(info, vec, xhat, rstd, slope, grad, low_grad, up, down):
    low, full = jnp.bfloat16, jnp.float32
    return row_call(
        pull_kernel,
        "pull_rows",
        [whole_spec(), row_spec(D), row_spec(PAIR), row_spec(FF), row_spec(D), row_spec(D)]
        + [whole_spec()] * 4,
        xhat.shape[0],
        [(WIDE, low), (WIDE, low), (D, full), (D, low), (D, low)],
        [D, FF],
        18 << 30,
        (info, vec, xhat, rstd, slope, grad, low_grad, *up, *down),
    )


def split_rest(values):
    high = values.astype(jnp.bfloat16)
    return high, (values - high.astype(jnp.float32)).astype(jnp.bfloat16)

def store_split(values, where, high_ref, rest_ref):
    high_ref[where], rest_ref[where] = split_rest(values)

def close_product(left, right, rows, cols):
    left_high, left_rest = left[0][rows, :], left[1][rows, :]
    right_high, right_rest = right[0][:, cols], right[1][:, cols]
    return matmul(
        jnp.concatenate([left_high, left_high, left_rest], axis=1),
        jnp.concatenate([right_high, right_rest, right_high], axis=0),
    )


def mirrored_product(left, right, finish):
    for first in range(0, D, TILE):
        rows = slice(first, first + TILE)
        wide = close_product(left, right, rows, slice(first, D))
        for last in range(first, D, TILE):
            tile = wide[:, last - first : last - first + TILE]
            cols = slice(last, last + TILE)
            finish(tile, rows, cols)
            if first < last:
                finish(jnp.transpose(tile), cols, rows)


def polar_kernel(
    start_ref,
    own_ref,
    other_ref,
    cols_ref,
    polar_ref,
    out_ref,
    gram,
    a_high,
    a_rest,
    q_high,
    q_rest,
    b_high,
    b_rest,
    r_high,
    r_rest,
):
    a, q, b, r = (a_high, a_rest), (q_high, q_rest), (b_high, b_rest), (r_high, r_rest)
    count = out_ref.shape[0]
    start = pl.multiple_of(start_ref[0], 8)
    whole = own_ref[...] + other_ref[...]
    row = lax.broadcasted_iota(jnp.int32, (D, D), 0)
    col = lax.broadcasted_iota(jnp.int32, (D, D), 1)
    scale = jnp.sqrt(jnp.sum(jnp.where(row == col, whole, 0.0), keepdims=True)) + 1e-07
    gram[...] = whole / (scale * scale)
    rows = lax.broadcasted_iota(jnp.int32, (count, D), 0) + start
    cols = lax.broadcasted_iota(jnp.int32, (count, D), 1)
    out_ref[...] = jnp.where(rows == cols, 1.0, 0.0)

    def sweep(index, carry):
        every = slice(0, D)
        store_split(gram[...], (every, every), a_high, a_rest)

        def step_tile(tile, where_rows, where_cols):
            step = poly_second * gram[where_rows, where_cols] + poly_third * tile
            if where_rows == where_cols:
                tile_row = lax.broadcasted_iota(jnp.int32, (TILE, TILE), 0)
                tile_col = lax.broadcasted_iota(jnp.int32, (TILE, TILE), 1)
                step = step + jnp.where(tile_row == tile_col, poly_first, 0.0)
            store_split(step, (where_rows, where_cols), q_high, q_rest)

        mirrored_product(a, a, step_tile)
        store_split(out_ref[...], (slice(0, count), every), r_high, r_rest)
        out_ref[...] = close_product(r, q, slice(0, count), every)

        @pl.when(index < NS_ITERS - 1)
        def _():
            def half_tile(tile, where_rows, where_cols):
                store_split(tile, (where_rows, where_cols), b_high, b_rest)

            def gram_tile(tile, where_rows, where_cols):
                gram[where_rows, where_cols] = tile

            mirrored_product(q, a, half_tile)
            mirrored_product(b, q, gram_tile)

        return carry

    lax.fori_loop(0, NS_ITERS, sweep, 0)
    both = jnp.concatenate(split_rest(out_ref[...] / scale), axis=0)
    for place in range(0, cols_ref.shape[1], D):
        spot = slice(place, place + D)
        product = matmul(both, cols_ref[:, spot])
        polar_ref[:, spot] = (product[:count] + product[count:]).astype(jnp.bfloat16)

def polar_rows(start, own, other, columns, count):
    half = pltpu.VMEM((D, D), jnp.bfloat16)
    short = pltpu.VMEM((count, D), jnp.bfloat16)
    return pl.pallas_call(
        polar_kernel,
        in_specs=[pl.BlockSpec(memory_space=pltpu.SMEM)]
        + [pl.BlockSpec(memory_space=pltpu.VMEM)] * 3,
        out_specs=pl.BlockSpec(memory_space=pltpu.VMEM),
        out_shape=jax.ShapeDtypeStruct((count, columns.shape[1]), jnp.bfloat16),
        scratch_shapes=[pltpu.VMEM((count, D), jnp.float32), pltpu.VMEM((D, D), jnp.float32)]
        + [half] * 6
        + [short] * 2,
        compiler_params=pltpu.CompilerParams(vmem_limit_bytes=40 << 20),
        name="polar_rows",
    )(start, own, other, columns)


def per_device(
    size,
    tokens,
    cotangent,
    counts,
    lengths,
    w_qkv,
    w_out,
    w_up,
    w_down,
    vectors,
    mom_qkv,
    mom_out,
    mom_up,
    mom_down,
    adam_first,
    adam_second,
):
    me = lax.axis_index("fsdp")
    core = lax.axis_index("row")
    slots = lengths.shape[0]
    rows = tokens.shape[0]
    up_rows = FF // D
    low = jnp.bfloat16

    block_rows = D // size
    qkv_half, up_half = w_qkv.shape[1], w_up.shape[1]
    vec_rows = vectors.shape[0]
    narrow = qkv_half - D

    def pick_core(early, late):
        return jnp.where(core == 0, early, late)

    def turn(values, cut):
        return pick_core(values, jnp.concatenate([values[:, cut:], values[:, :cut]], axis=1))

    vec_block = jnp.pad(vectors.T, ((0, 0), (0, VEC_PAD - vec_rows))).astype(low)
    first_block = jnp.concatenate([turn(w_qkv.astype(low), narrow), vec_block], axis=1)
    second_block = jnp.concatenate([w_up.astype(low), w_out.astype(low)], axis=1)
    third_block = w_down.astype(low)
    near, far = size.bit_length() - 3, size.bit_length() - 2
    steps = [1 << near, 1 << far, 3 << near]
    first_pieces = send_high(first_block, size)
    second_pieces = [second_block, flip(second_block, steps[0], size)]
    first_pieces, second_pieces, third_block = together(first_pieces, second_pieces, third_block)
    first_pieces = send_low(sort_high(first_pieces, size), size)
    second_pieces += [flip(second_pieces[0], step, size) for step in steps[1:]]
    first_pieces, second_pieces, third_block = together(first_pieces, second_pieces, third_block)
    first_own = sort_low(first_pieces)
    first_other = swap_cores(first_own)
    second_pieces = send_low(sort_high(second_pieces, size), size)
    third_pieces = [third_block, flip(third_block, steps[0], size)]

    spots = pick_core(jnp.array(SPOTS[0], jnp.int32), jnp.array(SPOTS[1], jnp.int32))
    live = jnp.arange(slots) % CAP < counts.reshape(-1)[jnp.arange(slots) // CAP]
    info = jnp.concatenate(
        [core.reshape(1).astype(jnp.int32), lengths, spots, jnp.where(live, lengths, 0)]
    )
    vec, bias_up, bias_own, bias_other = vector_tables(info, first_own, first_other)
    qkv_own, qkv_other = first_own[:, :qkv_half], first_other[:, :qkv_half]
    projected = jnp.concatenate(
        [
            (matmul(tokens, qkv_own) + bias_own[:1]).astype(low),
            (matmul(tokens, qkv_other) + bias_other[:1]).astype(low),
        ],
        axis=1,
    )
    projected, third_pieces = together(projected, third_pieces)
    third_pieces += [flip(third_pieces[0], step, size) for step in steps[1:]]
    context, log_total = attention(info, projected, slots)
    context, second_pieces, third_pieces = together(context, second_pieces, third_pieces)
    second_own = sort_low(second_pieces)
    third_pieces = send_low(sort_high(third_pieces, size), size)
    second_other = swap_cores(second_own)
    xhat_one, rstd_one, hidden_low, act_own, act_other, slope = raise_rows(
        info, vec, bias_up, tokens, context, second_own, second_other
    )
    act_own, act_other, *third_pieces = together(act_own, act_other, *third_pieces)
    third_own = sort_low(third_pieces)
    third_other = swap_cores(third_own)
    branch = matmul_nt(act_own, third_own)
    branch, third_other = together(branch, third_other)
    layer_out, top_grad, branch_low, high_sums = lower_rows(
        info, vec, xhat_one, branch, matmul_nt(act_other, third_other), cotangent
    )

    full = jnp.float32
    leaving = matmul_tn(branch_low, act_other).astype(low)
    leaving, branch_low = together(leaving, branch_low)
    down_arrived = swap_cores(leaving)
    down_own = matmul_tn(branch_low, act_own)
    down_own, down_arrived, branch_low = together(down_own, down_arrived, branch_low)
    down_kept, leaving = split_low([down_own + down_arrived.astype(full)], size)
    leaving, branch_low = together(leaving, branch_low)
    down_sent = fly_low(leaving, size)
    pulled = pull_rows(
        info,
        vec,
        xhat_one,
        rstd_one,
        slope,
        top_grad,
        branch_low,
        (second_own, second_other),
        (third_own, third_other),
    )
    pulled, down_sent = together(pulled, down_sent)
    pre_own, pre_other, skip_grad, attn_low, context_grad, low_sums, bias_sums = pulled
    down_kept, leaving = split_near(down_kept, down_sent, size)
    leaving, pre_own, pre_other, attn_low = together(leaving, pre_own, pre_other, attn_low)
    down_sent = fly_near(leaving, size)
    up_leaving = matmul_tn(hidden_low, pre_other).astype(low)
    up_leaving, pre_own, attn_low, down_sent = together(up_leaving, pre_own, attn_low, down_sent)
    up_arrived = swap_cores(up_leaving)
    down_kept, down_leaving = split_far(down_kept, down_sent, size)
    out_own = pick_core(attn_low[:, : D // 2], attn_low[:, D // 2 :])
    out_other = pick_core(attn_low[:, D // 2 :], attn_low[:, : D // 2])
    out_arrived = swap_cores(matmul_tn(context, out_other).astype(low))
    up_own = matmul_tn(hidden_low, pre_own)
    out_own = matmul_tn(context, out_own)
    up_own, out_own, up_arrived, out_arrived = together(up_own, out_own, up_arrived, out_arrived)
    wide_kept, leaving = split_low(
        [up_own + up_arrived.astype(full), out_own + out_arrived.astype(full)], size
    )
    leaving, down_leaving, context_grad = together(leaving, down_leaving, context_grad)
    wide_sent = fly_low(leaving, size)
    down_sent = fly_far(down_leaving, size)
    parts = attention_pull(info, projected, context_grad, log_total, slots)
    parts, down_sent = together(parts, down_sent)

    leaving = matmul_tn(tokens, parts[1]).astype(low)
    qkv_leaving, parts, wide_sent, down_sent = together(leaving, parts, wide_sent, down_sent)
    wide_kept, leaving = split_near(wide_kept, wide_sent, size)
    leaving, parts = together(leaving, parts)
    wide_sent = fly_near(leaving, size)
    qkv_arrived = swap_cores(qkv_leaving)
    qkv_part = matmul_tn(tokens, parts[0])
    (grad_down,) = add_four(down_kept, [down_sent])
    moment_down = moment_decay * mom_down + grad_down
    qkv_part, qkv_arrived, grads, moment_down = together(qkv_part, qkv_arrived, parts, moment_down)
    qkv_kept, leaving = split_low([qkv_part + qkv_arrived.astype(full)], size)
    leaving, grads, down_block = together(leaving, grads, moment_down.astype(low))
    qkv_sent = fly_low(leaving, size)
    down_sent = fly_far(down_block, size)
    wide_sent, down_sent = together(wide_sent, down_sent)
    wide_kept, wide_leaving = split_far(wide_kept, wide_sent, size)
    wide_sent = fly_far(wide_leaving, size)
    qkv_sent, wide_sent, down_sent = together(qkv_sent, wide_sent, down_sent)
    qkv_kept, leaving = split_high(qkv_kept, qkv_sent, size)
    leaving, wide_sent, down_sent = together(leaving, wide_sent, down_sent)
    qkv_sent = fly_high(leaving, size)
    grad_up, grad_out = add_four(wide_kept, [wide_sent])
    moment_up = moment_decay * mom_up + grad_up
    moment_out = moment_decay * mom_out + grad_out
    wide_block = jnp.concatenate([moment_up.astype(low), moment_out.astype(low)], axis=1)
    wide_sent = fly_far(wide_block, size)
    down_pair = place_far(down_block, down_sent, size)
    down_sent = fly_near(down_pair, size)
    mom_turned = turn(mom_qkv, narrow)
    vector_grad = vector_grads(info, low_sums, high_sums, bias_sums, grads[2])
    qkv_sent, wide_sent, down_sent, grads, vector_grad, mom_turned = together(
        qkv_sent, wide_sent, down_sent, grads, vector_grad, mom_turned
    )
    (grad_turned,) = add_four(qkv_kept, qkv_sent)
    qkv_block = (moment_decay * mom_turned + grad_turned).astype(low)
    wide_pair = place_far(wide_block, wide_sent, size)
    qkv_block, grad_turned, wide_pair = together(qkv_block, grad_turned, wide_pair)
    qkv_pieces = send_high(qkv_block, size)
    wide_sent = fly_near(wide_pair, size)
    vector_grad = vector_grad + swap_cores(vector_grad)
    vector_arrived = flip(vector_grad, 1, size)
    down_rows = place_near(down_pair, down_sent, size)
    grad_qkv = turn(grad_turned, D)
    moment_qkv = moment_decay * mom_qkv + grad_qkv
    grad_qkv, moment_qkv, qkv_pieces, wide_sent, down_rows = together(
        grad_qkv, moment_qkv, qkv_pieces, wide_sent, down_rows
    )
    wide_rows = place_near(wide_pair, wide_sent, size)

    qkv_rows = merge_rows(sort_high(qkv_pieces, size))
    place = me % GROUP

    def widen(values):
        return jnp.pad(values, ((0, 0), (0, WIDE - values.shape[1])))

    matrices = (
        widen(qkv_rows),
        widen(wide_rows[:, up_half:]),
        wide_rows[:, :up_half],
        down_rows,
    )

    def matrix_at(which):
        lower = jnp.where(which == 0, matrices[0], matrices[1])
        upper = jnp.where(which == 2, matrices[2], matrices[3])
        return jnp.where(which < 2, lower, upper)

    pieces = []
    for step in range(GROUP):
        pieces.append(matrix_at(place ^ step).reshape(-1, block_rows, WIDE))
    pieces, grads, vector_grad, vector_arrived = together(
        pieces, grads, vector_grad, vector_arrived
    )
    pieces = pieces[:1] + [flip(pieces[step], step, size) for step in range(1, GROUP)]
    vector_grad = vector_grad + vector_arrived
    vector_arrived = flip(vector_grad, 2, size)
    input_grad = (
        skip_grad + matmul_nt(grads[0], qkv_own) + matmul_nt(grads[1], qkv_other)
    )
    pieces, input_grad, vector_grad, vector_arrived = together(
        pieces, input_grad, vector_grad, vector_arrived
    )
    columns = sort_low(pieces)
    for bit in range(2, size.bit_length() - 3, 2):
        columns = sort_low(send_four(columns.reshape(4, -1, WIDE), bit, size))
    gram = matmul_nt(columns, columns)
    start = ((me - place) * block_rows).reshape(1).astype(jnp.int32)
    vector_grad = vector_grad + vector_arrived
    gram, vector_grad = together(gram, vector_grad)
    gram_arrived = swap_cores(gram)
    vector_arrived = flip(vector_grad, 4, size)
    gram_arrived, vector_arrived = together(gram_arrived, vector_arrived)
    vector_grad = vector_grad + vector_arrived
    polar = polar_rows(start, gram, gram_arrived, columns, GROUP * block_rows)
    polar, vector_grad = together(polar, vector_grad)
    for bit in range(3, size.bit_length() - 1):
        vector_grad = vector_grad + flip(vector_grad, 1 << bit, size)
    grad_vectors = lax.dynamic_slice(
        vector_grad, (core * vec_rows, me * block_rows), (vec_rows, block_rows)
    )
    polar = polar.reshape(GROUP, block_rows, WIDE)
    arrived = []
    for step in range(GROUP):
        block = lax.dynamic_index_in_dim(polar, place ^ step, 0, keepdims=False)
        arrived.append(flip(block, step, size) if step else block)
    arrived = sort_four(arrived, 0, 0)
    masters = (w_qkv, w_out, w_up, w_down)
    counts_of = (3 * D, D, FF, FF)
    updated = []
    for index in range(GROUP):
        ortho = arrived[index][:, : masters[index].shape[1]].astype(jnp.float32)
        if index == 0:
            ortho = turn(ortho, D)
        updated.append(
            masters[index] * (1.0 - muon_rate * decay_rate)
            - muon_rate * 0.2 * math.sqrt(counts_of[index]) * ortho
        )

    first_moment = beta_first * adam_first + (1.0 - beta_first) * grad_vectors
    second_moment = beta_second * adam_second + (1.0 - beta_second) * grad_vectors * grad_vectors
    direction = (
        first_moment
        / (1.0 - beta_first**STEP)
        / (jnp.sqrt(second_moment / (1.0 - beta_second**STEP)) + adam_eps)
    )
    new_vectors = vectors - adam_rate * (direction + decay_rate * vectors)
    return (
        layer_out,
        input_grad,
        grad_qkv,
        grad_out,
        grad_up,
        grad_down,
        grad_vectors,
        moment_qkv,
        moment_out,
        moment_up,
        moment_down,
        updated[0],
        updated[1],
        updated[2],
        updated[3],
        first_moment,
        second_moment,
        new_vectors,
    )


def solution(mesh):
    size = mesh.shape["fsdp"]

    def run(*arrays):
        return per_device(size, *arrays)

    weight = P("fsdp", "row")
    vector = P("row", "fsdp")
    sample = P(("fsdp", "row"), None)
    return jax.shard_map(
        run,
        mesh=mesh,
        in_specs=(sample, sample, sample, P(("fsdp", "row")))
        + (weight,) * 4
        + (vector,)
        + (weight,) * 4
        + (vector,) * 2,
        out_specs=(sample, sample)
        + (weight,) * 4
        + (vector,)
        + (weight,) * 8
        + (vector,) * 3,
        check_vma=False,
    )
```

```python
import math

import jax
import jax.numpy as jnp
from jax import lax
from jax.experimental import pallas as pl
from jax.experimental.layout import Layout, with_layout_constraint
from jax.experimental.pallas import tpu as pltpu
from jax.sharding import PartitionSpec as P

D = 768
FF = 3072
HEADS = 12
HEAD_DIM = 64
SEQ = 512
CAP = 1
MICRO = 2
NS_ITERS = 5
STEP = 10

norm_eps = 1e-05
mask_fill = -1e30
poly_first = 3.4445
poly_second = -4.775
poly_third = 2.0315
muon_rate = 0.2
adam_rate = 0.8
decay_rate = 0.01
moment_decay = 0.5
beta_first = 0.9
beta_second = 0.98
adam_eps = 1e-06

SWAP = [(0, 1), (1, 0)]
VEC_PAD = 128
GROUP = 4
TILE = 256
PARTS = 2
STRIDE = HEADS // 2 // PARTS
CHUNK = 256
ROWS = 256
VROWS = 8 + FF // D
SMALL = pl.CostEstimate(flops=1 << 20, bytes_accessed=1 << 16, transcendentals=0)
PAIR = 2 * HEAD_DIM
PAIRS = HEADS // 2
BLOCKS = 3 * PAIRS
INFO = 1 + CAP * MICRO
WIDE = FF // 2


def matmul(former, latter):
    return jnp.dot(former, latter, preferred_element_type=jnp.float32)


def matmul_tn(former, latter):
    return lax.dot_general(
        former, latter, (((0,), (0,)), ((), ())), preferred_element_type=jnp.float32
    )


def matmul_nt(former, latter):
    return lax.dot_general(
        former, latter, (((1,), (1,)), ((), ())), preferred_element_type=jnp.float32
    )


def by_rows(values):
    return with_layout_constraint(values, Layout(major_to_minor=tuple(range(values.ndim))))


def flip(values, mask, size):
    return by_rows(lax.ppermute(by_rows(values), "fsdp", [(i, i ^ mask) for i in range(size)]))


def swap_cores(values):
    return by_rows(lax.ppermute(by_rows(values), "row", SWAP))


def together(*values):
    return lax.optimization_barrier(values)


def my_bit(bit):
    return (lax.axis_index("fsdp") >> bit) & 1


def pair_of(bit):
    return (lax.axis_index("fsdp") >> bit) & 3


def send_four(values, bit, size):
    return [values] + [flip(values, step << bit, size) for step in (1, 2, 3)]


def sort_four(pieces, bit, axis):
    low, high = my_bit(bit) == 1, my_bit(bit + 1) == 1
    first = jnp.where(low, jnp.stack(pieces[1::-1], axis), jnp.stack(pieces[:2], axis))
    second = jnp.where(low, jnp.stack(pieces[:1:-1], axis), jnp.stack(pieces[2:], axis))
    return jnp.where(
        high,
        jnp.concatenate([second, first], axis),
        jnp.concatenate([first, second], axis),
    )


def merge_rows(values):
    return values.reshape(-1, values.shape[-1])


def send_high(block, size):
    return send_four(block, size.bit_length() - 3, size)


def sort_high(pieces, size):
    return sort_four(pieces, size.bit_length() - 3, 0)


def send_low(values, size):
    for bit in range(size.bit_length() - 5, 0, -2):
        values = sort_four(send_four(values, bit, size), bit, -3)
    return send_four(values, 0, size)


def sort_low(pieces):
    return merge_rows(sort_four(pieces, 0, -3))


def pick_four(parts, axis, place):
    picked = []
    for part in parts:
        terms = part if isinstance(part, tuple) else (part,)
        blocks = [lax.dynamic_index_in_dim(term, place, axis, keepdims=False) for term in terms]
        picked.append(sum(block.astype(jnp.float32) for block in blocks))
    return picked


def split_four(parts, axis, bit):
    mine = pair_of(bit)
    leaving = []
    for step in (1, 2, 3):
        pieces = pick_four(parts, axis, mine ^ step)
        leaving.append(jnp.concatenate([part.astype(jnp.bfloat16) for part in pieces], axis=-1))
    return pick_four(parts, axis, mine), leaving


def fly_four(leaving, bit, size):
    return [flip(piece, step << bit, size) for step, piece in zip((1, 2, 3), leaving)]


def split_two(parts, axis, bit):
    mine = my_bit(bit)
    pieces = pick_four(parts, axis, 1 - mine)
    leaving = jnp.concatenate([part.astype(jnp.bfloat16) for part in pieces], axis=-1)
    return pick_four(parts, axis, mine), leaving


def place_two(values, arrived, bit, axis):
    return jnp.where(
        my_bit(bit) == 1,
        jnp.stack([arrived, values], axis),
        jnp.stack([values, arrived], axis),
    )


def add_four(kept, arrived):
    totals, place = [], 0
    for part in kept:
        cols = slice(place, place + part.shape[-1])
        place = cols.stop
        for piece in arrived:
            part = part + piece[..., cols].astype(jnp.float32)
        totals.append(part)
    return totals


def split_low(parts, size):
    shape = (4,) * ((size.bit_length() - 1) // 2) + (D // size, -1)
    parts = [tuple(term.reshape(shape) for term in part) for part in parts]
    return split_four(parts, len(shape) - 3, 0)


def fly_low(leaving, size):
    return fly_four(leaving, 0, size)


def add_low(kept, arrived, size):
    parts = add_four(kept, arrived)
    for bit in range(2, size.bit_length() - 3, 2):
        kept, leaving = split_four(parts, parts[0].ndim - 3, bit)
        parts = add_four(kept, fly_four(leaving, bit, size))
    return parts


def split_high(kept, arrived, size):
    return split_four(add_low(kept, arrived, size), 0, size.bit_length() - 3)


def split_near(kept, arrived, size):
    parts = [part.reshape((2, 2) + part.shape[1:]) for part in add_low(kept, arrived, size)]
    return split_two(parts, 1, size.bit_length() - 3)


def split_far(kept, arrived, size):
    return split_two(add_four(kept, [arrived]), 0, size.bit_length() - 2)


def fly_near(values, size):
    return flip(values, 1 << size.bit_length() - 3, size)


def fly_far(values, size):
    return flip(values, 1 << size.bit_length() - 2, size)


def place_far(values, arrived, size):
    return place_two(values, arrived, size.bit_length() - 2, 0)


def place_near(values, arrived, size):
    return merge_rows(place_two(values, arrived, size.bit_length() - 3, 1))


def fly_high(leaving, size):
    return fly_four(leaving, size.bit_length() - 3, size)


erf_slope = 0.3275911
erf_terms = (1.061405429, -1.453152027, 1.421413741, -0.284496736, 0.254829592)


def gelu_parts(pre_act):
    bell = jnp.exp(pre_act * pre_act * -0.5)
    inverse = 1.0 / (1.0 + jnp.abs(pre_act) * (erf_slope * math.sqrt(0.5)))
    poly = 0.5 * erf_terms[0] * inverse + 0.5 * erf_terms[1]
    for term in erf_terms[2:]:
        poly = poly * inverse + 0.5 * term
    tail = poly * inverse * bell
    cdf = jnp.where(pre_act < 0.0, tail, 1.0 - tail)
    return pre_act * cdf, cdf + pre_act * bell * (1.0 / math.sqrt(2.0 * math.pi))


def norm_parts(values):
    center = values - jnp.mean(values, axis=-1, keepdims=True)
    rstd = lax.rsqrt(jnp.mean(center * center, axis=-1, keepdims=True) + norm_eps)
    return center * rstd, rstd


def norm_pull(grad, gain, xhat, rstd):
    scaled = grad * gain
    return rstd * (
        scaled
        - jnp.mean(scaled, axis=-1, keepdims=True)
        - xhat * jnp.mean(scaled * xhat, axis=-1, keepdims=True)
    )


def head_lanes(shape, head):
    lane = lax.broadcasted_iota(jnp.int32, shape, 1)
    return (lane >= HEAD_DIM) if head else (lane < HEAD_DIM), lane == (0 if head else HEAD_DIM)


def head_operands(query, key, length, head):
    inside, spare = head_lanes(query.shape, head)
    zero = jnp.zeros_like(query)
    query_in = jnp.where(inside, query * jnp.bfloat16(0.125), zero)
    query_mask = jnp.where(spare, jnp.ones_like(query), query_in)
    row = lax.broadcasted_iota(jnp.int32, query.shape, 0)
    fill = jnp.where(row < length, 0.0, mask_fill).astype(jnp.bfloat16)
    key_mask = jnp.where(inside, key, jnp.where(spare, fill, zero))
    return query_in, query_mask, key_mask, inside


def attention_kernel(info, query_ref, key_ref, value_ref, ctx_ref, total_ref):
    length = info[1 + pl.program_id(0)]
    for pair in range(STRIDE):
        cols = slice(pair * PAIR, (pair + 1) * PAIR)
        query, key = query_ref[:, cols], key_ref[:, cols]
        value = jnp.transpose(value_ref[:, cols])
        operands = [head_operands(query, key, length, head) for head in range(2)]
        scores = [matmul_nt(operand[2], operand[1]) for operand in operands]
        parts = []
        for head in range(2):
            top = jnp.max(scores[head], axis=0, keepdims=True)
            powers = jnp.exp(scores[head] - top)
            total = jnp.sum(powers, axis=0, keepdims=True)
            probs = (powers * (1.0 / total)).astype(jnp.bfloat16)
            total_ref[0, pair, head : head + 1, :] = top + jnp.log(total)
            parts.append(matmul(value[head * HEAD_DIM : (head + 1) * HEAD_DIM], probs))
        ctx_ref[:, cols] = jnp.transpose(jnp.concatenate(parts, axis=0)).astype(jnp.bfloat16)


def pull_pair(length, query, key, value, grad, total_ref, queries_ref):
    operands = [head_operands(query, key, length, head) for head in range(2)]
    grads = [jnp.where(operand[3], grad, jnp.zeros_like(grad)) for operand in operands]
    flat_key = jnp.transpose(key * jnp.bfloat16(0.125))
    jobs = [(head, first) for first in range(0, SEQ, CHUNK) for head in range(2)]

    def begin(head, first):
        spot = slice(first, first + CHUNK)
        return (
            matmul_nt(operands[head][2], operands[head][1][spot]),
            matmul_nt(value, grads[head][spot]),
        )

    ready = begin(*jobs[0])
    key_grad = value_grad = jnp.zeros((SEQ, PAIR), jnp.float32)
    flat = []
    for index, (head, first) in enumerate(jobs):
        scores, prob_grad = ready
        if index + 1 < len(jobs):
            ready = begin(*jobs[index + 1])
        spot = slice(first, first + CHUNK)
        probs = jnp.exp(scores - total_ref[head : head + 1, spot])
        row_dot = jnp.sum(probs * prob_grad, axis=0, keepdims=True)
        score_grad = (probs * (prob_grad - row_dot)).astype(jnp.bfloat16)
        value_grad += matmul(probs.astype(jnp.bfloat16), grads[head][spot])
        key_grad += matmul(score_grad, operands[head][0][spot])
        flat.append(matmul(flat_key[head * HEAD_DIM : (head + 1) * HEAD_DIM], score_grad))
        if head:
            queries_ref[spot, :] = jnp.transpose(jnp.concatenate(flat, axis=0)).astype(jnp.bfloat16)
            flat = []
    return queries_ref[...], key_grad.astype(jnp.bfloat16), value_grad.astype(jnp.bfloat16)


def attention_pull_kernel(
    info,
    query_ref,
    key_ref,
    value_ref,
    grad_ref,
    total_ref,
    own_ref,
    other_ref,
    sum_ref,
    queries_ref,
    out_buffer,
    sems,
):
    length = info[1 + pl.program_id(0)]
    early = info[0] == 0
    part = pl.program_id(1)
    step = pl.program_id(0) * PARTS + part
    last = pl.num_programs(0) * PARTS - 1
    slot = lax.rem(step, 2)
    rows = pl.ds(pl.multiple_of(pl.program_id(0) * SEQ, SEQ), SEQ)
    width = STRIDE * PAIR

    def copy(which, ref, block, slot):
        cols = pl.ds(pl.multiple_of(block * width, width), width)
        return pltpu.make_async_copy(
            out_buffer.at[slot, which], ref.at[rows, cols], sems.at[slot, which]
        )

    def wait(slot):
        for which in range(3):
            copy(which, own_ref, 0, slot).wait()

    @pl.when(step >= 2)
    def _():
        wait(slot)

    for pair in range(STRIDE):
        cols = slice(pair * PAIR, (pair + 1) * PAIR)
        query_grad, key_grad, value_grad = pull_pair(
            length,
            query_ref[:, cols],
            key_ref[:, cols],
            value_ref[:, cols],
            grad_ref[:, cols],
            total_ref.at[0, pair],
            queries_ref.at[pair],
        )
        out_buffer[slot, 0, :, cols] = jnp.where(early, query_grad, value_grad)
        out_buffer[slot, 1, :, cols] = jnp.where(early, value_grad, query_grad)
        out_buffer[slot, 2, :, cols] = key_grad
        for place, values in enumerate((query_grad, value_grad)):
            total = jnp.sum(values.astype(jnp.float32), axis=0, keepdims=True)
            sum_ref[0, pair, place : place + 1, :] = total
    copy(0, own_ref, part, slot).start()
    copy(1, other_ref, part, slot).start()
    mine = (part == 0) == early

    @pl.when(mine)
    def _():
        copy(2, own_ref, PARTS, slot).start()

    @pl.when(jnp.logical_not(mine))
    def _():
        copy(2, other_ref, PARTS, slot).start()

    @pl.when(step == last)
    def _():
        wait(1 - slot)
        wait(slot)


def pick(place):
    def spot(s, t, info):
        return s, place(t, info[0])

    return pl.BlockSpec((SEQ, STRIDE * PAIR), spot)


def query_place(part, core):
    return 3 * core + part


def key_place(part, core):
    return lax.select(core == 0, 2 + 3 * part, 5 - 3 * part)


def value_place(part, core):
    return 3 - 3 * core + part


def part_spec():
    return pl.BlockSpec((SEQ, STRIDE * PAIR), lambda s, t, info: (s, t))


def part_rows(width):
    return pl.BlockSpec((1, STRIDE, 2, width), lambda s, t, info: (s, t, 0, 0))


def attention(info, qkv, slots):
    rows = qkv.shape[0]
    return pl.pallas_call(
        attention_kernel,
        grid_spec=pltpu.PrefetchScalarGridSpec(
            num_scalar_prefetch=1,
            grid=(slots, PARTS),
            in_specs=[pick(query_place), pick(key_place), pick(value_place)],
            out_specs=[part_spec(), part_rows(SEQ)],
        ),
        out_shape=[
            jax.ShapeDtypeStruct((rows, D), jnp.bfloat16),
            jax.ShapeDtypeStruct((slots, PAIRS, 2, SEQ), jnp.float32),
        ],
        compiler_params=pltpu.CompilerParams(vmem_limit_bytes=52 << 20),
        cost_estimate=SMALL,
        name="attention",
    )(info, qkv, qkv, qkv)


def attention_pull(info, qkv, grad, log_total, slots):
    rows = qkv.shape[0]
    table = jax.ShapeDtypeStruct((rows, BLOCKS // 2 * PAIR), jnp.bfloat16)
    return pl.pallas_call(
        attention_pull_kernel,
        grid_spec=pltpu.PrefetchScalarGridSpec(
            num_scalar_prefetch=1,
            grid=(slots, PARTS),
            in_specs=[pick(query_place), pick(key_place), pick(value_place)]
            + [part_spec(), part_rows(SEQ)],
            out_specs=[pl.BlockSpec(memory_space=pl.ANY)] * 2 + [part_rows(PAIR)],
            scratch_shapes=[
                pltpu.VMEM((STRIDE, SEQ, PAIR), jnp.bfloat16),
                pltpu.VMEM((2, 3, SEQ, STRIDE * PAIR), jnp.bfloat16),
                pltpu.SemaphoreType.DMA((2, 3)),
            ],
        ),
        out_shape=[table] * 2 + [jax.ShapeDtypeStruct((slots, PAIRS, 2, PAIR), jnp.float32)],
        compiler_params=pltpu.CompilerParams(vmem_limit_bytes=52 << 20),
        cost_estimate=SMALL,
        name="attention_pull",
    )(info, qkv, qkv, qkv, grad, log_total)


def join_halves(core, own, other):
    return jnp.where(
        core == 0,
        jnp.concatenate([own, other], axis=1),
        jnp.concatenate([other, own], axis=1),
    )


def vector_kernel(info, own_ref, other_ref, vec_ref, bias_ref, own_bias_ref, other_bias_ref):
    early_core = info[0] == 0
    rows = VROWS // 2
    own = jnp.transpose(own_ref[...].astype(jnp.float32))[:rows]
    other = jnp.transpose(other_ref[...].astype(jnp.float32))[:rows]
    vec = jnp.concatenate(
        [jnp.where(early_core, own, other), jnp.where(early_core, other, own)], axis=0
    )
    vec_ref[0:VROWS, :] = vec
    up_rows = FF // D
    for place in range(up_rows):
        early, late = 5 + place, 5 + (place + up_rows // 2) % up_rows
        row = jnp.where(early_core, vec[early : early + 1], vec[late : late + 1])
        bias_ref[0:1, place * D : (place + 1) * D] = row
    own_bias_ref[...] = jnp.zeros_like(own_bias_ref)
    other_bias_ref[...] = jnp.zeros_like(other_bias_ref)
    own_bias_ref[0:1, :D] = jnp.where(early_core, vec[0:1], vec[1:2])
    other_bias_ref[0:1, :D] = jnp.where(early_core, vec[1:2], vec[0:1])


def vector_tables(info, own, other):
    half = own.shape[1] - VEC_PAD
    spec = pl.BlockSpec((D, VEC_PAD), lambda i: (0, half // VEC_PAD))
    shapes = [(16, D), (8, FF), (8, half), (8, half)]
    return pl.pallas_call(
        vector_kernel,
        grid=(1,),
        in_specs=[pl.BlockSpec(memory_space=pltpu.SMEM), spec, spec],
        out_specs=[pl.BlockSpec(shape, lambda i: (0, 0)) for shape in shapes],
        out_shape=[jax.ShapeDtypeStruct(shape, jnp.float32) for shape in shapes],
        name="vector_tables",
    )(info, own, other)


def vector_grad_kernel(info, low_ref, high_ref, bias_ref, head_ref, out_ref):
    early_core = info[0] == 0
    out_ref[...] = jnp.zeros_like(out_ref)
    for pair in range(PAIRS):
        cols = slice(pair * PAIR, (pair + 1) * PAIR)
        out_ref[0:2, cols] = jnp.sum(head_ref[:, pair], axis=0)
    out_ref[2:5, :] = low_ref[0:3, :]
    up_rows = FF // D
    for place in range(up_rows):
        late = (place + up_rows // 2) % up_rows
        out_ref[5 + place : 6 + place, :] = jnp.where(
            early_core,
            bias_ref[0:1, place * D : (place + 1) * D],
            bias_ref[0:1, late * D : (late + 1) * D],
        )
    out_ref[5 + up_rows : 8 + up_rows, :] = high_ref[0:3, :]


def vector_grads(info, low_sums, high_sums, bias_sums, head_sums):
    whole = pl.BlockSpec(memory_space=pltpu.VMEM)
    return pl.pallas_call(
        vector_grad_kernel,
        in_specs=[pl.BlockSpec(memory_space=pltpu.SMEM)] + [whole] * 4,
        out_specs=whole,
        out_shape=jax.ShapeDtypeStruct((16, D), jnp.float32),
        name="vector_grads",
    )(info, low_sums, high_sums, bias_sums, head_sums)


def hidden_pieces(own, other):
    return [
        (ref, slice(first, first + D), place + first)
        for place, ref in ((0, own), (WIDE, other))
        for first in range(0, WIDE, D)
    ]


OUT_COLS = slice(WIDE, WIDE + D // 2)


def raise_kernel(
    info,
    vec_ref,
    bias_ref,
    x_ref,
    ctx_ref,
    own,
    other,
    xhat_ref,
    rstd_ref,
    low_ref,
    own_act_ref,
    other_act_ref,
    slope_ref,
):
    ctx = ctx_ref[...]
    attended = join_halves(info[0], matmul(ctx, own[:, OUT_COLS]), matmul(ctx, other[:, OUT_COLS]))
    xhat, rstd = norm_parts(x_ref[...].astype(jnp.float32) + (attended + vec_ref[2:3, :]))
    xhat_ref[...] = xhat
    rstd_ref[...] = jnp.broadcast_to(rstd, rstd_ref.shape)
    hidden = (xhat * vec_ref[3:4, :] + vec_ref[4:5, :]).astype(jnp.bfloat16)
    low_ref[...] = hidden
    for ref, cols, place in hidden_pieces(own, other):
        spot = slice(place, place + D)
        act, slope = gelu_parts(matmul(hidden, ref[:, cols]) + bias_ref[0:1, spot])
        act_ref = own_act_ref if place < WIDE else other_act_ref
        act_ref[:, cols] = act.astype(jnp.bfloat16)
        slope_ref[:, spot] = slope.astype(jnp.bfloat16)


def add_sums(ref, sums):
    first = pl.program_id(0) == 0
    for place, values in enumerate(sums):
        total = jnp.sum(values, axis=0, keepdims=True)
        spot = slice(place, place + 1)
        ref[spot, :] = jnp.where(first, total, ref[spot, :] + total)


def lower_kernel(
    info, vec_ref, xhat_ref, first_ref, second_ref, cot_ref, out_ref, grad_ref, low_ref, sum_ref
):
    first = pl.program_id(0) * ROWS
    hidden = xhat_ref[...] * vec_ref[3:4, :] + vec_ref[4:5, :]
    xhat, rstd = norm_parts(hidden + (first_ref[...] + second_ref[...] + vec_ref[9:10, :]))
    gain = vec_ref[10:11, :]
    out_ref[...] = (xhat * gain + vec_ref[11:12, :]).astype(jnp.bfloat16)
    limit = info[INFO + lax.div(first, SEQ)]
    row = lax.broadcasted_iota(jnp.int32, (ROWS, 1), 0) + lax.rem(first, SEQ)
    cot = jnp.where(row < limit, cot_ref[...].astype(jnp.float32), 0.0)
    grad = norm_pull(cot, gain, xhat, rstd)
    grad_ref[...] = grad
    low = grad.astype(jnp.bfloat16)
    low_ref[...] = low
    add_sums(sum_ref, (low.astype(jnp.float32), cot * xhat, cot))


def pull_kernel(
    info,
    vec_ref,
    xhat_ref,
    rstd_ref,
    slope_ref,
    grad_ref,
    low_ref,
    up_own,
    up_other,
    own,
    other,
    own_pre_ref,
    other_pre_ref,
    skip_ref,
    attn_ref,
    ctx_ref,
    sum_ref,
    bias_ref,
):
    core = info[0]
    low = low_ref[...]
    hidden_grad = grad_ref[...]
    for down, up in zip(hidden_pieces(own, other), hidden_pieces(up_own, up_other)):
        ref, cols, place = down
        spot = slice(place, place + D)
        pre = matmul(low, ref[:, cols]) * slope_ref[:, spot].astype(jnp.float32)
        pre = pre.astype(jnp.bfloat16)
        pre_ref = own_pre_ref if place < WIDE else other_pre_ref
        pre_ref[:, cols] = pre
        hidden_grad = hidden_grad + matmul_nt(pre, up[0][:, up[1]])
    xhat = xhat_ref[...]
    skip = norm_pull(hidden_grad, vec_ref[3:4, :], xhat, rstd_ref[:, 0:1])
    skip_ref[...] = skip
    attn = skip.astype(jnp.bfloat16)
    attn_ref[...] = attn
    left, right = attn[:, : D // 2], attn[:, D // 2 :]
    ctx = matmul_nt(jnp.where(core == 0, left, right), up_own[:, OUT_COLS])
    ctx = ctx + matmul_nt(jnp.where(core == 0, right, left), up_other[:, OUT_COLS])
    ctx_ref[...] = ctx.astype(jnp.bfloat16)
    add_sums(sum_ref, (attn.astype(jnp.float32), hidden_grad * xhat, hidden_grad))
    add_sums(bias_ref.at[:, :WIDE], (own_pre_ref[...].astype(jnp.float32),))
    add_sums(bias_ref.at[:, WIDE:], (other_pre_ref[...].astype(jnp.float32),))


def row_spec(width):
    return pl.BlockSpec((ROWS, width), lambda i: (i, 0))


def whole_spec():
    return pl.BlockSpec(memory_space=pltpu.VMEM)


def row_call(kernel, name, in_specs, rows, outs, sums, flops, operands):
    shapes = [jax.ShapeDtypeStruct((rows, width), kind) for width, kind in outs]
    shapes += [jax.ShapeDtypeStruct((8, width), jnp.float32) for width in sums]
    return pl.pallas_call(
        kernel,
        grid=(rows // ROWS,),
        in_specs=[pl.BlockSpec(memory_space=pltpu.SMEM)] + in_specs,
        out_specs=[row_spec(width) for width, kind in outs]
        + [pl.BlockSpec((8, width), lambda i: (0, 0)) for width in sums],
        out_shape=shapes,
        compiler_params=pltpu.CompilerParams(vmem_limit_bytes=52 << 20),
        cost_estimate=SMALL,
        name=name,
    )(*operands)


def raise_rows(info, vec, bias, tokens, context, own, other):
    low, full = jnp.bfloat16, jnp.float32
    return row_call(
        raise_kernel,
        "raise_rows",
        [whole_spec()] * 2 + [row_spec(D)] * 2 + [whole_spec()] * 2,
        tokens.shape[0],
        [(D, full), (PAIR, full), (D, low), (WIDE, low), (WIDE, low), (FF, low)],
        [],
        14 << 30,
        (info, vec, bias, tokens, context, own, other),
    )


def lower_rows(info, vec, xhat, first, second, cotangent):
    low, full = jnp.bfloat16, jnp.float32
    return row_call(
        lower_kernel,
        "lower_rows",
        [whole_spec()] + [row_spec(D)] * 4,
        first.shape[0],
        [(D, low), (D, full), (D, low)],
        [D],
        4 << 30,
        (info, vec, xhat, first, second, cotangent),
    )


def pull_rows(info, vec, xhat, rstd, slope, grad, low_grad, up, down):
    low, full = jnp.bfloat16, jnp.float32
    return row_call(
        pull_kernel,
        "pull_rows",
        [whole_spec(), row_spec(D), row_spec(PAIR), row_spec(FF), row_spec(D), row_spec(D)]
        + [whole_spec()] * 4,
        xhat.shape[0],
        [(WIDE, low), (WIDE, low), (D, full), (D, low), (D, low)],
        [D, FF],
        18 << 30,
        (info, vec, xhat, rstd, slope, grad, low_grad, *up, *down),
    )


def split_rest(values):
    high = values.astype(jnp.bfloat16)
    return high, (values - high.astype(jnp.float32)).astype(jnp.bfloat16)

def store_split(values, where, high_ref, rest_ref):
    high_ref[where], rest_ref[where] = split_rest(values)

def close_product(left, right, rows, cols):
    left_high, left_rest = left[0][rows, :], left[1][rows, :]
    right_high, right_rest = right[0][:, cols], right[1][:, cols]
    return matmul(
        jnp.concatenate([left_high, left_high, left_rest], axis=1),
        jnp.concatenate([right_high, right_rest, right_high], axis=0),
    )


def mirrored_product(left, right, finish):
    for first in range(0, D, TILE):
        rows = slice(first, first + TILE)
        wide = close_product(left, right, rows, slice(first, D))
        for last in range(first, D, TILE):
            tile = wide[:, last - first : last - first + TILE]
            cols = slice(last, last + TILE)
            finish(tile, rows, cols)
            if first < last:
                finish(jnp.transpose(tile), cols, rows)


def polar_kernel(
    start_ref,
    own_ref,
    other_ref,
    cols_ref,
    polar_ref,
    out_ref,
    gram,
    a_high,
    a_rest,
    q_high,
    q_rest,
    b_high,
    b_rest,
    r_high,
    r_rest,
):
    a, q, b, r = (a_high, a_rest), (q_high, q_rest), (b_high, b_rest), (r_high, r_rest)
    count = out_ref.shape[0]
    start = pl.multiple_of(start_ref[0], 16)
    whole = own_ref[...] + other_ref[...]
    row = lax.broadcasted_iota(jnp.int32, (D, D), 0)
    col = lax.broadcasted_iota(jnp.int32, (D, D), 1)
    scale = jnp.sqrt(jnp.sum(jnp.where(row == col, whole, 0.0), keepdims=True)) + 1e-07
    gram[...] = whole / (scale * scale)
    whole_rows = (slice(0, count), slice(0, D))

    def sweep(index, carry):
        every = slice(0, D)
        store_split(gram[...], (every, every), a_high, a_rest)

        def step_tile(tile, where_rows, where_cols):
            step = poly_second * gram[where_rows, where_cols] + poly_third * tile
            if where_rows == where_cols:
                tile_row = lax.broadcasted_iota(jnp.int32, (TILE, TILE), 0)
                tile_col = lax.broadcasted_iota(jnp.int32, (TILE, TILE), 1)
                step = step + jnp.where(tile_row == tile_col, poly_first, 0.0)
            store_split(step, (where_rows, where_cols), q_high, q_rest)

        mirrored_product(a, a, step_tile)

        @pl.when(index == 0)
        def _():
            rows = pl.ds(start, count)
            out_ref[...] = q_high[rows, :].astype(jnp.float32) + q_rest[rows, :].astype(jnp.float32)

        @pl.when(index > 0)
        def _():
            store_split(out_ref[...], whole_rows, r_high, r_rest)
            out_ref[...] = close_product(r, q, slice(0, count), every)

        def half_tile(tile, where_rows, where_cols):
            store_split(tile, (where_rows, where_cols), b_high, b_rest)

        def gram_tile(tile, where_rows, where_cols):
            gram[where_rows, where_cols] = tile

        mirrored_product(q, a, half_tile)
        mirrored_product(b, q, gram_tile)
        return carry

    lax.fori_loop(0, NS_ITERS - 1, sweep, 0)
    every = slice(0, D)
    store_split(gram[...], (every, every), a_high, a_rest)
    before = out_ref[...]
    store_split(before, whole_rows, r_high, r_rest)
    once = close_product(r, a, slice(0, count), every)
    store_split(once, whole_rows, r_high, r_rest)
    twice = close_product(r, a, slice(0, count), every)
    out_ref[...] = poly_first * before + poly_second * once + poly_third * twice
    both = jnp.concatenate(split_rest(out_ref[...] / scale), axis=0)
    for place in range(0, cols_ref.shape[1], D):
        spot = slice(place, place + D)
        product = matmul(both, cols_ref[:, spot])
        polar_ref[:, spot] = (product[:count] + product[count:]).astype(jnp.bfloat16)

def polar_rows(start, own, other, columns, count):
    half = pltpu.VMEM((D, D), jnp.bfloat16)
    short = pltpu.VMEM((count, D), jnp.bfloat16)
    return pl.pallas_call(
        polar_kernel,
        in_specs=[pl.BlockSpec(memory_space=pltpu.SMEM)]
        + [pl.BlockSpec(memory_space=pltpu.VMEM)] * 3,
        out_specs=pl.BlockSpec(memory_space=pltpu.VMEM),
        out_shape=jax.ShapeDtypeStruct((count, columns.shape[1]), jnp.bfloat16),
        scratch_shapes=[pltpu.VMEM((count, D), jnp.float32), pltpu.VMEM((D, D), jnp.float32)]
        + [half] * 6
        + [short] * 2,
        compiler_params=pltpu.CompilerParams(vmem_limit_bytes=40 << 20),
        name="polar_rows",
    )(start, own, other, columns)


def per_device(
    size,
    tokens,
    cotangent,
    counts,
    lengths,
    w_qkv,
    w_out,
    w_up,
    w_down,
    vectors,
    mom_qkv,
    mom_out,
    mom_up,
    mom_down,
    adam_first,
    adam_second,
):
    me = lax.axis_index("fsdp")
    core = lax.axis_index("row")
    slots = lengths.shape[0]
    rows = tokens.shape[0]
    up_rows = FF // D
    low = jnp.bfloat16

    block_rows = D // size
    qkv_half, up_half = w_qkv.shape[1], w_up.shape[1]
    vec_rows = vectors.shape[0]
    narrow = qkv_half - D

    def pick_core(early, late):
        return jnp.where(core == 0, early, late)

    def turn(values, cut):
        return pick_core(values, jnp.concatenate([values[:, cut:], values[:, :cut]], axis=1))

    vec_block = jnp.pad(vectors.T, ((0, 0), (0, VEC_PAD - vec_rows))).astype(low)
    first_block = jnp.concatenate([turn(w_qkv.astype(low), narrow), vec_block], axis=1)
    second_block = jnp.concatenate([w_up.astype(low), w_out.astype(low)], axis=1)
    third_block = w_down.astype(low)
    near, far = size.bit_length() - 3, size.bit_length() - 2
    steps = [1 << near, 1 << far, 3 << near]
    first_pieces = send_high(first_block, size)
    second_pieces = [second_block, flip(second_block, steps[0], size)]
    first_pieces, second_pieces, third_block = together(first_pieces, second_pieces, third_block)
    first_pieces = send_low(sort_high(first_pieces, size), size)
    second_pieces += [flip(second_pieces[0], step, size) for step in steps[1:]]
    first_pieces, second_pieces, third_block = together(first_pieces, second_pieces, third_block)
    first_own = sort_low(first_pieces)
    first_other = swap_cores(first_own)
    second_pieces = send_low(sort_high(second_pieces, size), size)
    third_pieces = [third_block, flip(third_block, steps[0], size)]

    live = jnp.arange(slots) % CAP < counts.reshape(-1)[jnp.arange(slots) // CAP]
    info = jnp.concatenate(
        [core.reshape(1).astype(jnp.int32), lengths, jnp.where(live, lengths, 0)]
    )
    vec, bias_up, bias_own, bias_other = vector_tables(info, first_own, first_other)
    qkv_own, qkv_other = first_own[:, :qkv_half], first_other[:, :qkv_half]
    projected = jnp.concatenate(
        [
            (matmul(tokens, qkv_own) + bias_own[:1]).astype(low),
            (matmul(tokens, qkv_other) + bias_other[:1]).astype(low),
        ],
        axis=1,
    )
    projected, third_pieces = together(projected, third_pieces)
    third_pieces += [flip(third_pieces[0], step, size) for step in steps[1:]]
    context, log_total = attention(info, projected, slots)
    context, second_pieces, third_pieces = together(context, second_pieces, third_pieces)
    second_own = sort_low(second_pieces)
    third_pieces = send_low(sort_high(third_pieces, size), size)
    second_other = swap_cores(second_own)
    xhat_one, rstd_one, hidden_low, act_own, act_other, slope = raise_rows(
        info, vec, bias_up, tokens, context, second_own, second_other
    )
    act_own, act_other, *third_pieces = together(act_own, act_other, *third_pieces)
    third_own = sort_low(third_pieces)
    third_other = swap_cores(third_own)
    branch = matmul_nt(act_own, third_own)
    branch, third_other = together(branch, third_other)
    layer_out, top_grad, branch_low, high_sums = lower_rows(
        info, vec, xhat_one, branch, matmul_nt(act_other, third_other), cotangent
    )

    leaving = matmul_tn(branch_low, act_other).astype(low)
    leaving, branch_low = together(leaving, branch_low)
    down_arrived = swap_cores(leaving)
    down_own = matmul_tn(branch_low, act_own)
    down_own, down_arrived, branch_low = together(down_own, down_arrived, branch_low)
    down_kept, leaving = split_low([(down_own, down_arrived)], size)
    leaving, branch_low = together(leaving, branch_low)
    down_sent = fly_low(leaving, size)
    pulled = pull_rows(
        info,
        vec,
        xhat_one,
        rstd_one,
        slope,
        top_grad,
        branch_low,
        (second_own, second_other),
        (third_own, third_other),
    )
    pulled, down_sent = together(pulled, down_sent)
    pre_own, pre_other, skip_grad, attn_low, context_grad, low_sums, bias_sums = pulled
    down_kept, leaving = split_near(down_kept, down_sent, size)
    leaving, pre_own, pre_other, attn_low = together(leaving, pre_own, pre_other, attn_low)
    down_sent = fly_near(leaving, size)
    up_leaving = matmul_tn(hidden_low, pre_other).astype(low)
    up_leaving, pre_own, attn_low, down_sent = together(up_leaving, pre_own, attn_low, down_sent)
    up_arrived = swap_cores(up_leaving)
    down_kept, down_leaving = split_far(down_kept, down_sent, size)
    out_own = pick_core(attn_low[:, : D // 2], attn_low[:, D // 2 :])
    out_other = pick_core(attn_low[:, D // 2 :], attn_low[:, : D // 2])
    out_arrived = swap_cores(matmul_tn(context, out_other).astype(low))
    up_own = matmul_tn(hidden_low, pre_own)
    out_own = matmul_tn(context, out_own)
    up_own, out_own, up_arrived, out_arrived = together(up_own, out_own, up_arrived, out_arrived)
    wide_kept, leaving = split_low([(up_own, up_arrived), (out_own, out_arrived)], size)
    leaving, down_leaving, context_grad = together(leaving, down_leaving, context_grad)
    wide_sent = fly_low(leaving, size)
    down_sent = fly_far(down_leaving, size)
    parts = attention_pull(info, projected, context_grad, log_total, slots)
    parts, down_sent = together(parts, down_sent)

    leaving = matmul_tn(tokens, parts[1]).astype(low)
    qkv_leaving, parts, wide_sent, down_sent = together(leaving, parts, wide_sent, down_sent)
    wide_kept, leaving = split_near(wide_kept, wide_sent, size)
    leaving, parts = together(leaving, parts)
    wide_sent = fly_near(leaving, size)
    qkv_arrived = swap_cores(qkv_leaving)
    qkv_part = matmul_tn(tokens, parts[0])
    (grad_down,) = add_four(down_kept, [down_sent])
    moment_down = moment_decay * mom_down + grad_down
    qkv_part, qkv_arrived, grads, moment_down = together(qkv_part, qkv_arrived, parts, moment_down)
    qkv_kept, leaving = split_low([(qkv_part + qkv_arrived.astype(jnp.float32),)], size)
    leaving, grads, down_block = together(leaving, grads, moment_down.astype(low))
    qkv_sent = fly_low(leaving, size)
    down_sent = fly_far(down_block, size)
    wide_sent, down_sent = together(wide_sent, down_sent)
    wide_kept, wide_leaving = split_far(wide_kept, wide_sent, size)
    wide_sent = fly_far(wide_leaving, size)
    qkv_sent, wide_sent, down_sent = together(qkv_sent, wide_sent, down_sent)
    qkv_kept, leaving = split_high(qkv_kept, qkv_sent, size)
    leaving, wide_sent, down_sent = together(leaving, wide_sent, down_sent)
    qkv_sent = fly_high(leaving, size)
    grad_up, grad_out = add_four(wide_kept, [wide_sent])
    moment_up = moment_decay * mom_up + grad_up
    moment_out = moment_decay * mom_out + grad_out
    wide_block = jnp.concatenate([moment_up.astype(low), moment_out.astype(low)], axis=1)
    wide_sent = fly_far(wide_block, size)
    down_pair = place_far(down_block, down_sent, size)
    down_sent = fly_near(down_pair, size)
    mom_turned = turn(mom_qkv, narrow)
    vector_grad = vector_grads(info, low_sums, high_sums, bias_sums, grads[2])
    qkv_sent, wide_sent, down_sent, grads, vector_grad, mom_turned = together(
        qkv_sent, wide_sent, down_sent, grads, vector_grad, mom_turned
    )
    (grad_turned,) = add_four(qkv_kept, qkv_sent)
    qkv_block = (moment_decay * mom_turned + grad_turned).astype(low)
    wide_pair = place_far(wide_block, wide_sent, size)
    qkv_block, grad_turned, wide_pair = together(qkv_block, grad_turned, wide_pair)
    qkv_pieces = send_high(qkv_block, size)
    wide_sent = fly_near(wide_pair, size)
    vector_grad = vector_grad + swap_cores(vector_grad)
    vector_arrived = flip(vector_grad, 1, size)
    down_rows = place_near(down_pair, down_sent, size)
    grad_qkv = turn(grad_turned, D)
    moment_qkv = moment_decay * mom_qkv + grad_qkv
    grad_qkv, moment_qkv, qkv_pieces, wide_sent, down_rows = together(
        grad_qkv, moment_qkv, qkv_pieces, wide_sent, down_rows
    )
    wide_rows = place_near(wide_pair, wide_sent, size)

    qkv_rows = merge_rows(sort_high(qkv_pieces, size))
    place = me % GROUP

    def widen(values):
        return jnp.pad(values, ((0, 0), (0, WIDE - values.shape[1])))

    matrices = (
        widen(qkv_rows),
        widen(wide_rows[:, up_half:]),
        wide_rows[:, :up_half],
        down_rows,
    )

    def matrix_at(which):
        lower = jnp.where(which == 0, matrices[0], matrices[1])
        upper = jnp.where(which == 2, matrices[2], matrices[3])
        return jnp.where(which < 2, lower, upper)

    pieces = []
    for step in range(GROUP):
        pieces.append(matrix_at(place ^ step).reshape(-1, block_rows, WIDE))
    pieces, grads, vector_grad, vector_arrived = together(
        pieces, grads, vector_grad, vector_arrived
    )
    pieces = pieces[:1] + [flip(pieces[step], step, size) for step in range(1, GROUP)]
    vector_grad = vector_grad + vector_arrived
    vector_arrived = flip(vector_grad, 2, size)
    input_grad = (
        skip_grad + matmul_nt(grads[0], qkv_own) + matmul_nt(grads[1], qkv_other)
    )
    pieces, input_grad, vector_grad, vector_arrived = together(
        pieces, input_grad, vector_grad, vector_arrived
    )
    columns = sort_low(pieces)
    for bit in range(2, size.bit_length() - 3, 2):
        columns = sort_low(send_four(columns.reshape(4, -1, WIDE), bit, size))
    gram = matmul_nt(columns, columns)
    start = ((me - place) * block_rows).reshape(1).astype(jnp.int32)
    vector_grad = vector_grad + vector_arrived
    gram, vector_grad = together(gram, vector_grad)
    gram_arrived = swap_cores(gram)
    vector_arrived = flip(vector_grad, 4, size)
    gram_arrived, vector_arrived = together(gram_arrived, vector_arrived)
    vector_grad = vector_grad + vector_arrived
    polar = polar_rows(start, gram, gram_arrived, columns, GROUP * block_rows)
    polar, vector_grad = together(polar, vector_grad)
    for bit in range(3, size.bit_length() - 1):
        vector_grad = vector_grad + flip(vector_grad, 1 << bit, size)
    grad_vectors = lax.dynamic_slice(
        vector_grad, (core * vec_rows, me * block_rows), (vec_rows, block_rows)
    )
    polar = polar.reshape(GROUP, block_rows, WIDE)
    arrived = []
    for step in range(GROUP):
        block = lax.dynamic_index_in_dim(polar, place ^ step, 0, keepdims=False)
        arrived.append(flip(block, step, size) if step else block)
    arrived = sort_four(arrived, 0, 0)
    masters = (w_qkv, w_out, w_up, w_down)
    counts_of = (3 * D, D, FF, FF)
    updated = []
    for index in range(GROUP):
        ortho = arrived[index][:, : masters[index].shape[1]].astype(jnp.float32)
        if index == 0:
            ortho = turn(ortho, D)
        updated.append(
            masters[index] * (1.0 - muon_rate * decay_rate)
            - muon_rate * 0.2 * math.sqrt(counts_of[index]) * ortho
        )

    first_moment = beta_first * adam_first + (1.0 - beta_first) * grad_vectors
    second_moment = beta_second * adam_second + (1.0 - beta_second) * grad_vectors * grad_vectors
    direction = (
        first_moment
        / (1.0 - beta_first**STEP)
        / (jnp.sqrt(second_moment / (1.0 - beta_second**STEP)) + adam_eps)
    )
    new_vectors = vectors - adam_rate * (direction + decay_rate * vectors)
    return (
        layer_out,
        input_grad,
        grad_qkv,
        grad_out,
        grad_up,
        grad_down,
        grad_vectors,
        moment_qkv,
        moment_out,
        moment_up,
        moment_down,
        updated[0],
        updated[1],
        updated[2],
        updated[3],
        first_moment,
        second_moment,
        new_vectors,
    )


def solution(mesh):
    size = mesh.shape["fsdp"]

    def run(*arrays):
        return per_device(size, *arrays)

    weight = P("fsdp", "row")
    vector = P("row", "fsdp")
    sample = P(("fsdp", "row"), None)
    return jax.shard_map(
        run,
        mesh=mesh,
        in_specs=(sample, sample, sample, P(("fsdp", "row")))
        + (weight,) * 4
        + (vector,)
        + (weight,) * 4
        + (vector,) * 2,
        out_specs=(sample, sample)
        + (weight,) * 4
        + (vector,)
        + (weight,) * 8
        + (vector,) * 3,
        check_vma=False,
    )
```

```python
import math

import jax
import jax.numpy as jnp
from jax import lax
from jax.experimental import pallas as pl
from jax.experimental.layout import Layout, with_layout_constraint
from jax.experimental.pallas import tpu as pltpu
from jax.sharding import PartitionSpec as P

D = 768
FF = 3072
HEADS = 12
HEAD_DIM = 64
SEQ = 512
CAP = 1
MICRO = 2
NS_ITERS = 5
STEP = 10

norm_eps = 1e-05
mask_fill = -1e30
poly_first = 3.4445
poly_second = -4.775
poly_third = 2.0315
muon_rate = 0.2
adam_rate = 0.8
decay_rate = 0.01
moment_decay = 0.5
beta_first = 0.9
beta_second = 0.98
adam_eps = 1e-06

SWAP = [(0, 1), (1, 0)]
VEC_PAD = 128
GROUP = 4
TILE = 256
PARTS = 2
STRIDE = HEADS // 2 // PARTS
CHUNK = 256
ROWS = 256
VROWS = 8 + FF // D
SMALL = pl.CostEstimate(flops=1 << 20, bytes_accessed=1 << 16, transcendentals=0)
PAIR = 2 * HEAD_DIM
PAIRS = HEADS // 2
BLOCKS = 3 * PAIRS
INFO = 1 + CAP * MICRO
WIDE = FF // 2


def matmul(former, latter):
    return jnp.dot(former, latter, preferred_element_type=jnp.float32)


def matmul_tn(former, latter):
    return lax.dot_general(
        former, latter, (((0,), (0,)), ((), ())), preferred_element_type=jnp.float32
    )


def matmul_nt(former, latter):
    return lax.dot_general(
        former, latter, (((1,), (1,)), ((), ())), preferred_element_type=jnp.float32
    )


def by_rows(values):
    return with_layout_constraint(values, Layout(major_to_minor=tuple(range(values.ndim))))


def flip(values, mask, size):
    return by_rows(lax.ppermute(by_rows(values), "fsdp", [(i, i ^ mask) for i in range(size)]))


def swap_cores(values):
    return by_rows(lax.ppermute(by_rows(values), "row", SWAP))


def together(*values):
    return lax.optimization_barrier(values)


def my_bit(bit):
    return (lax.axis_index("fsdp") >> bit) & 1


def pair_of(bit):
    return (lax.axis_index("fsdp") >> bit) & 3


def send_four(values, bit, size):
    return [values] + [flip(values, step << bit, size) for step in (1, 2, 3)]


def sort_four(pieces, bit, axis):
    low, high = my_bit(bit) == 1, my_bit(bit + 1) == 1
    first = jnp.where(low, jnp.stack(pieces[1::-1], axis), jnp.stack(pieces[:2], axis))
    second = jnp.where(low, jnp.stack(pieces[:1:-1], axis), jnp.stack(pieces[2:], axis))
    return jnp.where(
        high,
        jnp.concatenate([second, first], axis),
        jnp.concatenate([first, second], axis),
    )


def merge_rows(values):
    return values.reshape(-1, values.shape[-1])


def send_high(block, size):
    return send_four(block, size.bit_length() - 3, size)


def sort_high(pieces, size):
    return sort_four(pieces, size.bit_length() - 3, 0)


def send_low(values, size):
    for bit in range(size.bit_length() - 5, 0, -2):
        values = sort_four(send_four(values, bit, size), bit, -3)
    return send_four(values, 0, size)


def sort_low(pieces):
    return merge_rows(sort_four(pieces, 0, -3))


def pick_four(parts, axis, place):
    picked = []
    for part in parts:
        terms = part if isinstance(part, tuple) else (part,)
        blocks = [lax.dynamic_index_in_dim(term, place, axis, keepdims=False) for term in terms]
        picked.append(sum(block.astype(jnp.float32) for block in blocks))
    return picked


def split_four(parts, axis, bit):
    mine = pair_of(bit)
    leaving = []
    for step in (1, 2, 3):
        pieces = pick_four(parts, axis, mine ^ step)
        leaving.append(jnp.concatenate([part.astype(jnp.bfloat16) for part in pieces], axis=-1))
    return pick_four(parts, axis, mine), leaving


def fly_four(leaving, bit, size):
    return [flip(piece, step << bit, size) for step, piece in zip((1, 2, 3), leaving)]


def split_two(parts, axis, bit):
    mine = my_bit(bit)
    pieces = pick_four(parts, axis, 1 - mine)
    leaving = jnp.concatenate([part.astype(jnp.bfloat16) for part in pieces], axis=-1)
    return pick_four(parts, axis, mine), leaving


def place_two(values, arrived, bit, axis):
    return jnp.where(
        my_bit(bit) == 1,
        jnp.stack([arrived, values], axis),
        jnp.stack([values, arrived], axis),
    )


def add_four(kept, arrived):
    totals, place = [], 0
    for part in kept:
        cols = slice(place, place + part.shape[-1])
        place = cols.stop
        for piece in arrived:
            part = part + piece[..., cols].astype(jnp.float32)
        totals.append(part)
    return totals


def split_low(parts, size):
    shape = (4,) * ((size.bit_length() - 1) // 2) + (D // size, -1)
    parts = [tuple(term.reshape(shape) for term in part) for part in parts]
    return split_four(parts, len(shape) - 3, 0)


def fly_low(leaving, size):
    return fly_four(leaving, 0, size)


def add_low(kept, arrived, size):
    parts = add_four(kept, arrived)
    for bit in range(2, size.bit_length() - 3, 2):
        kept, leaving = split_four(parts, parts[0].ndim - 3, bit)
        parts = add_four(kept, fly_four(leaving, bit, size))
    return parts


def split_high(kept, arrived, size):
    return split_four(add_low(kept, arrived, size), 0, size.bit_length() - 3)


def split_near(kept, arrived, size):
    parts = [part.reshape((2, 2) + part.shape[1:]) for part in add_low(kept, arrived, size)]
    return split_two(parts, 1, size.bit_length() - 3)


def split_far(kept, arrived, size):
    return split_two(add_four(kept, [arrived]), 0, size.bit_length() - 2)


def fly_near(values, size):
    return flip(values, 1 << size.bit_length() - 3, size)


def fly_far(values, size):
    return flip(values, 1 << size.bit_length() - 2, size)


def place_far(values, arrived, size):
    return place_two(values, arrived, size.bit_length() - 2, 0)


def place_near(values, arrived, size):
    return merge_rows(place_two(values, arrived, size.bit_length() - 3, 1))


def fly_high(leaving, size):
    return fly_four(leaving, size.bit_length() - 3, size)


erf_slope = 0.3275911
erf_terms = (1.061405429, -1.453152027, 1.421413741, -0.284496736, 0.254829592)


def gelu_parts(pre_act):
    bell = jnp.exp(pre_act * pre_act * -0.5)
    inverse = 1.0 / (1.0 + jnp.abs(pre_act) * (erf_slope * math.sqrt(0.5)))
    poly = 0.5 * erf_terms[0] * inverse + 0.5 * erf_terms[1]
    for term in erf_terms[2:]:
        poly = poly * inverse + 0.5 * term
    tail = poly * inverse * bell
    cdf = jnp.where(pre_act < 0.0, tail, 1.0 - tail)
    return pre_act * cdf, cdf + pre_act * bell * (1.0 / math.sqrt(2.0 * math.pi))


def norm_parts(values):
    center = values - jnp.mean(values, axis=-1, keepdims=True)
    rstd = lax.rsqrt(jnp.mean(center * center, axis=-1, keepdims=True) + norm_eps)
    return center * rstd, rstd


def norm_pull(grad, gain, xhat, rstd):
    scaled = grad * gain
    return rstd * (
        scaled
        - jnp.mean(scaled, axis=-1, keepdims=True)
        - xhat * jnp.mean(scaled * xhat, axis=-1, keepdims=True)
    )


def head_lanes(shape, head):
    lane = lax.broadcasted_iota(jnp.int32, shape, 1)
    return (lane >= HEAD_DIM) if head else (lane < HEAD_DIM), lane == (0 if head else HEAD_DIM)


def head_operands(query, key, length, head):
    inside, spare = head_lanes(query.shape, head)
    zero = jnp.zeros_like(query)
    query_in = jnp.where(inside, query * jnp.bfloat16(0.125), zero)
    query_mask = jnp.where(spare, jnp.ones_like(query), query_in)
    row = lax.broadcasted_iota(jnp.int32, query.shape, 0)
    fill = jnp.where(row < length, 0.0, mask_fill).astype(jnp.bfloat16)
    key_mask = jnp.where(inside, key, jnp.where(spare, fill, zero))
    return query_in, query_mask, key_mask, inside


def attention_kernel(info, query_ref, key_ref, value_ref, ctx_ref, total_ref):
    length = info[1 + pl.program_id(0)]
    for pair in range(STRIDE):
        cols = slice(pair * PAIR, (pair + 1) * PAIR)
        query, key = query_ref[:, cols], key_ref[:, cols]
        value = jnp.transpose(value_ref[:, cols])
        operands = [head_operands(query, key, length, head) for head in range(2)]
        scores = [matmul_nt(operand[2], operand[1]) for operand in operands]
        parts = []
        for head in range(2):
            top = jnp.max(scores[head], axis=0, keepdims=True)
            powers = jnp.exp(scores[head] - top)
            total = jnp.sum(powers, axis=0, keepdims=True)
            probs = (powers * (1.0 / total)).astype(jnp.bfloat16)
            total_ref[0, pair, head : head + 1, :] = top + jnp.log(total)
            parts.append(matmul(value[head * HEAD_DIM : (head + 1) * HEAD_DIM], probs))
        ctx_ref[:, cols] = jnp.transpose(jnp.concatenate(parts, axis=0)).astype(jnp.bfloat16)


def pull_pair(length, query, key, value, grad, total_ref, queries_ref):
    operands = [head_operands(query, key, length, head) for head in range(2)]
    grads = [jnp.where(operand[3], grad, jnp.zeros_like(grad)) for operand in operands]
    flat_key = jnp.transpose(key * jnp.bfloat16(0.125))
    jobs = [(head, first) for first in range(0, SEQ, CHUNK) for head in range(2)]

    def begin(head, first):
        spot = slice(first, first + CHUNK)
        return (
            matmul_nt(operands[head][2], operands[head][1][spot]),
            matmul_nt(value, grads[head][spot]),
        )

    ready = begin(*jobs[0])
    key_grad = value_grad = jnp.zeros((SEQ, PAIR), jnp.float32)
    flat = []
    for index, (head, first) in enumerate(jobs):
        scores, prob_grad = ready
        if index + 1 < len(jobs):
            ready = begin(*jobs[index + 1])
        spot = slice(first, first + CHUNK)
        probs = jnp.exp(scores - total_ref[head : head + 1, spot])
        row_dot = jnp.sum(probs * prob_grad, axis=0, keepdims=True)
        score_grad = (probs * (prob_grad - row_dot)).astype(jnp.bfloat16)
        value_grad += matmul(probs.astype(jnp.bfloat16), grads[head][spot])
        key_grad += matmul(score_grad, operands[head][0][spot])
        flat.append(matmul(flat_key[head * HEAD_DIM : (head + 1) * HEAD_DIM], score_grad))
        if head:
            queries_ref[spot, :] = jnp.transpose(jnp.concatenate(flat, axis=0)).astype(jnp.bfloat16)
            flat = []
    return queries_ref[...], key_grad.astype(jnp.bfloat16), value_grad.astype(jnp.bfloat16)


def attention_pull_kernel(
    info,
    query_ref,
    key_ref,
    value_ref,
    grad_ref,
    total_ref,
    own_ref,
    other_ref,
    sum_ref,
    queries_ref,
    out_buffer,
    sems,
):
    length = info[1 + pl.program_id(0)]
    early = info[0] == 0
    part = pl.program_id(1)
    step = pl.program_id(0) * PARTS + part
    last = pl.num_programs(0) * PARTS - 1
    slot = lax.rem(step, 2)
    rows = pl.ds(pl.multiple_of(pl.program_id(0) * SEQ, SEQ), SEQ)
    width = STRIDE * PAIR

    def copy(which, ref, block, slot):
        cols = pl.ds(pl.multiple_of(block * width, width), width)
        return pltpu.make_async_copy(
            out_buffer.at[slot, which], ref.at[rows, cols], sems.at[slot, which]
        )

    def wait(slot):
        for which in range(3):
            copy(which, own_ref, 0, slot).wait()

    @pl.when(step >= 2)
    def _():
        wait(slot)

    for pair in range(STRIDE):
        cols = slice(pair * PAIR, (pair + 1) * PAIR)
        query_grad, key_grad, value_grad = pull_pair(
            length,
            query_ref[:, cols],
            key_ref[:, cols],
            value_ref[:, cols],
            grad_ref[:, cols],
            total_ref.at[0, pair],
            queries_ref.at[pair],
        )
        out_buffer[slot, 0, :, cols] = jnp.where(early, query_grad, value_grad)
        out_buffer[slot, 1, :, cols] = jnp.where(early, value_grad, query_grad)
        out_buffer[slot, 2, :, cols] = key_grad
        for place, values in enumerate((query_grad, value_grad)):
            total = jnp.sum(values.astype(jnp.float32), axis=0, keepdims=True)
            sum_ref[0, pair, place : place + 1, :] = total
    copy(0, own_ref, part, slot).start()
    copy(1, other_ref, part, slot).start()
    mine = (part == 0) == early

    @pl.when(mine)
    def _():
        copy(2, own_ref, PARTS, slot).start()

    @pl.when(jnp.logical_not(mine))
    def _():
        copy(2, other_ref, PARTS, slot).start()

    @pl.when(step == last)
    def _():
        wait(1 - slot)
        wait(slot)


def pick(place):
    def spot(s, t, info):
        return s, place(t, info[0])

    return pl.BlockSpec((SEQ, STRIDE * PAIR), spot)


def query_place(part, core):
    return 3 * core + part


def key_place(part, core):
    return lax.select(core == 0, 2 + 3 * part, 5 - 3 * part)


def value_place(part, core):
    return 3 - 3 * core + part


def part_spec():
    return pl.BlockSpec((SEQ, STRIDE * PAIR), lambda s, t, info: (s, t))


def part_rows(width):
    return pl.BlockSpec((1, STRIDE, 2, width), lambda s, t, info: (s, t, 0, 0))


def attention(info, qkv, slots):
    rows = qkv.shape[0]
    return pl.pallas_call(
        attention_kernel,
        grid_spec=pltpu.PrefetchScalarGridSpec(
            num_scalar_prefetch=1,
            grid=(slots, PARTS),
            in_specs=[pick(query_place), pick(key_place), pick(value_place)],
            out_specs=[part_spec(), part_rows(SEQ)],
        ),
        out_shape=[
            jax.ShapeDtypeStruct((rows, D), jnp.bfloat16),
            jax.ShapeDtypeStruct((slots, PAIRS, 2, SEQ), jnp.float32),
        ],
        compiler_params=pltpu.CompilerParams(vmem_limit_bytes=52 << 20),
        cost_estimate=SMALL,
        name="attention",
    )(info, qkv, qkv, qkv)


def attention_pull(info, qkv, grad, log_total, slots):
    rows = qkv.shape[0]
    table = jax.ShapeDtypeStruct((rows, BLOCKS // 2 * PAIR), jnp.bfloat16)
    return pl.pallas_call(
        attention_pull_kernel,
        grid_spec=pltpu.PrefetchScalarGridSpec(
            num_scalar_prefetch=1,
            grid=(slots, PARTS),
            in_specs=[pick(query_place), pick(key_place), pick(value_place)]
            + [part_spec(), part_rows(SEQ)],
            out_specs=[pl.BlockSpec(memory_space=pl.ANY)] * 2 + [part_rows(PAIR)],
            scratch_shapes=[
                pltpu.VMEM((STRIDE, SEQ, PAIR), jnp.bfloat16),
                pltpu.VMEM((2, 3, SEQ, STRIDE * PAIR), jnp.bfloat16),
                pltpu.SemaphoreType.DMA((2, 3)),
            ],
        ),
        out_shape=[table] * 2 + [jax.ShapeDtypeStruct((slots, PAIRS, 2, PAIR), jnp.float32)],
        compiler_params=pltpu.CompilerParams(vmem_limit_bytes=52 << 20),
        cost_estimate=SMALL,
        name="attention_pull",
    )(info, qkv, qkv, qkv, grad, log_total)


def join_halves(core, own, other):
    return jnp.where(
        core == 0,
        jnp.concatenate([own, other], axis=1),
        jnp.concatenate([other, own], axis=1),
    )


def vector_kernel(info, own_ref, other_ref, vec_ref, bias_ref, own_bias_ref, other_bias_ref):
    early_core = info[0] == 0
    rows = VROWS // 2
    own = jnp.transpose(own_ref[...].astype(jnp.float32))[:rows]
    other = jnp.transpose(other_ref[...].astype(jnp.float32))[:rows]
    vec = jnp.concatenate(
        [jnp.where(early_core, own, other), jnp.where(early_core, other, own)], axis=0
    )
    vec_ref[0:VROWS, :] = vec
    up_rows = FF // D
    for place in range(up_rows):
        early, late = 5 + place, 5 + (place + up_rows // 2) % up_rows
        row = jnp.where(early_core, vec[early : early + 1], vec[late : late + 1])
        bias_ref[0:1, place * D : (place + 1) * D] = row
    own_bias_ref[...] = jnp.zeros_like(own_bias_ref)
    other_bias_ref[...] = jnp.zeros_like(other_bias_ref)
    own_bias_ref[0:1, :D] = jnp.where(early_core, vec[0:1], vec[1:2])
    other_bias_ref[0:1, :D] = jnp.where(early_core, vec[1:2], vec[0:1])


def vector_tables(info, own, other):
    half = own.shape[1] - VEC_PAD
    spec = pl.BlockSpec((D, VEC_PAD), lambda i: (0, half // VEC_PAD))
    shapes = [(16, D), (8, FF), (8, half), (8, half)]
    return pl.pallas_call(
        vector_kernel,
        grid=(1,),
        in_specs=[pl.BlockSpec(memory_space=pltpu.SMEM), spec, spec],
        out_specs=[pl.BlockSpec(shape, lambda i: (0, 0)) for shape in shapes],
        out_shape=[jax.ShapeDtypeStruct(shape, jnp.float32) for shape in shapes],
        name="vector_tables",
    )(info, own, other)


def vector_grad_kernel(info, low_ref, high_ref, bias_ref, head_ref, out_ref):
    early_core = info[0] == 0
    out_ref[...] = jnp.zeros_like(out_ref)
    for pair in range(PAIRS):
        cols = slice(pair * PAIR, (pair + 1) * PAIR)
        out_ref[0:2, cols] = jnp.sum(head_ref[:, pair], axis=0)
    out_ref[2:5, :] = low_ref[0:3, :]
    up_rows = FF // D
    for place in range(up_rows):
        late = (place + up_rows // 2) % up_rows
        out_ref[5 + place : 6 + place, :] = jnp.where(
            early_core,
            bias_ref[0:1, place * D : (place + 1) * D],
            bias_ref[0:1, late * D : (late + 1) * D],
        )
    out_ref[5 + up_rows : 8 + up_rows, :] = high_ref[0:3, :]


def vector_grads(info, low_sums, high_sums, bias_sums, head_sums):
    whole = pl.BlockSpec(memory_space=pltpu.VMEM)
    return pl.pallas_call(
        vector_grad_kernel,
        in_specs=[pl.BlockSpec(memory_space=pltpu.SMEM)] + [whole] * 4,
        out_specs=whole,
        out_shape=jax.ShapeDtypeStruct((16, D), jnp.float32),
        name="vector_grads",
    )(info, low_sums, high_sums, bias_sums, head_sums)


def hidden_pieces(own, other):
    return [
        (ref, slice(first, first + D), place + first)
        for place, ref in ((0, own), (WIDE, other))
        for first in range(0, WIDE, D)
    ]


OUT_COLS = slice(WIDE, WIDE + D // 2)


def raise_kernel(
    info,
    vec_ref,
    bias_ref,
    x_ref,
    ctx_ref,
    own,
    other,
    xhat_ref,
    rstd_ref,
    low_ref,
    own_act_ref,
    other_act_ref,
    slope_ref,
):
    ctx = ctx_ref[...]
    attended = join_halves(info[0], matmul(ctx, own[:, OUT_COLS]), matmul(ctx, other[:, OUT_COLS]))
    xhat, rstd = norm_parts(x_ref[...].astype(jnp.float32) + (attended + vec_ref[2:3, :]))
    xhat_ref[...] = xhat
    rstd_ref[...] = jnp.broadcast_to(rstd, rstd_ref.shape)
    hidden = (xhat * vec_ref[3:4, :] + vec_ref[4:5, :]).astype(jnp.bfloat16)
    low_ref[...] = hidden
    for ref, cols, place in hidden_pieces(own, other):
        spot = slice(place, place + D)
        act, slope = gelu_parts(matmul(hidden, ref[:, cols]) + bias_ref[0:1, spot])
        act_ref = own_act_ref if place < WIDE else other_act_ref
        act_ref[:, cols] = act.astype(jnp.bfloat16)
        slope_ref[:, spot] = slope.astype(jnp.bfloat16)


def add_sums(ref, sums):
    first = pl.program_id(0) == 0
    for place, values in enumerate(sums):
        total = jnp.sum(values, axis=0, keepdims=True)
        spot = slice(place, place + 1)
        ref[spot, :] = jnp.where(first, total, ref[spot, :] + total)


def lower_kernel(
    info, vec_ref, xhat_ref, branch_ref, cot_ref, out_ref, grad_ref, low_ref, sum_ref
):
    first = pl.program_id(0) * ROWS
    hidden = xhat_ref[...] * vec_ref[3:4, :] + vec_ref[4:5, :]
    xhat, rstd = norm_parts(hidden + (branch_ref[...] + vec_ref[9:10, :]))
    gain = vec_ref[10:11, :]
    out_ref[...] = (xhat * gain + vec_ref[11:12, :]).astype(jnp.bfloat16)
    limit = info[INFO + lax.div(first, SEQ)]
    row = lax.broadcasted_iota(jnp.int32, (ROWS, 1), 0) + lax.rem(first, SEQ)
    cot = jnp.where(row < limit, cot_ref[...].astype(jnp.float32), 0.0)
    grad = norm_pull(cot, gain, xhat, rstd)
    grad_ref[...] = grad
    low = grad.astype(jnp.bfloat16)
    low_ref[...] = low
    add_sums(sum_ref, (low.astype(jnp.float32), cot * xhat, cot))


def pull_kernel(
    info,
    vec_ref,
    xhat_ref,
    rstd_ref,
    slope_ref,
    grad_ref,
    low_ref,
    up_own,
    up_other,
    own,
    other,
    own_pre_ref,
    other_pre_ref,
    skip_ref,
    attn_ref,
    ctx_ref,
    sum_ref,
    bias_ref,
):
    core = info[0]
    low = low_ref[...]
    hidden_grad = grad_ref[...]
    for down, up in zip(hidden_pieces(own, other), hidden_pieces(up_own, up_other)):
        ref, cols, place = down
        spot = slice(place, place + D)
        pre = matmul(low, ref[:, cols]) * slope_ref[:, spot].astype(jnp.float32)
        pre = pre.astype(jnp.bfloat16)
        pre_ref = own_pre_ref if place < WIDE else other_pre_ref
        pre_ref[:, cols] = pre
        hidden_grad = hidden_grad + matmul_nt(pre, up[0][:, up[1]])
    xhat = xhat_ref[...]
    skip = norm_pull(hidden_grad, vec_ref[3:4, :], xhat, rstd_ref[:, 0:1])
    skip_ref[...] = skip
    attn = skip.astype(jnp.bfloat16)
    attn_ref[...] = attn
    left, right = attn[:, : D // 2], attn[:, D // 2 :]
    ctx = matmul_nt(jnp.where(core == 0, left, right), up_own[:, OUT_COLS])
    ctx = ctx + matmul_nt(jnp.where(core == 0, right, left), up_other[:, OUT_COLS])
    ctx_ref[...] = ctx.astype(jnp.bfloat16)
    add_sums(sum_ref, (attn.astype(jnp.float32), hidden_grad * xhat, hidden_grad))
    add_sums(bias_ref.at[:, :WIDE], (own_pre_ref[...].astype(jnp.float32),))
    add_sums(bias_ref.at[:, WIDE:], (other_pre_ref[...].astype(jnp.float32),))


def row_spec(width):
    return pl.BlockSpec((ROWS, width), lambda i: (i, 0))


def whole_spec():
    return pl.BlockSpec(memory_space=pltpu.VMEM)


def row_call(kernel, name, in_specs, rows, outs, sums, flops, operands):
    shapes = [jax.ShapeDtypeStruct((rows, width), kind) for width, kind in outs]
    shapes += [jax.ShapeDtypeStruct((8, width), jnp.float32) for width in sums]
    return pl.pallas_call(
        kernel,
        grid=(rows // ROWS,),
        in_specs=[pl.BlockSpec(memory_space=pltpu.SMEM)] + in_specs,
        out_specs=[row_spec(width) for width, kind in outs]
        + [pl.BlockSpec((8, width), lambda i: (0, 0)) for width in sums],
        out_shape=shapes,
        compiler_params=pltpu.CompilerParams(vmem_limit_bytes=52 << 20),
        cost_estimate=SMALL,
        name=name,
    )(*operands)


def raise_rows(info, vec, bias, tokens, context, own, other):
    low, full = jnp.bfloat16, jnp.float32
    return row_call(
        raise_kernel,
        "raise_rows",
        [whole_spec()] * 2 + [row_spec(D)] * 2 + [whole_spec()] * 2,
        tokens.shape[0],
        [(D, full), (PAIR, full), (D, low), (WIDE, low), (WIDE, low), (FF, low)],
        [],
        14 << 30,
        (info, vec, bias, tokens, context, own, other),
    )


def lower_rows(info, vec, xhat, branch, cotangent):
    low, full = jnp.bfloat16, jnp.float32
    return row_call(
        lower_kernel,
        "lower_rows",
        [whole_spec()] + [row_spec(D)] * 3,
        branch.shape[0],
        [(D, low), (D, full), (D, low)],
        [D],
        4 << 30,
        (info, vec, xhat, branch, cotangent),
    )


def pull_rows(info, vec, xhat, rstd, slope, grad, low_grad, up, down):
    low, full = jnp.bfloat16, jnp.float32
    return row_call(
        pull_kernel,
        "pull_rows",
        [whole_spec(), row_spec(D), row_spec(PAIR), row_spec(FF), row_spec(D), row_spec(D)]
        + [whole_spec()] * 4,
        xhat.shape[0],
        [(WIDE, low), (WIDE, low), (D, full), (D, low), (D, low)],
        [D, FF],
        18 << 30,
        (info, vec, xhat, rstd, slope, grad, low_grad, *up, *down),
    )


def split_rest(values):
    high = values.astype(jnp.bfloat16)
    return high, (values - high.astype(jnp.float32)).astype(jnp.bfloat16)

def store_split(values, where, high_ref, rest_ref):
    high_ref[where], rest_ref[where] = split_rest(values)

def close_product(left, right, rows, cols):
    left_high, left_rest = left[0][rows, :], left[1][rows, :]
    right_high, right_rest = right[0][:, cols], right[1][:, cols]
    return matmul(
        jnp.concatenate([left_high, left_high, left_rest], axis=1),
        jnp.concatenate([right_high, right_rest, right_high], axis=0),
    )


def mirrored_product(left, right, finish):
    for first in range(0, D, TILE):
        rows = slice(first, first + TILE)
        wide = close_product(left, right, rows, slice(first, D))
        for last in range(first, D, TILE):
            tile = wide[:, last - first : last - first + TILE]
            cols = slice(last, last + TILE)
            finish(tile, rows, cols)
            if first < last:
                finish(jnp.transpose(tile), cols, rows)


def polar_kernel(
    start_ref,
    own_ref,
    other_ref,
    cols_ref,
    polar_ref,
    out_ref,
    gram,
    a_high,
    a_rest,
    q_high,
    q_rest,
    b_high,
    b_rest,
    r_high,
    r_rest,
):
    a, q, b, r = (a_high, a_rest), (q_high, q_rest), (b_high, b_rest), (r_high, r_rest)
    count = out_ref.shape[0]
    start = pl.multiple_of(start_ref[0], 16)
    whole = own_ref[...] + other_ref[...]
    row = lax.broadcasted_iota(jnp.int32, (D, D), 0)
    col = lax.broadcasted_iota(jnp.int32, (D, D), 1)
    scale = jnp.sqrt(jnp.sum(jnp.where(row == col, whole, 0.0), keepdims=True)) + 1e-07
    gram[...] = whole / (scale * scale)
    whole_rows = (slice(0, count), slice(0, D))

    def sweep(index, carry):
        every = slice(0, D)
        store_split(gram[...], (every, every), a_high, a_rest)

        def step_tile(tile, where_rows, where_cols):
            step = poly_second * gram[where_rows, where_cols] + poly_third * tile
            if where_rows == where_cols:
                tile_row = lax.broadcasted_iota(jnp.int32, (TILE, TILE), 0)
                tile_col = lax.broadcasted_iota(jnp.int32, (TILE, TILE), 1)
                step = step + jnp.where(tile_row == tile_col, poly_first, 0.0)
            store_split(step, (where_rows, where_cols), q_high, q_rest)

        mirrored_product(a, a, step_tile)

        @pl.when(index == 0)
        def _():
            rows = pl.ds(start, count)
            out_ref[...] = q_high[rows, :].astype(jnp.float32) + q_rest[rows, :].astype(jnp.float32)

        @pl.when(index > 0)
        def _():
            store_split(out_ref[...], whole_rows, r_high, r_rest)
            out_ref[...] = close_product(r, q, slice(0, count), every)

        def half_tile(tile, where_rows, where_cols):
            store_split(tile, (where_rows, where_cols), b_high, b_rest)

        def gram_tile(tile, where_rows, where_cols):
            gram[where_rows, where_cols] = tile

        mirrored_product(q, a, half_tile)
        mirrored_product(b, q, gram_tile)
        return carry

    lax.fori_loop(0, NS_ITERS - 1, sweep, 0)
    every = slice(0, D)
    store_split(gram[...], (every, every), a_high, a_rest)
    before = out_ref[...]
    store_split(before, whole_rows, r_high, r_rest)
    once = close_product(r, a, slice(0, count), every)
    store_split(once, whole_rows, r_high, r_rest)
    twice = close_product(r, a, slice(0, count), every)
    out_ref[...] = poly_first * before + poly_second * once + poly_third * twice
    both = jnp.concatenate(split_rest(out_ref[...] / scale), axis=0)
    for place in range(0, cols_ref.shape[1], D):
        spot = slice(place, place + D)
        product = matmul(both, cols_ref[:, spot])
        polar_ref[:, spot] = (product[:count] + product[count:]).astype(jnp.bfloat16)

def polar_rows(start, own, other, columns, count):
    half = pltpu.VMEM((D, D), jnp.bfloat16)
    short = pltpu.VMEM((count, D), jnp.bfloat16)
    return pl.pallas_call(
        polar_kernel,
        in_specs=[pl.BlockSpec(memory_space=pltpu.SMEM)]
        + [pl.BlockSpec(memory_space=pltpu.VMEM)] * 3,
        out_specs=pl.BlockSpec(memory_space=pltpu.VMEM),
        out_shape=jax.ShapeDtypeStruct((count, columns.shape[1]), jnp.bfloat16),
        scratch_shapes=[pltpu.VMEM((count, D), jnp.float32), pltpu.VMEM((D, D), jnp.float32)]
        + [half] * 6
        + [short] * 2,
        compiler_params=pltpu.CompilerParams(vmem_limit_bytes=40 << 20),
        name="polar_rows",
    )(start, own, other, columns)


def per_device(
    size,
    tokens,
    cotangent,
    counts,
    lengths,
    w_qkv,
    w_out,
    w_up,
    w_down,
    vectors,
    mom_qkv,
    mom_out,
    mom_up,
    mom_down,
    adam_first,
    adam_second,
):
    me = lax.axis_index("fsdp")
    core = lax.axis_index("row")
    slots = lengths.shape[0]
    rows = tokens.shape[0]
    up_rows = FF // D
    low = jnp.bfloat16

    block_rows = D // size
    qkv_half, up_half = w_qkv.shape[1], w_up.shape[1]
    vec_rows = vectors.shape[0]
    narrow = qkv_half - D

    def pick_core(early, late):
        return jnp.where(core == 0, early, late)

    def turn(values, cut):
        return pick_core(values, jnp.concatenate([values[:, cut:], values[:, :cut]], axis=1))

    vec_block = jnp.pad(vectors.T, ((0, 0), (0, VEC_PAD - vec_rows))).astype(low)
    first_block = jnp.concatenate([turn(w_qkv.astype(low), narrow), vec_block], axis=1)
    second_block = jnp.concatenate([w_up.astype(low), w_out.astype(low)], axis=1)
    third_block = w_down.astype(low)
    near, far = size.bit_length() - 3, size.bit_length() - 2
    steps = [1 << near, 1 << far, 3 << near]
    first_pieces = send_high(first_block, size)
    first_pieces, second_block, third_block = together(first_pieces, second_block, third_block)
    first_pieces = send_low(sort_high(first_pieces, size), size)
    second_pieces = send_high(second_block, size)
    first_pieces, second_pieces, third_block = together(first_pieces, second_pieces, third_block)
    first_own = sort_low(first_pieces)
    first_other = swap_cores(first_own)
    second_pieces = send_low(sort_high(second_pieces, size), size)
    third_pieces = [third_block, flip(third_block, steps[0], size)]

    live = jnp.arange(slots) % CAP < counts.reshape(-1)[jnp.arange(slots) // CAP]
    info = jnp.concatenate(
        [core.reshape(1).astype(jnp.int32), lengths, jnp.where(live, lengths, 0)]
    )
    vec, bias_up, bias_own, bias_other = vector_tables(info, first_own, first_other)
    qkv_own, qkv_other = first_own[:, :qkv_half], first_other[:, :qkv_half]
    projected = jnp.concatenate(
        [
            (matmul(tokens, qkv_own) + bias_own[:1]).astype(low),
            (matmul(tokens, qkv_other) + bias_other[:1]).astype(low),
        ],
        axis=1,
    )
    projected, third_pieces = together(projected, third_pieces)
    third_pieces += [flip(third_pieces[0], step, size) for step in steps[1:]]
    context, log_total = attention(info, projected, slots)
    context, second_pieces, third_pieces = together(context, second_pieces, third_pieces)
    second_own = sort_low(second_pieces)
    third_pieces = send_low(sort_high(third_pieces, size), size)
    second_other = swap_cores(second_own)
    xhat_one, rstd_one, hidden_low, act_own, act_other, slope = raise_rows(
        info, vec, bias_up, tokens, context, second_own, second_other
    )
    act_own, act_other, *third_pieces = together(act_own, act_other, *third_pieces)
    third_own = sort_low(third_pieces)
    third_other = swap_cores(third_own)
    branch = matmul_nt(act_own, third_own)
    branch, third_other = together(branch, third_other)
    layer_out, top_grad, branch_low, high_sums = lower_rows(
        info, vec, xhat_one, branch + matmul_nt(act_other, third_other), cotangent
    )

    leaving = matmul_tn(branch_low, act_other).astype(low)
    leaving, branch_low = together(leaving, branch_low)
    down_arrived = swap_cores(leaving)
    down_own = matmul_tn(branch_low, act_own)
    down_own, down_arrived, branch_low = together(down_own, down_arrived, branch_low)
    down_kept, leaving = split_low([(down_own, down_arrived)], size)
    leaving, branch_low = together(leaving, branch_low)
    down_sent = fly_low(leaving, size)
    pulled = pull_rows(
        info,
        vec,
        xhat_one,
        rstd_one,
        slope,
        top_grad,
        branch_low,
        (second_own, second_other),
        (third_own, third_other),
    )
    pulled, down_sent = together(pulled, down_sent)
    pre_own, pre_other, skip_grad, attn_low, context_grad, low_sums, bias_sums = pulled
    down_kept, leaving = split_near(down_kept, down_sent, size)
    leaving, pre_own, pre_other, attn_low = together(leaving, pre_own, pre_other, attn_low)
    down_sent = fly_near(leaving, size)
    up_leaving = matmul_tn(hidden_low, pre_other).astype(low)
    up_leaving, pre_own, attn_low, down_sent = together(up_leaving, pre_own, attn_low, down_sent)
    up_arrived = swap_cores(up_leaving)
    down_kept, down_leaving = split_far(down_kept, down_sent, size)
    out_own = pick_core(attn_low[:, : D // 2], attn_low[:, D // 2 :])
    out_other = pick_core(attn_low[:, D // 2 :], attn_low[:, : D // 2])
    out_arrived = swap_cores(matmul_tn(context, out_other).astype(low))
    up_own = matmul_tn(hidden_low, pre_own)
    out_own = matmul_tn(context, out_own)
    up_own, out_own, up_arrived, out_arrived = together(up_own, out_own, up_arrived, out_arrived)
    wide_kept, leaving = split_low([(up_own, up_arrived), (out_own, out_arrived)], size)
    leaving, down_leaving, context_grad = together(leaving, down_leaving, context_grad)
    wide_sent = fly_low(leaving, size)
    down_sent = fly_far(down_leaving, size)
    parts = attention_pull(info, projected, context_grad, log_total, slots)
    parts, down_sent = together(parts, down_sent)

    leaving = matmul_tn(tokens, parts[1]).astype(low)
    qkv_leaving, parts, wide_sent, down_sent = together(leaving, parts, wide_sent, down_sent)
    wide_kept, leaving = split_near(wide_kept, wide_sent, size)
    leaving, parts = together(leaving, parts)
    wide_sent = fly_near(leaving, size)
    qkv_arrived = swap_cores(qkv_leaving)
    qkv_part = matmul_tn(tokens, parts[0])
    (grad_down,) = add_four(down_kept, [down_sent])
    moment_down = moment_decay * mom_down + grad_down
    qkv_part, qkv_arrived, grads, moment_down = together(qkv_part, qkv_arrived, parts, moment_down)
    qkv_kept, leaving = split_low([(qkv_part + qkv_arrived.astype(jnp.float32),)], size)
    leaving, grads, down_block = together(leaving, grads, moment_down.astype(low))
    qkv_sent = fly_low(leaving, size)
    down_sent = fly_far(down_block, size)
    wide_sent, down_sent = together(wide_sent, down_sent)
    wide_kept, wide_leaving = split_far(wide_kept, wide_sent, size)
    wide_sent = fly_far(wide_leaving, size)
    qkv_sent, wide_sent, down_sent = together(qkv_sent, wide_sent, down_sent)
    qkv_kept, leaving = split_high(qkv_kept, qkv_sent, size)
    leaving, wide_sent, down_sent = together(leaving, wide_sent, down_sent)
    qkv_sent = fly_high(leaving, size)
    grad_up, grad_out = add_four(wide_kept, [wide_sent])
    moment_up = moment_decay * mom_up + grad_up
    moment_out = moment_decay * mom_out + grad_out
    wide_block = jnp.concatenate([moment_up.astype(low), moment_out.astype(low)], axis=1)
    wide_sent = fly_far(wide_block, size)
    down_pair = place_far(down_block, down_sent, size)
    down_sent = fly_near(down_pair, size)
    mom_turned = turn(mom_qkv, narrow)
    vector_grad = vector_grads(info, low_sums, high_sums, bias_sums, grads[2])
    qkv_sent, wide_sent, down_sent, grads, vector_grad, mom_turned = together(
        qkv_sent, wide_sent, down_sent, grads, vector_grad, mom_turned
    )
    (grad_turned,) = add_four(qkv_kept, qkv_sent)
    qkv_block = (moment_decay * mom_turned + grad_turned).astype(low)
    wide_pair = place_far(wide_block, wide_sent, size)
    qkv_block, grad_turned, wide_pair = together(qkv_block, grad_turned, wide_pair)
    qkv_pieces = send_high(qkv_block, size)
    wide_sent = fly_near(wide_pair, size)
    vector_grad = vector_grad + swap_cores(vector_grad)
    vector_arrived = flip(vector_grad, 1, size)
    down_rows = place_near(down_pair, down_sent, size)
    grad_qkv = turn(grad_turned, D)
    moment_qkv = moment_decay * mom_qkv + grad_qkv
    grad_qkv, moment_qkv, qkv_pieces, wide_sent, down_rows = together(
        grad_qkv, moment_qkv, qkv_pieces, wide_sent, down_rows
    )
    wide_rows = place_near(wide_pair, wide_sent, size)

    qkv_rows = merge_rows(sort_high(qkv_pieces, size))
    place = me % GROUP

    def widen(values):
        return jnp.pad(values, ((0, 0), (0, WIDE - values.shape[1])))

    matrices = (
        widen(qkv_rows),
        widen(wide_rows[:, up_half:]),
        wide_rows[:, :up_half],
        down_rows,
    )

    def matrix_at(which):
        lower = jnp.where(which == 0, matrices[0], matrices[1])
        upper = jnp.where(which == 2, matrices[2], matrices[3])
        return jnp.where(which < 2, lower, upper)

    pieces = []
    for step in range(GROUP):
        pieces.append(matrix_at(place ^ step).reshape(-1, block_rows, WIDE))
    pieces, grads, vector_grad, vector_arrived = together(
        pieces, grads, vector_grad, vector_arrived
    )
    pieces = pieces[:1] + [flip(pieces[step], step, size) for step in range(1, GROUP)]
    vector_grad = vector_grad + vector_arrived
    vector_arrived = flip(vector_grad, 2, size)
    input_grad = (
        skip_grad + matmul_nt(grads[0], qkv_own) + matmul_nt(grads[1], qkv_other)
    )
    pieces, input_grad, vector_grad, vector_arrived = together(
        pieces, input_grad, vector_grad, vector_arrived
    )
    columns = sort_low(pieces)
    for bit in range(2, size.bit_length() - 3, 2):
        columns = sort_low(send_four(columns.reshape(4, -1, WIDE), bit, size))
    gram = matmul_nt(columns, columns)
    start = ((me - place) * block_rows).reshape(1).astype(jnp.int32)
    vector_grad = vector_grad + vector_arrived
    gram, vector_grad = together(gram, vector_grad)
    gram_arrived = swap_cores(gram)
    vector_arrived = flip(vector_grad, 4, size)
    gram_arrived, vector_arrived = together(gram_arrived, vector_arrived)
    vector_grad = vector_grad + vector_arrived
    polar = polar_rows(start, gram, gram_arrived, columns, GROUP * block_rows)
    polar, vector_grad = together(polar, vector_grad)
    for bit in range(3, size.bit_length() - 1):
        vector_grad = vector_grad + flip(vector_grad, 1 << bit, size)
    grad_vectors = lax.dynamic_slice(
        vector_grad, (core * vec_rows, me * block_rows), (vec_rows, block_rows)
    )
    polar = polar.reshape(GROUP, block_rows, WIDE)
    arrived = []
    for step in range(GROUP):
        block = lax.dynamic_index_in_dim(polar, place ^ step, 0, keepdims=False)
        arrived.append(flip(block, step, size) if step else block)
    arrived = sort_four(arrived, 0, 0)
    masters = (w_qkv, w_out, w_up, w_down)
    counts_of = (3 * D, D, FF, FF)
    updated = []
    for index in range(GROUP):
        ortho = arrived[index][:, : masters[index].shape[1]].astype(jnp.float32)
        if index == 0:
            ortho = turn(ortho, D)
        updated.append(
            masters[index] * (1.0 - muon_rate * decay_rate)
            - muon_rate * 0.2 * math.sqrt(counts_of[index]) * ortho
        )

    first_moment = beta_first * adam_first + (1.0 - beta_first) * grad_vectors
    second_moment = beta_second * adam_second + (1.0 - beta_second) * grad_vectors * grad_vectors
    direction = (
        first_moment
        / (1.0 - beta_first**STEP)
        / (jnp.sqrt(second_moment / (1.0 - beta_second**STEP)) + adam_eps)
    )
    new_vectors = vectors - adam_rate * (direction + decay_rate * vectors)
    return (
        layer_out,
        input_grad,
        grad_qkv,
        grad_out,
        grad_up,
        grad_down,
        grad_vectors,
        moment_qkv,
        moment_out,
        moment_up,
        moment_down,
        updated[0],
        updated[1],
        updated[2],
        updated[3],
        first_moment,
        second_moment,
        new_vectors,
    )


def solution(mesh):
    size = mesh.shape["fsdp"]

    def run(*arrays):
        return per_device(size, *arrays)

    weight = P("fsdp", "row")
    vector = P("row", "fsdp")
    sample = P(("fsdp", "row"), None)
    return jax.shard_map(
        run,
        mesh=mesh,
        in_specs=(sample, sample, sample, P(("fsdp", "row")))
        + (weight,) * 4
        + (vector,)
        + (weight,) * 4
        + (vector,) * 2,
        out_specs=(sample, sample)
        + (weight,) * 4
        + (vector,)
        + (weight,) * 8
        + (vector,) * 3,
        check_vma=False,
    )
```
